32 devices in a mesh: stream: 4 (over y, core), lat: 8 (over z, x).
Axes of the slice: x: 2, y: 2, z: 4, core: 2. Of those that a mesh axis runs over, the one named last changes fastest.
Arguments:
- inverse: bfloat16 [16, 4, 4, 512, 512], P('lat', 'stream'), may hold values from -2 to 2
- upwind: bfloat16 [16, 4, 4, 64, 512], P('lat', 'stream'), may hold values from -0.75 to 0.75
- lateral: bfloat16 [16, 4, 4, 64, 512], P('lat', 'stream'), may hold values from -0.375 to 0.375
- inlet_trace: float32 [16, 64, 256], P('lat'), may hold values from -6 to 6
- previous: bfloat16 [16, 4, 4, 512, 256], P('lat', 'stream'), may hold values from -6 to 6
- uptake_rate: float32 [256], replicated, may hold values from 0.3 to 3
- affinity: float32 [256], replicated, may hold values from 0.5 to 4
- flow_order: int32 [16, 4, 4], P('lat', 'stream'), may hold values from 0 to 3, each once within a row
Outputs:
- concentration: bfloat16 [16, 4, 4, 512, 256], P('lat', 'stream')
The draws below stay inside these ranges and needn't reach their ends.
Inputs may be any that keep to these rules, and one draw needn't show every extreme that they name: `flow_order`: each row of 4 entries lists 0 to 3 once each.
All inputs are finite; a program needn't handle non-finite values.
Results may differ from the reference program's by a relative error of at most 0.002.
Values sent between devices are 32-bit elements; how exact they have to be, the bound alone decides.
No kernel may reach another device: no remote copies, remote signals or barrier semaphores. Data moves between devices by JAX's collectives and lax.ppermute only.
A program may use at most 64 MiB of HBM per device.

```python
import math
import jax
import jax.numpy as jnp
from jax import lax

NODES_1D = 8
NODES = 512
FACE = 64
TRACERS = 256
ROW_DEV = 4
ITERS = 2
COLS = 16
BLOCKS = 4


def draw_inverse(key, part):
    first_key, second_key = jax.random.split(jax.random.fold_in(key, 11))
    full_shape = (COLS, BLOCKS, ROW_DEV, NODES, NODES)
    diagonal = jnp.exp(jax.random.uniform(first_key, full_shape[:-1], jnp.float32, math.log(0.8), math.log(1.25)))
    spread_part = 0.4 * jax.random.normal(second_key, full_shape, jnp.float32) / math.sqrt(NODES)
    unit_matrix = jnp.eye(NODES, dtype=jnp.float32)
    return (spread_part + diagonal[..., None] * unit_matrix).astype(jnp.bfloat16)


def level_of(own_key, dims, shards, least, largest):
    factor_of, own = 1.0, jax.random.fold_in(own_key, 6)
    for dim, parts in shards:
        steps = jnp.exp(jax.random.uniform(jax.random.fold_in(own, dim), (parts,), jnp.float32, least / len(shards), largest / len(shards)))
        factor_of = factor_of * jnp.repeat(steps, dims[dim] // parts).reshape([-1 if axis == dim else 1 for axis in range(len(dims))])
    return factor_of


def gaussian(key, shape, scale, limit, pieces=(), kind=jnp.bfloat16):
    entries = scale * jax.random.normal(key, shape, jnp.float32)
    if pieces:
        entries = entries * level_of(key, shape, pieces, -0.22, 0.18)
    return jnp.clip(entries, -limit, limit).astype(kind)


def setup_inputs(seed: int = 0) -> dict:
    key_of = jax.random.split(jax.random.key(seed), 9)
    inverse = draw_inverse(jax.random.fold_in(key_of[8], 71), 0)
    upwind = gaussian(key_of[1], (COLS, BLOCKS, ROW_DEV, FACE, NODES), (0.9 / NODES_1D), 0.75, ((0, 8), (1, 4)))
    lateral = gaussian(key_of[2], (COLS, BLOCKS, ROW_DEV, FACE, NODES), (0.5 / NODES_1D), 0.375, ((0, 8), (1, 4)))
    inlet_trace = gaussian(key_of[3], (COLS, FACE, TRACERS), 1.0, 6.0, ((0, 8),), jnp.float32)
    previous = gaussian(key_of[4], (COLS, BLOCKS, ROW_DEV, NODES, TRACERS), 1.0, 6.0, ((0, 8), (1, 4)))
    uptake_rate = jnp.clip(jnp.exp(jax.random.uniform(key_of[5], (TRACERS,), jnp.float32, math.log(0.3), math.log(3.0))), 0.3, 3.0)
    affinity = jnp.clip(jnp.exp(jax.random.uniform(key_of[6], (TRACERS,), jnp.float32, math.log(0.5), math.log(4.0))), 0.5, 4.0)
    flow_order = jax.vmap(lambda own: jax.random.permutation(own, ROW_DEV))(jax.random.split(key_of[7], COLS * BLOCKS)).reshape((COLS, BLOCKS, ROW_DEV)).astype(jnp.int32)
    return {"inverse": inverse, "upwind": upwind, "lateral": lateral, "inlet_trace": inlet_trace, "previous": previous, "uptake_rate": uptake_rate, "affinity": affinity, "flow_order": flow_order}


HIGHEST = lax.Precision.HIGHEST


def lateral_face(nodal_field):
    leading = nodal_field.shape[:-2]
    shaped = nodal_field.reshape(leading + (NODES_1D, NODES_1D, NODES_1D, TRACERS))
    return shaped[..., :, NODES_1D - 1, :, :].reshape(leading + (FACE, TRACERS))


def langmuir(lagged, uptake_rate, affinity):
    return uptake_rate * lagged / (1.0 + affinity * jnp.abs(lagged))


def reference(inverse, upwind, lateral, inlet_trace, previous, uptake_rate, affinity, flow_order):
    current = previous.astype(jnp.float32)
    columns = jnp.arange(COLS)
    for sweep_index in range(ITERS):
        lagged = current
        traces = lateral_face(lagged)
        lateral_in = jnp.concatenate([jnp.zeros_like(traces[:1]), traces[:-1]], axis=0)

        def block_step(inflow, block_index):
            order_block = lax.dynamic_index_in_dim(flow_order, block_index, 1, False)
            inverse_block = lax.dynamic_index_in_dim(inverse, block_index, 1, False)
            upwind_block = lax.dynamic_index_in_dim(upwind, block_index, 1, False)
            lateral_block = lax.dynamic_index_in_dim(lateral, block_index, 1, False)
            lagged_block = lax.dynamic_index_in_dim(lagged, block_index, 1, False)
            side_block = lax.dynamic_index_in_dim(lateral_in, block_index, 1, False)

            def element_step(carried, position):
                chosen = lax.dynamic_index_in_dim(order_block, position, 1, False).astype(jnp.int32)
                matrix = inverse_block[columns, chosen].astype(jnp.float32)
                up_part = upwind_block[columns, chosen].astype(jnp.float32)
                side_part = lateral_block[columns, chosen].astype(jnp.float32)
                source = langmuir(lagged_block[columns, chosen], uptake_rate, affinity)
                right_side = source + jnp.einsum('cfn,cfg->cng', side_part, side_block[columns, chosen], precision=HIGHEST)
                right_side = right_side + jnp.einsum('cfn,cfg->cng', up_part, carried, precision=HIGHEST)
                solved = jnp.einsum('cmn,cng->cmg', matrix, right_side, precision=HIGHEST)
                return solved[:, NODES - FACE:, :], solved

            outflow, solved_all = lax.scan(element_step, inflow, jnp.arange(ROW_DEV))
            placed = jnp.moveaxis(solved_all, 0, 1)
            storage_rank = jnp.argsort(order_block, axis=1).astype(jnp.int32)
            stored = jnp.take_along_axis(placed, storage_rank[:, :, None, None], axis=1)
            return outflow, stored

        final_trace, blocks_out = lax.scan(block_step, inlet_trace, jnp.arange(BLOCKS))
        current = jnp.moveaxis(blocks_out, 0, 1)
    return current.astype(jnp.bfloat16)
```

```python
import functools

import jax
import jax.numpy as jnp
from jax import lax
from jax.experimental import pallas as pl
from jax.experimental.pallas import tpu as pltpu
from jax.sharding import PartitionSpec as P

NODES_1D = 8
F32 = jnp.float32
BF16 = jnp.bfloat16
MIB = 1 << 20


def from_behind(value, axis, steps):
    count = lax.axis_size(axis)
    initial, last = (max(0, -steps), min(count, count - steps))
    return lax.ppermute(value, axis, [(source, source + steps) for source in range(initial, last)])


def split(x):
    high = x.astype(BF16)
    return high, (x - high.astype(F32)).astype(BF16)


def dot(x, y):
    return jnp.dot(x, y, preferred_element_type=F32)


def dot_split(x, y):
    return dot(x[0], y[0]) + (dot(x[0], y[1]) + dot(x[1], y[0]))


def langmuir(lagged, rate, affinity):
    below = 1.0 + affinity * jnp.abs(lagged)
    guess = pl.reciprocal(below, approx=True)
    guess = guess * (2.0 - below * guess)
    guess = guess * (2.0 - below * guess)
    return rate * lagged * guess


def lateral_rows(field, per_side):
    plane = per_side * per_side
    return jnp.concatenate(
        [field[a * plane + plane - per_side : (a + 1) * plane] for a in range(per_side)], axis=0
    )


def traces_kernel(per_side, prev, out):
    plane = per_side * per_side
    for c in range(out.shape[0]):
        for j in range(out.shape[1]):
            for a in range(per_side):
                rows = prev[c, j, a].astype(F32)
                out[c, j, a * per_side : (a + 1) * per_side] = rows[rows.shape[0] - per_side :]


def first_kernel(
    per_side, order, inv_hbm, up_hbm, lat_hbm, prev_hbm, rate, affinity,
    inv, maps, free, side_maps, tails, rows_high, rows_low, block_map,
    faces, lagged, tail_scratch, row_scratch, sems,
):
    cols, count = order.shape[0], order.shape[2]
    face = up_hbm.shape[3]
    nodes = inv.shape[1]

    def copies(i):
        c, p = i // count, i % count
        j = order[c, 0, p]
        return (
            pltpu.make_async_copy(inv_hbm.at[c, 0, j], inv.at[i], sems.at[0, i]),
            pltpu.make_async_copy(up_hbm.at[c, 0, j], faces.at[i, pl.ds(0, face)], sems.at[1, i]),
            pltpu.make_async_copy(lat_hbm.at[c, 0, j], faces.at[i, pl.ds(face, face)], sems.at[2, i]),
            pltpu.make_async_copy(prev_hbm.at[c, 0, j], lagged.at[i], sems.at[3, i]),
        )

    for i in range(cols * count):
        for copy in copies(i):
            copy.start()

    def element(i, _):
        for copy in copies(i):
            copy.wait()
        matrix = inv[i]
        both = lax.dot_general(matrix, faces[i], (((1,), (1,)), ((), ())), preferred_element_type=F32)
        high, low = split(both)
        maps[i] = jnp.concatenate([high, high, low], axis=1)
        tail = both[nodes - face :]
        tail_scratch[i] = tail
        side = lateral_rows(both, per_side)
        s_high, s_low = split(side)
        side_maps[i] = jnp.concatenate([s_high, s_high, s_low], axis=1)
        source = langmuir(lagged[i].astype(F32), rate[...], affinity[...])
        s_high, s_low = split(source)
        free[i] = dot(matrix, s_high) + dot(matrix, s_low)
        return 0

    lax.fori_loop(0, cols * count, element, 0)

    wide = count * face
    row_id = lax.broadcasted_iota(jnp.int32, (face, wide), 0)
    lane_id = lax.broadcasted_iota(jnp.int32, (face, wide), 1)
    for p in range(count):
        for c in range(cols):
            i = c * count + p
            unit = jnp.where(lane_id == row_id + p * face, 1.0, 0.0)
            if p == 0:
                row = unit
            else:
                row = row_scratch[c] + unit
            r = split(row)
            rows_high[c, pl.ds(p * face, face)] = r[0]
            rows_low[c, pl.ds(p * face, face)] = r[1]
            step = split(tail_scratch[i][:, :face])
            row_scratch[c] = dot_split(step, r)
            tails[i] = tail_scratch[i]
    for c in range(cols):
        r = split(row_scratch[c])
        rows_high[c, pl.ds(count * face, face)] = r[0]
        rows_low[c, pl.ds(count * face, face)] = r[1]
        block_map[c] = row_scratch[c][:, :face]


def side_kernel(
    with_map, order, arrived, local, free, tails, rows_high, rows_low, block_map,
    sides, ends, message, high, low,
):
    cols, count = order.shape[0], order.shape[2]
    nodes, tracers = free.shape[1:]
    face = tails.shape[1]
    for c in range(cols):
        for p in range(count):
            i = c * count + p
            j = order[c, 0, p]
            side = arrived[j] if c == 0 else local[c - 1, j]
            s = split(side)
            sides[i, 0] = s[0]
            sides[i, 1] = s[1]
            tail = split(tails[i][:, face:])
            ends[i] = free[i, pl.ds(nodes - face, face)] + dot_split(tail, s)
    for c in range(cols):
        for p in range(count - 1):
            e = split(ends[c * count + p])
            high[c, pl.ds(p * face, face)] = e[0]
            low[c, pl.ds(p * face, face)] = e[1]
        last = pl.ds(count * face, face)
        row = (rows_high[c, last][:, face:], rows_low[c, last][:, face:])
        offset = ends[c * count + count - 1] + dot_split(row, (high[c], low[c]))
        message[c, :, pl.ds(0, tracers)] = offset
        if with_map:
            message[c, :, pl.ds(tracers, face)] = block_map[c]


def enter(place, inlet, gathered, mapped, rows_high, rows_low, sides, ends, stack, high, low):
    cols, face, tracers = inlet.shape
    count = ends.shape[0] // cols
    for c in range(cols):
        def block(k, entering):
            m = split(mapped[k, c, :, pl.ds(tracers, face)])
            return dot_split(m, split(entering)) + gathered[k, c, :, pl.ds(0, tracers)]

        entering = lax.fori_loop(0, place[0], block, inlet[c])
        e = split(entering)
        high[c, pl.ds(0, face)] = e[0]
        low[c, pl.ds(0, face)] = e[1]
        for p in range(count - 1):
            e = split(ends[c * count + p])
            high[c, pl.ds((p + 1) * face, face)] = e[0]
            low[c, pl.ds((p + 1) * face, face)] = e[1]
        span = pl.ds(0, count * face)
        inflow = dot_split((rows_high[c, span], rows_low[c, span]), (high[c], low[c]))
        for p in range(count):
            i = c * count + p
            f = split(inflow[p * face : (p + 1) * face])
            stack[i, pl.ds(0, face)] = f[0]
            stack[i, pl.ds(face, face)] = sides[i, 0]
            stack[i, pl.ds(2 * face, face)] = f[1]
            stack[i, pl.ds(3 * face, face)] = sides[i, 1]
            stack[i, pl.ds(4 * face, face)] = f[0]
            stack[i, pl.ds(5 * face, face)] = sides[i, 0]


def trace_kernel(
    per_side, order, place, inlet, gathered, rows_high, rows_low, sides, ends, free, side_maps,
    stack, trace, high, low,
):
    enter(place, inlet, gathered, gathered, rows_high, rows_low, sides, ends, stack, high, low)
    cols, count = order.shape[0], order.shape[2]
    for p in range(count):
        i = (cols - 1) * count + p
        trace[order[cols - 1, 0, p]] = lateral_rows(free.at[i], per_side) + dot(side_maps[i], stack[i])


def second_kernel(per_side, order, inv, maps, free, stack, rate, affinity, free_out, local):
    cols, count = order.shape[0], order.shape[2]

    def element(i, _):
        swept = free[i] + dot(maps[i], stack[i])
        local[i // count, order[i // count, 0, i % count]] = lateral_rows(swept, per_side)
        s_high, s_low = split(langmuir(swept, rate[...], affinity[...]))
        matrix = inv[i]
        free_out[i] = dot(matrix, s_high) + dot(matrix, s_low)
        return 0

    lax.fori_loop(0, cols * count, element, 0)


def last_kernel(
    order, place, inlet, gathered, mapped, rows_high, rows_low, sides, ends, free, maps,
    out_hbm, stack, high, low, staged, sems,
):
    enter(place, inlet, gathered, mapped, rows_high, rows_low, sides, ends, stack, high, low)
    cols, count = order.shape[0], order.shape[2]

    def copy(i):
        c, p = i // count, i % count
        return pltpu.make_async_copy(staged.at[i], out_hbm.at[c, 0, order[c, 0, p]], sems.at[i])

    def element(i, _):
        staged[i] = (free[i] + dot(maps[i], stack[i])).astype(BF16)
        copy(i).start()
        return 0

    lax.fori_loop(0, cols * count, element, 0)

    def finish(i, _):
        copy(i).wait()
        return 0

    lax.fori_loop(0, cols * count, finish, 0)


def per_device(inverse, upwind, lateral, inlet_trace, previous, uptake_rate, affinity, flow_order):
    cols, _, count, nodes, _ = inverse.shape
    face = upwind.shape[3]
    tracers = previous.shape[-1]
    per_side = NODES_1D
    items = cols * count
    wide = count * face

    def vmem(shape, kind=F32):
        return pltpu.VMEM(shape, kind)

    whole = pl.BlockSpec(memory_space=pltpu.VMEM)
    small = pl.BlockSpec(memory_space=pltpu.SMEM)
    hbm = pl.BlockSpec(memory_space=pl.ANY)

    def call(kernel, name, ins, outs, scratch, flops, limit=24):
        return pl.pallas_call(
            kernel,
            name=name,
            in_specs=ins,
            out_specs=[hbm if isinstance(o, jax.ShapeDtypeStruct) else whole for o in outs],
            out_shape=outs,
            scratch_shapes=scratch,
            cost_estimate=pl.CostEstimate(flops=flops, bytes_accessed=MIB, transcendentals=0),
            compiler_params=pltpu.CompilerParams(vmem_limit_bytes=limit * MIB),
        )

    rate, aff = uptake_rate.reshape(1, tracers), affinity.reshape(1, tracers)
    place = lax.axis_index("stream").astype(jnp.int32).reshape(1)
    dense = 2 * items * nodes * nodes * tracers

    block = 2 * per_side
    shaped = previous.reshape(cols, count, per_side, per_side * per_side, tracers)
    old_traces = pl.pallas_call(
        functools.partial(traces_kernel, per_side),
        name="old_traces",
        grid=(1,),
        in_specs=[
            pl.BlockSpec(
                (cols, count, per_side, block, tracers),
                lambda _: (0, 0, 0, per_side * per_side // block - 1, 0),
            )
        ],
        out_specs=pl.BlockSpec((cols, count, face, tracers), lambda _: (0, 0, 0, 0)),
        out_shape=jax.ShapeDtypeStruct((cols, count, face, tracers), F32),
    )(shaped)
    arrived = from_behind(old_traces[cols - 1], "lat", 1)

    inv, maps, free, side_maps, tails, rows_high, rows_low, block_map = call(
        functools.partial(first_kernel, per_side),
        "first_sweep",
        [small, hbm, hbm, hbm, hbm, whole, whole],
        [
            vmem((items, nodes, nodes), BF16),
            vmem((items, nodes, 6 * face), BF16),
            vmem((items, nodes, tracers)),
            vmem((items, face, 6 * face), BF16),
            vmem((items, face, 2 * face)),
            vmem((cols, wide + face, wide), BF16),
            vmem((cols, wide + face, wide), BF16),
            vmem((cols, face, face)),
        ],
        [
            vmem((items, 2 * face, nodes), BF16),
            vmem((items, nodes, tracers), BF16),
            vmem((items, face, 2 * face)),
            vmem((cols, face, wide)),
            pltpu.SemaphoreType.DMA((4, items)),
        ],
        3 * dense,
    )(flow_order, inverse, upwind, lateral, previous, rate, aff)

    def add_sides(arrived, local, free, with_map):
        return call(
            functools.partial(side_kernel, with_map),
            "add_sides",
            [small] + [whole] * 7,
            [
                vmem((items, 2, face, tracers), BF16),
                vmem((items, face, tracers)),
                vmem((cols, face, tracers + (face if with_map else 0))),
            ],
            [vmem((cols, wide - face, tracers), BF16)] * 2,
            dense // 100,
        )(flow_order, arrived, local, free, tails, rows_high, rows_low, block_map)

    sides, ends, message = add_sides(arrived, old_traces, free, True)
    mapped = lax.all_gather(message, "stream")

    stack, trace = call(
        functools.partial(trace_kernel, per_side),
        "entering",
        [small, small] + [whole] * 8,
        [vmem((items, 6 * face, tracers), BF16), vmem((count, face, tracers))],
        [vmem((cols, wide, tracers), BF16)] * 2,
        dense // 100,
    )(flow_order, place, inlet_trace, mapped, rows_high, rows_low, sides, ends, free, side_maps)
    arrived = from_behind(trace, "lat", 1)

    free, local = call(
        functools.partial(second_kernel, per_side),
        "second_sweep",
        [small] + [whole] * 6,
        [vmem((items, nodes, tracers)), vmem((cols, count, face, tracers))],
        [],
        3 * dense,
    )(flow_order, inv, maps, free, stack, rate, aff)

    sides, ends, message = add_sides(arrived, local, free, False)
    gathered = lax.all_gather(message, "stream")

    (out,) = call(
        last_kernel,
        "result",
        [small, small] + [whole] * 9,
        [jax.ShapeDtypeStruct(previous.shape, BF16)],
        [
            vmem((items, 6 * face, tracers), BF16),
            vmem((cols, wide, tracers), BF16),
            vmem((cols, wide, tracers), BF16),
            vmem((items, nodes, tracers), BF16),
            pltpu.SemaphoreType.DMA((items,)),
        ],
        dense,
    )(flow_order, place, inlet_trace, gathered, mapped, rows_high, rows_low, sides, ends, free, maps)
    return out


def solution(mesh):
    placed = (
        P("lat", "stream", None, None, None),
        P("lat", "stream", None, None, None),
        P("lat", "stream", None, None, None),
        P("lat", None, None),
        P("lat", "stream", None, None, None),
        P(),
        P(),
        P("lat", "stream", None),
    )
    return jax.shard_map(
        per_device,
        mesh=mesh,
        in_specs=placed,
        out_specs=P("lat", "stream", None, None, None),
        check_vma=False,
    )
```

```python
import jax
import jax.numpy as jnp
from jax import lax
from jax.experimental import pallas as pl
from jax.experimental.pallas import tpu as pltpu
from jax.sharding import PartitionSpec as P

NODES_1D = 8
F32 = jnp.float32
BF16 = jnp.bfloat16
MIB = 1 << 20

WHOLE = pl.BlockSpec(memory_space=pltpu.VMEM)
SMALL = pl.BlockSpec(memory_space=pltpu.SMEM)
HBM = pl.BlockSpec(memory_space=pltpu.HBM)


def run(body, name, ins, outs, scratch, flops):
    names = [*ins, *outs, *scratch]

    def kernel(*refs):
        body(**dict(zip(names, refs)))

    values = pl.pallas_call(
        kernel,
        name=name,
        in_specs=[spec for _, spec in ins.values()],
        out_specs=[HBM if isinstance(o, jax.ShapeDtypeStruct) else WHOLE for o in outs.values()],
        out_shape=list(outs.values()),
        scratch_shapes=list(scratch.values()),
        cost_estimate=pl.CostEstimate(flops=flops, bytes_accessed=MIB, transcendentals=0),
        compiler_params=pltpu.CompilerParams(vmem_limit_bytes=24 * MIB),
    )(*[array for array, _ in ins.values()])
    return dict(zip(outs, values))


def split(x):
    high = x.astype(BF16)
    return high, (x - high.astype(F32)).astype(BF16)


def dot(x, y):
    return jnp.dot(x, y, preferred_element_type=F32)


def dot_split(x, y):
    return dot(x[0], y[0]) + (dot(x[0], y[1]) + dot(x[1], y[0]))


def langmuir(lagged, rate, affinity):
    below = 1.0 + affinity * jnp.abs(lagged)
    guess = pltpu.reciprocal(below, approx=True)
    guess = guess * (2.0 - below * guess)
    guess = guess * (2.0 - below * guess)
    return rate * lagged * guess


def lateral_rows(field, per_side):
    plane = per_side * per_side
    return jnp.concatenate(
        [field[a * plane + plane - per_side : (a + 1) * plane] for a in range(per_side)], axis=0
    )


def pack_map(mapping, lanes):
    face = mapping.shape[0]
    rows = face * face // lanes
    return jnp.concatenate([mapping[q * rows : (q + 1) * rows] for q in range(lanes // face)], axis=1)


def unpack_map(packed, face):
    return jnp.concatenate(
        [packed[:, q * face : (q + 1) * face] for q in range(packed.shape[1] // face)], axis=0
    )


def per_device(inverse, upwind, lateral, inlet_trace, previous, uptake_rate, affinity, flow_order):
    cols, _, count, nodes, _ = inverse.shape
    face = upwind.shape[3]
    tracers = previous.shape[-1]
    per_side = NODES_1D
    plane = per_side * per_side
    wide = count * face
    packed = face * face // tracers
    streams, lats = lax.axis_size("stream"), lax.axis_size("lat")
    stages = streams.bit_length() - 1
    assert streams == 1 << stages
    groups = [list(range(1, cols)), [0]] if cols > 1 else [[0]]

    rate = (uptake_rate.reshape(1, tracers), WHOLE)
    aff = (affinity.reshape(1, tracers), WHOLE)
    order = (flow_order, SMALL)
    place = (jnp.stack([lax.axis_index("stream"), lax.axis_index("lat")]).astype(jnp.int32), SMALL)
    dense = 2 * count * nodes * nodes * tracers
    vmem = pltpu.VMEM
    whole = lambda *arrays: [(a, WHOLE) for a in arrays]

    def to_next(value):
        return lax.ppermute(value, "lat", [(i, (i + 1) % lats) for i in range(lats)])

    def swap(value, stage):
        return lax.ppermute(value, "stream", [(i, i ^ (1 << stage)) for i in range(streams)])

    def bit(place, stage):
        return ((place[0] >> stage) & 1) == 1

    shaped = previous.reshape(cols, count, per_side, plane, tracers)
    tail_rows = pl.ds(plane - 2 * per_side, 2 * per_side)

    def old_trace(old, trace, staged, sem):
        copy = pltpu.make_async_copy(old.at[cols - 1, :, :, tail_rows], staged, sem)
        copy.start()
        copy.wait()
        for j in range(count):
            for a in range(per_side):
                trace[j, pl.ds(a * per_side, per_side)] = staged[j, a].astype(F32)[per_side:]

    trace = run(
        old_trace,
        "old_trace",
        {"old": (shaped, HBM)},
        {"trace": vmem((count, face, tracers), F32)},
        {"staged": vmem((count, per_side, 2 * per_side, tracers), BF16), "sem": pltpu.SemaphoreType.DMA},
        dense // 100,
    )["trace"]
    arrived = to_next(trace)

    def add_side(i, side, free, tails, sides, ends):
        s = split(side)
        sides[i, 0] = s[0]
        sides[i, 1] = s[1]
        tail = split(tails[i][:, face:])
        ends[i] = free[i, pl.ds(nodes - face, face)] + dot_split(tail, s)

    def offset(n, rows_high, rows_low, ends, high, low):
        for p in range(count - 1):
            e = split(ends[n * count + p])
            high[n, pl.ds(p * face, face)] = e[0]
            low[n, pl.ds(p * face, face)] = e[1]
        last = pl.ds(wide, face)
        row = (rows_high[n, last][:, face:], rows_low[n, last][:, face:])
        return ends[n * count + count - 1] + dot_split(row, (high[n], low[n]))

    side_outs = lambda size: {
        "sides": vmem((size * count, 2, face, tracers), BF16),
        "ends": vmem((size * count, face, tracers), F32),
    }
    offset_scratch = lambda size: {
        "high": vmem((size, wide - face, tracers), BF16),
        "low": vmem((size, wide - face, tracers), BF16),
    }

    def first(group):
        size = len(group)
        items = size * count
        local = group[0] > 0

        def body(
            order, inverse, upwind, lateral, previous, old, rate, affinity, inv, maps, free, side_maps, tails,
            rows_high, rows_low, faces, lagged, source_high, source_low, row, sems,
            sides=None, ends=None, message=None, block_map=None, high=None, low=None, staged=None, old_sems=None,
        ):
            def copies(i):
                c, p = group[i // count], i % count
                j = order[c, 0, p]
                return (
                    pltpu.make_async_copy(previous.at[c, 0, j], lagged.at[i], sems.at[0, i]),
                    pltpu.make_async_copy(upwind.at[c, 0, j], faces.at[i, pl.ds(0, face)], sems.at[1, i]),
                    pltpu.make_async_copy(lateral.at[c, 0, j], faces.at[i, pl.ds(face, face)], sems.at[2, i]),
                    pltpu.make_async_copy(inverse.at[c, 0, j], inv.at[i], sems.at[3, i]),
                )

            def old_copy(n):
                return pltpu.make_async_copy(
                    old.at[group[n] - 1, :, :, tail_rows], staged.at[n], old_sems.at[n]
                )

            for i in range(items):
                for copy in copies(i):
                    copy.start()
            if local:
                for n in range(size):
                    old_copy(n).start()

            row_id = lax.broadcasted_iota(jnp.int32, (face, wide), 0)
            lane_id = lax.broadcasted_iota(jnp.int32, (face, wide), 1)
            for i in range(items + 1):
                if i < items:
                    n, p = i // count, i % count
                    for copy in copies(i):
                        copy.wait()
                    both = lax.dot_general(
                        inv[i], faces[i], (((1,), (1,)), ((), ())), preferred_element_type=F32
                    )
                    b_high, b_low = split(both)
                    maps[i] = jnp.concatenate([b_high, b_high, b_low], axis=1)
                    tails[i] = both[nodes - face :]
                    s = split(lateral_rows(both, per_side))
                    side_maps[i] = jnp.concatenate([s[0], s[0], s[1]], axis=1)
                    s = split(langmuir(lagged[i].astype(F32), rate[...], affinity[...]))
                    source_high[i % 2], source_low[i % 2] = s
                    unit = jnp.where(lane_id == row_id + p * face, 1.0, 0.0)
                    r = split(unit if p == 0 else row[n] + unit)
                    rows_high[n, pl.ds(p * face, face)] = r[0]
                    rows_low[n, pl.ds(p * face, face)] = r[1]
                    row[n] = dot_split(split(tails[i][:, :face]), r)
                    if p == count - 1:
                        r = split(row[n])
                        rows_high[n, pl.ds(wide, face)] = r[0]
                        rows_low[n, pl.ds(wide, face)] = r[1]
                        if not local:
                            block_map[n] = pack_map(row[n][:, :face], tracers)
                if i > 0:
                    k = (i - 1) % 2
                    free[i - 1] = dot(inv[i - 1], source_high[k]) + dot(inv[i - 1], source_low[k])
            if local:
                for n in range(size):
                    old_copy(n).wait()
                    for p in range(count):
                        j = order[group[n], 0, p]
                        side = jnp.concatenate(
                            [staged[n, j, a].astype(F32)[per_side:] for a in range(per_side)], axis=0
                        )
                        add_side(n * count + p, side, free, tails, sides, ends)
                    message[n, pl.ds(0, face)] = offset(n, rows_high, rows_low, ends, high, low)
                    message[n, pl.ds(face, packed)] = pack_map(row[n][:, :face], tracers)

        outs = {
            "inv": vmem((items, nodes, nodes), BF16),
            "maps": vmem((items, nodes, 6 * face), BF16),
            "free": vmem((items, nodes, tracers), F32),
            "side_maps": vmem((items, face, 6 * face), BF16),
            "tails": vmem((items, face, 2 * face), F32),
            "rows_high": vmem((size, wide + face, wide), BF16),
            "rows_low": vmem((size, wide + face, wide), BF16),
        }
        scratch = {
            "faces": vmem((items, 2 * face, nodes), BF16),
            "lagged": vmem((items, nodes, tracers), BF16),
            "source_high": vmem((2, nodes, tracers), BF16),
            "source_low": vmem((2, nodes, tracers), BF16),
            "row": vmem((size, face, wide), F32),
            "sems": pltpu.SemaphoreType.DMA((4, items)),
        }
        if local:
            outs |= side_outs(size) | {"message": vmem((size, face + packed, tracers), F32)}
            scratch |= offset_scratch(size) | {
                "staged": vmem((size, count, per_side, 2 * per_side, tracers), BF16),
                "old_sems": pltpu.SemaphoreType.DMA((size,)),
            }
        else:
            outs |= {"block_map": vmem((size, packed, tracers), F32)}
        ins = {
            "order": order,
            "inverse": (inverse, HBM),
            "upwind": (upwind, HBM),
            "lateral": (lateral, HBM),
            "previous": (previous, HBM),
            "old": (shaped, HBM),
            "rate": rate,
            "affinity": aff,
        }
        return run(body, "first_sweep", ins, outs, scratch, 3 * size * dense)

    def arrived_side(place, arrived, j):
        return jnp.where(place[1] > 0, arrived[j], 0.0)

    def first_sides(state, arrived):
        def body(
            order, place, arrived, free, tails, rows_high, rows_low, block_map, sides, ends, message, high, low
        ):
            for p in range(count):
                add_side(p, arrived_side(place, arrived, order[0, 0, p]), free, tails, sides, ends)
            message[0, pl.ds(0, face)] = offset(0, rows_high, rows_low, ends, high, low)
            message[0, pl.ds(face, packed)] = block_map[0]

        keys = ("free", "tails", "rows_high", "rows_low", "block_map")
        ins = {"order": order, "place": place, "arrived": (arrived, WHOLE)}
        outs = side_outs(1) | {"message": vmem((1, face + packed, tracers), F32)}
        return run(
            body, "first_sides", ins | {k: (state[k], WHOLE) for k in keys}, outs, offset_scratch(1), dense // 50
        )

    def combine_first(stage, own, other):
        size = own.shape[0]

        def body(place, own, other, message):
            upper = bit(place, stage)
            for n in range(size):
                up = jnp.where(upper, own[n], other[n])
                low = jnp.where(upper, other[n], own[n])
                m = split(unpack_map(up[face:], face))
                message[n, pl.ds(0, face)] = dot_split(m, split(low[:face])) + up[:face]
                mapped = dot_split(m, split(unpack_map(low[face:], face)))
                message[n, pl.ds(face, packed)] = pack_map(mapped, tracers)

        ins = {"place": place, "own": (own, WHOLE), "other": (other, WHOLE)}
        return run(body, "combine", ins, {"message": vmem(own.shape, F32)}, {}, dense // 100)["message"]

    def combine_second(stage, own, other, old):
        def body(place, own, other, message, **old):
            upper = bit(place, stage)
            for g, group in enumerate(groups):
                for n, c in enumerate(group):
                    mine, theirs = old["own%d" % g], old["other%d" % g]
                    m = jnp.where(upper, mine[n, pl.ds(face, packed)], theirs[n, pl.ds(face, packed)])
                    up = jnp.where(upper, own[c], other[c])
                    low = jnp.where(upper, other[c], own[c])
                    message[c] = dot_split(split(unpack_map(m, face)), split(low)) + up

        ins = {"place": place, "own": (own, WHOLE), "other": (other, WHOLE)}
        old = {"%s%d" % (k, g): (a[g], WHOLE) for g in range(len(groups)) for k, a in old.items()}
        names = {k: old[k] for k in sorted(old)}
        ordered = ins | names

        def by_name(**refs):
            body(**refs)

        return run(by_name, "combine", ordered, {"message": vmem(own.shape, F32)}, {}, dense // 100)["message"]

    def enter(place, group, inlet, offsets, mapped, rows_high, rows_low, sides, ends, stack, high, low):
        for n, c in enumerate(group):
            entering = inlet[c]
            for stage in reversed(range(stages)):
                m = split(unpack_map(mapped[stage](n, c), face))
                beyond = dot_split(m, split(entering)) + offsets[stage](n, c)
                entering = jnp.where(bit(place, stage), beyond, entering)
            e = split(entering)
            high[n, pl.ds(0, face)] = e[0]
            low[n, pl.ds(0, face)] = e[1]
            for p in range(count - 1):
                e = split(ends[n * count + p])
                high[n, pl.ds((p + 1) * face, face)] = e[0]
                low[n, pl.ds((p + 1) * face, face)] = e[1]
            span = pl.ds(0, wide)
            inflow = dot_split((rows_high[n, span], rows_low[n, span]), (high[n], low[n]))
            for p in range(count):
                i = n * count + p
                f = split(inflow[p * face : (p + 1) * face])
                stack[i, pl.ds(0, face)] = f[0]
                stack[i, pl.ds(face, face)] = sides[i, 0]
                stack[i, pl.ds(2 * face, face)] = f[1]
                stack[i, pl.ds(3 * face, face)] = sides[i, 1]
                stack[i, pl.ds(4 * face, face)] = f[0]
                stack[i, pl.ds(5 * face, face)] = sides[i, 0]

    def enter_first(group, state, received):
        size = len(group)
        last = group[-1] == cols - 1

        def body(
            order, place, inlet, rows_high, rows_low, sides, ends, free, side_maps, stack, high, low,
            trace=None, **received,
        ):
            got = [received["got%d" % s] for s in range(stages)]
            enter(
                place, group, inlet,
                [lambda n, c, r=r: r[n, pl.ds(0, face)] for r in got],
                [lambda n, c, r=r: r[n, pl.ds(face, packed)] for r in got],
                rows_high, rows_low, sides, ends, stack, high, low,
            )
            if last:
                for p in range(count):
                    i = (size - 1) * count + p
                    trace[order[cols - 1, 0, p]] = lateral_rows(free.at[i], per_side) + dot(
                        side_maps[i], stack[i]
                    )

        keys = ("rows_high", "rows_low", "sides", "ends", "free", "side_maps")
        ins = {"order": order, "place": place, "inlet": (inlet_trace, WHOLE)}
        ins |= {k: (state[k], WHOLE) for k in keys} | {"got%d" % s: (r, WHOLE) for s, r in enumerate(received)}
        outs = {"stack": vmem((size * count, 6 * face, tracers), BF16)}
        if last:
            outs["trace"] = vmem((count, face, tracers), F32)
        scratch = {"high": vmem((size, wide, tracers), BF16), "low": vmem((size, wide, tracers), BF16)}
        return run(body, "entering", ins, outs, scratch, dense // 50)

    def second(group, state):
        size = len(group)
        items = size * count

        def body(order, inv, maps, free, stack, rate, affinity, fresh, traces, source_high, source_low):
            for i in range(items + 1):
                if i < items:
                    swept = free[i] + dot(maps[i], stack[i])
                    traces[i // count, order[group[i // count], 0, i % count]] = lateral_rows(swept, per_side)
                    s = split(langmuir(swept, rate[...], affinity[...]))
                    source_high[i % 2], source_low[i % 2] = s
                if i > 0:
                    k = (i - 1) % 2
                    fresh[i - 1] = dot(inv[i - 1], source_high[k]) + dot(inv[i - 1], source_low[k])

        ins = {"order": order} | {k: (state[k], WHOLE) for k in ("inv", "maps", "free", "stack")}
        ins |= {"rate": rate, "affinity": aff}
        outs = {
            "fresh": vmem((items, nodes, tracers), F32),
            "traces": vmem((size, count, face, tracers), F32),
        }
        scratch = {
            "source_high": vmem((2, nodes, tracers), BF16),
            "source_low": vmem((2, nodes, tracers), BF16),
        }
        return run(body, "second_sweep", ins, outs, scratch, 3 * size * dense)

    def spread(states, keys):
        return {"%s%d" % (k, g): (state[k], WHOLE) for g, state in enumerate(states) for k in keys}

    def second_sides(states, arrived):
        def body(order, place, arrived, message, **refs):
            get = lambda key, g: refs["%s%d" % (key, g)]
            for g, group in enumerate(groups):
                for n, c in enumerate(group):
                    for p in range(count):
                        j = order[c, 0, p]
                        if c == 0:
                            side = arrived_side(place, arrived, j)
                        else:
                            h = next(h for h, other in enumerate(groups) if c - 1 in other)
                            side = get("traces", h)[groups[h].index(c - 1), j]
                        add_side(n * count + p, side, get("fresh", g), get("tails", g), get("sides", g), get("ends", g))
                    message[c] = offset(
                        n, get("rows_high", g), get("rows_low", g), get("ends", g), get("high", g), get("low", g)
                    )

        ins = {"order": order, "place": place, "arrived": (arrived, WHOLE)}
        ins |= spread(states, ("fresh", "traces", "tails", "rows_high", "rows_low"))
        outs = {"message": vmem((cols, face, tracers), F32)}
        scratch = {}
        for g, group in enumerate(groups):
            outs |= {"%s%d" % (k, g): v for k, v in side_outs(len(group)).items()}
            scratch |= {"%s%d" % (k, g): v for k, v in offset_scratch(len(group)).items()}
        return run(body, "second_sides", ins, outs, scratch, dense // 50)

    def result(states, offsets):
        def body(order, place, inlet, out, staged, sems, **refs):
            get = lambda key, g: refs["%s%d" % (key, g)]
            started = []
            for g, group in enumerate(groups):
                enter(
                    place, group, inlet,
                    [lambda n, c, s=s: refs["offset%d" % s][c] for s in range(stages)],
                    [lambda n, c, s=s: refs["mapped%d_%d" % (s, g)][n, pl.ds(face, packed)] for s in range(stages)],
                    get("rows_high", g), get("rows_low", g), get("sides", g), get("ends", g),
                    get("stack", g), get("high", g), get("low", g),
                )
            for g, group in enumerate(groups):
                for n, c in enumerate(group):
                    for p in range(count):
                        i, k = n * count + p, len(started)
                        staged[k] = (get("fresh", g)[i] + dot(get("maps", g)[i], get("stack", g)[i])).astype(BF16)
                        copy = pltpu.make_async_copy(staged.at[k], out.at[c, 0, order[c, 0, p]], sems.at[k])
                        copy.start()
                        started.append(copy)
            for copy in started:
                copy.wait()

        ins = {"order": order, "place": place, "inlet": (inlet_trace, WHOLE)}
        ins |= {"offset%d" % s: (o, WHOLE) for s, o in enumerate(offsets)}
        for g, state in enumerate(states):
            ins |= {"mapped%d_%d" % (s, g): (r, WHOLE) for s, r in enumerate(state["received"])}
        ins |= spread(states, ("rows_high", "rows_low", "sides", "ends", "fresh", "maps"))
        scratch = {
            "staged": vmem((cols * count, nodes, tracers), BF16),
            "sems": pltpu.SemaphoreType.DMA((cols * count,)),
        }
        for g, group in enumerate(groups):
            scratch["stack%d" % g] = vmem((len(group) * count, 6 * face, tracers), BF16)
            scratch["high%d" % g] = vmem((len(group), wide, tracers), BF16)
            scratch["low%d" % g] = vmem((len(group), wide, tracers), BF16)
        outs = {"out": jax.ShapeDtypeStruct(previous.shape, BF16)}
        return run(body, "result", ins, outs, scratch, cols * dense)["out"]

    def exchange_first(message):
        sent, received = [message], [swap(message, 0)] if stages else []
        for stage in range(1, stages):
            sent.append(combine_first(stage - 1, sent[-1], received[-1]))
            received.append(swap(sent[-1], stage))
        return sent, received

    states = []
    for group in groups:
        state = first(group)
        if 0 in group:
            state |= first_sides(state, arrived)
        state["sent"], state["received"] = exchange_first(state["message"])
        states.append(state)
    for group, state in zip(groups, states):
        state |= enter_first(group, state, state["received"])
        if "trace" in state:
            arrived = to_next(state["trace"])
    for group, state in zip(groups, states):
        state |= second(group, state)
    sided = second_sides(states, arrived)
    for g, state in enumerate(states):
        state["sides"], state["ends"] = sided["sides%d" % g], sided["ends%d" % g]
    message, offsets = sided["message"], []
    for stage in range(stages):
        offsets.append(swap(message, stage))
        if stage + 1 < stages:
            old = {"own": [s["sent"][stage] for s in states], "other": [s["received"][stage] for s in states]}
            message = combine_second(stage, message, offsets[-1], old)
    return result(states, offsets)


def solution(mesh):
    placed = (
        P("lat", "stream", None, None, None),
        P("lat", "stream", None, None, None),
        P("lat", "stream", None, None, None),
        P("lat", None, None),
        P("lat", "stream", None, None, None),
        P(),
        P(),
        P("lat", "stream", None),
    )
    return jax.shard_map(
        per_device,
        mesh=mesh,
        in_specs=placed,
        out_specs=P("lat", "stream", None, None, None),
        check_vma=False,
    )
```

```python
from types import SimpleNamespace

import jax
import jax.numpy as jnp
from jax import lax
from jax.experimental import pallas as pl
from jax.experimental.pallas import tpu as pltpu
from jax.sharding import PartitionSpec as P

NODES_1D = 8
F32 = jnp.float32
BF16 = jnp.bfloat16
MIB = 1 << 20
VMEM = pltpu.VMEM
HBM = pltpu.HBM
SMEM = pltpu.SMEM


def run(body, name, ins, outs, scratch, flops):
    pairs = [a if isinstance(a, tuple) else (a, VMEM) for a in ins]
    return pl.pallas_call(
        body,
        name=name,
        in_specs=[pl.BlockSpec(memory_space=space) for _, space in pairs],
        out_specs=[pl.BlockSpec(memory_space=o.memory_space) for o in outs],
        out_shape=outs,
        scratch_shapes=scratch,
        cost_estimate=pl.CostEstimate(flops=flops, bytes_accessed=MIB, transcendentals=0),
        compiler_params=pltpu.CompilerParams(vmem_limit_bytes=24 * MIB),
    )(*[a if space is VMEM else pltpu.with_memory_space_constraint(a, space) for a, space in pairs])


def split(x):
    high = x.astype(BF16)
    return high, (x - high.astype(F32)).astype(BF16)


def dot(x, y):
    return jnp.dot(x, y, preferred_element_type=F32)


def dot_split(x, y):
    return dot(x[0], y[0]) + (dot(x[0], y[1]) + dot(x[1], y[0]))


def langmuir(lagged, rate, affinity):
    return rate * lagged * pltpu.reciprocal(1.0 + affinity * jnp.abs(lagged), approx=True)


def lateral_rows(field, per_side):
    plane = per_side * per_side
    return jnp.concatenate(
        [field[a * plane + plane - per_side : (a + 1) * plane] for a in range(per_side)], axis=0
    )


def pack_map(mapping, lanes):
    face = mapping.shape[0]
    rows = face * face // lanes
    return jnp.concatenate([mapping[q * rows : (q + 1) * rows] for q in range(lanes // face)], axis=1)


def unpack_map(packed, face):
    return jnp.concatenate(
        [packed[:, q * face : (q + 1) * face] for q in range(packed.shape[1] // face)], axis=0
    )


def bit(stage):
    return ((lax.axis_index("stream") >> stage) & 1) == 1


def per_device(inverse, upwind, lateral, inlet_trace, previous, uptake_rate, affinity, flow_order):
    cols, _, count, nodes, _ = inverse.shape
    face = upwind.shape[3]
    tracers = previous.shape[-1]
    per_side = NODES_1D
    plane = per_side * per_side
    wide = count * face
    packed = face * face // tracers
    streams, lats = lax.axis_size("stream"), lax.axis_size("lat")
    stages = streams.bit_length() - 1
    assert streams == 1 << stages
    groups = [list(range(1, cols)), [0]] if cols > 1 else [[0]]
    home = {c: (g, n) for g, group in enumerate(groups) for n, c in enumerate(group)}
    dense = 2 * count * nodes * nodes * tracers

    def to_next(value):
        return lax.ppermute(value, "lat", [(i, (i + 1) % lats) for i in range(lats)])

    def swap(value, stage):
        return lax.ppermute(value, "stream", [(i, i ^ (1 << stage)) for i in range(streams)])

    shaped = previous.reshape(cols, count, per_side, plane, tracers)

    def load_small(old, order, rate, aff, inlet, o_trace, o_old, o_order, o_rate, o_aff, o_inlet, staged, sems):
        rows = pl.ds(plane - 2 * per_side, 2 * per_side)
        copies = [pltpu.make_async_copy(old.at[c, :, :, rows], staged.at[c], sems.at[c]) for c in range(cols)]
        small = ((order, o_order), (rate, o_rate), (aff, o_aff), (inlet, o_inlet))
        copies += [pltpu.make_async_copy(a, b, sems.at[cols + k]) for k, (a, b) in enumerate(small)]
        for copy in reversed(copies[:cols]):
            copy.start()
        for copy in copies[cols:]:
            copy.start()
        for c in reversed(range(cols)):
            copies[c].wait()
            for j in range(count):
                for a in range(per_side):
                    part = staged[c, j, a].astype(F32)[per_side:]
                    if c == cols - 1:
                        o_trace[j, pl.ds(a * per_side, per_side)] = part
                    else:
                        o_old[c, j, pl.ds(a * per_side, per_side)] = part
        for copy in copies[cols:]:
            copy.wait()

    trace, old, order, rate, aff, inlet = run(
        load_small,
        "load_small",
        [
            (shaped, HBM),
            (flow_order.reshape(cols, count), HBM),
            (uptake_rate.reshape(1, tracers), HBM),
            (affinity.reshape(1, tracers), HBM),
            (inlet_trace, HBM),
        ],
        [
            VMEM((count, face, tracers), F32),
            VMEM((max(cols - 1, 1), count, face, tracers), F32),
            SMEM((cols, count), jnp.int32),
            VMEM((1, tracers), F32),
            VMEM((1, tracers), F32),
            VMEM((cols, face, tracers), F32),
        ],
        [VMEM((cols, count, per_side, 2 * per_side, tracers), BF16), pltpu.SemaphoreType.DMA((cols + 4,))],
        dense // 100,
    )
    order = (order, SMEM)
    arrived = to_next(trace)

    def end_of(free, tails, i, s):
        return free[i, pl.ds(nodes - face, face)] + dot_split(split(tails[i][:, face:]), s)

    def offset(n, rows_high, rows_low, ends, high, low):
        for p in range(count - 1):
            e = split(ends[n * count + p])
            high[n, pl.ds(p * face, face)] = e[0]
            low[n, pl.ds(p * face, face)] = e[1]
        last = pl.ds(wide, face)
        row = (rows_high[n, last][:, face:], rows_low[n, last][:, face:])
        return ends[n * count + count - 1] + dot_split(row, (high[n], low[n]))

    def side_outs(size):
        return [VMEM((size * count, 2, face, tracers), BF16), VMEM((size * count, face, tracers), F32)]

    def offset_scratch(size):
        return [VMEM((size, wide - face, tracers), BF16)] * 2

    def sweep_scratch():
        return [VMEM((2, nodes, tracers), BF16)] * 2

    def loaded(size):
        return [
            VMEM((size * count, nodes, nodes), BF16),
            VMEM((size * count, 2 * face, nodes), BF16),
            VMEM((size * count, nodes, tracers), BF16),
        ]

    def first(g, fetched):
        group = groups[g]
        size = len(group)
        items = size * count
        local = group[0] > 0
        loads = fetched is None

        def body(*refs):
            refs = list(refs)
            take = lambda k: [refs.pop(0) for _ in range(k)]
            (order_r,) = take(1)
            if loads:
                hbm = take(4)
            else:
                fields = take(3)
            rate_r, aff_r, old_r = take(3)
            if loads:
                fields_of = [take(1) if h == g else take(3) for h in range(len(groups))]
            maps, free, side_maps, tails, rows_high, rows_low, message = take(7)
            if local:
                sides, ends = take(2)
            source_high, source_low, row = take(3)
            if loads:
                (sems,) = take(1)
                fields_of[g] += take(2)
                fields = fields_of[g]

                def copies(h, i):
                    c, j = groups[h][i // count], i % count
                    to_inv, to_faces, to_lagged = fields_of[h]
                    k = c * count + j
                    return (
                        pltpu.make_async_copy(hbm[3].at[c, 0, j], to_lagged.at[i], sems.at[0, k]),
                        pltpu.make_async_copy(hbm[1].at[c, 0, j], to_faces.at[i, pl.ds(0, face)], sems.at[1, k]),
                        pltpu.make_async_copy(hbm[2].at[c, 0, j], to_faces.at[i, pl.ds(face, face)], sems.at[2, k]),
                        pltpu.make_async_copy(hbm[0].at[c, 0, j], to_inv.at[i], sems.at[3, k]),
                    )

                for h in range(len(groups)):
                    for i in range(len(groups[h]) * count):
                        for copy in copies(h, i):
                            copy.start()

            inv, faces, lagged = fields
            for i in range(items + 1):
                if i < items:
                    if loads:
                        for copy in copies(g, i):
                            copy.wait()
                    both = lax.dot_general(
                        inv[i], faces[i], (((1,), (1,)), ((), ())), preferred_element_type=F32
                    )
                    b_high, b_low = split(both)
                    maps[i] = jnp.concatenate([b_high, b_high, b_low], axis=1)
                    tails[i] = both[nodes - face :]
                    s = split(lateral_rows(both, per_side))
                    side_maps[i] = jnp.concatenate([s[0], s[0], s[1]], axis=1)
                    s = split(langmuir(lagged[i].astype(F32), rate_r[...], aff_r[...]))
                    source_high[i % 2], source_low[i % 2] = s
                if i > 0:
                    k = (i - 1) % 2
                    free[i - 1] = dot(inv[i - 1], source_high[k]) + dot(inv[i - 1], source_low[k])

            row_id = lax.broadcasted_iota(jnp.int32, (face, wide), 0)
            lane_id = lax.broadcasted_iota(jnp.int32, (face, wide), 1)
            outflow = [None] * size
            for p in range(count):
                for n, c in enumerate(group):
                    j = order_r[c, p]
                    i = n * count + j
                    step = split(tails[i][:, :face])
                    unit = jnp.where(lane_id == row_id + p * face, 1.0, 0.0)
                    r = split(unit if p == 0 else row[n] + unit)
                    rows_high[n, pl.ds(p * face, face)] = r[0]
                    rows_low[n, pl.ds(p * face, face)] = r[1]
                    row[n] = dot_split(step, r)
                    if local:
                        s = split(old_r[c - 1, j])
                        sides[n * count + p, 0] = s[0]
                        sides[n * count + p, 1] = s[1]
                        end = end_of(free, tails, i, s)
                        ends[n * count + p] = end
                        outflow[n] = end if p == 0 else end + dot_split(step, split(outflow[n]))
            for n in range(size):
                r = split(row[n])
                rows_high[n, pl.ds(wide, face)] = r[0]
                rows_low[n, pl.ds(wide, face)] = r[1]
                message[n, pl.ds(face, packed)] = pack_map(row[n][:, :face], tracers)
                if local:
                    message[n, pl.ds(0, face)] = outflow[n]
            if loads:
                for h in range(len(groups)):
                    if h != g:
                        for i in range(len(groups[h]) * count):
                            for copy in copies(h, i):
                                copy.wait()

        outs = [
            VMEM((items, nodes, 6 * face), BF16),
            VMEM((items, nodes, tracers), F32),
            VMEM((items, face, 6 * face), BF16),
            VMEM((items, face, 2 * face), F32),
            VMEM((size, wide + face, wide), BF16),
            VMEM((size, wide + face, wide), BF16),
            VMEM((size, face + packed, tracers), F32),
        ]
        if local:
            outs += side_outs(size)
        scratch = sweep_scratch() + [VMEM((size, face, wide), F32)]
        if loads:
            others = [loaded(len(groups[h])) for h in range(len(groups))]
            scratch += [pltpu.SemaphoreType.DMA((4, cols * count))] + others[g][1:]
            others[g] = others[g][:1]
            outs = sum(others, []) + outs
            fields = [(a, HBM) for a in (inverse, upwind, lateral, previous)]
        else:
            fields = fetched[g]
        values = run(body, "first", [order, *fields, rate, aff, old], outs, scratch, 3 * size * dense)
        if loads:
            fetched = []
            for other in others:
                fetched.append(values[: len(other)])
                values = values[len(other) :]
        state = SimpleNamespace(inv=fetched[g][0])
        state.maps, state.free, state.side_maps, state.tails, state.high, state.low, state.message = values[:7]
        if local:
            state.sides, state.ends = values[7:]
        return state, fetched

    def arrived_side(arrived, j):
        return split(jnp.where(lax.axis_index("lat") > 0, arrived[j], 0.0))

    def first_sides(state, arrived):
        def body(order, arrived, free, tails, rows_high, rows_low, mapped, sides, ends, message, high, low):
            for p in range(count):
                j = order[0, p]
                s = arrived_side(arrived, j)
                sides[p, 0] = s[0]
                sides[p, 1] = s[1]
                ends[p] = end_of(free, tails, j, s)
            message[0, pl.ds(0, face)] = offset(0, rows_high, rows_low, ends, high, low)
            message[0, pl.ds(face, packed)] = mapped[0, pl.ds(face, packed)]

        state.sides, state.ends, state.message = run(
            body,
            "first_sides",
            [order, arrived, state.free, state.tails, state.high, state.low, state.message],
            side_outs(1) + [VMEM((1, face + packed, tracers), F32)],
            offset_scratch(1),
            dense // 50,
        )

    def combine_first(stage, own, other):
        def body(own, other, message):
            upper = bit(stage)
            for n in range(own.shape[0]):
                up = jnp.where(upper, own[n], other[n])
                low = jnp.where(upper, other[n], own[n])
                m = split(unpack_map(up[face:], face))
                message[n, pl.ds(0, face)] = dot_split(m, split(low[:face])) + up[:face]
                mapped = dot_split(m, split(unpack_map(low[face:], face)))
                message[n, pl.ds(face, packed)] = pack_map(mapped, tracers)

        return run(body, "combine", [own, other], [VMEM(own.shape, F32)], [], dense // 100)[0]

    def combine_second(stage, own, other, old_own, old_other):
        def body(own, other, *refs):
            message = refs[-1]
            upper = bit(stage)
            for c in range(cols):
                g, n = home[c]
                mine, theirs = refs[2 * g], refs[2 * g + 1]
                m = jnp.where(upper, mine[n, pl.ds(face, packed)], theirs[n, pl.ds(face, packed)])
                up = jnp.where(upper, own[c], other[c])
                low = jnp.where(upper, other[c], own[c])
                message[c] = dot_split(split(unpack_map(m, face)), split(low)) + up

        ins = [own, other]
        for pair in zip(old_own, old_other):
            ins += pair
        return run(body, "combine", ins, [VMEM(own.shape, F32)], [], dense // 100)[0]

    def enter(group, order, inlet, offsets, mapped, rows_high, rows_low, sides, ends, stack, high, low):
        for n, c in enumerate(group):
            entering = inlet[c]
            for stage in reversed(range(stages)):
                m = split(unpack_map(mapped[stage](n, c), face))
                beyond = dot_split(m, split(entering)) + offsets[stage](n, c)
                entering = jnp.where(bit(stage), beyond, entering)
            e = split(entering)
            high[n, pl.ds(0, face)] = e[0]
            low[n, pl.ds(0, face)] = e[1]
            for p in range(count - 1):
                e = split(ends[n * count + p])
                high[n, pl.ds((p + 1) * face, face)] = e[0]
                low[n, pl.ds((p + 1) * face, face)] = e[1]
            span = pl.ds(0, wide)
            inflow = dot_split((rows_high[n, span], rows_low[n, span]), (high[n], low[n]))
            for p in range(count):
                i = n * count + order[c, p]
                f = split(inflow[p * face : (p + 1) * face])
                side = (sides[n * count + p, 0], sides[n * count + p, 1])
                for q, part in enumerate((f[0], side[0], f[1], side[1], f[0], side[0])):
                    stack[i, pl.ds(q * face, face)] = part

    def enter_scratch(size):
        return [VMEM((size, wide, tracers), BF16)] * 2

    def enter_first(group, state):
        size = len(group)
        last = group[-1] == cols - 1

        def body(order, inlet, rows_high, rows_low, sides, ends, free, side_maps, *refs):
            got, refs = refs[:stages], refs[stages:]
            stack, (high, low) = refs[0], refs[-2:]
            enter(
                group, order, inlet,
                [lambda n, c, r=r: r[n, pl.ds(0, face)] for r in got],
                [lambda n, c, r=r: r[n, pl.ds(face, packed)] for r in got],
                rows_high, rows_low, sides, ends, stack, high, low,
            )
            if last:
                for j in range(count):
                    i = (size - 1) * count + j
                    refs[1][j] = lateral_rows(free.at[i], per_side) + dot(side_maps[i], stack[i])

        outs = [VMEM((size * count, 6 * face, tracers), BF16)]
        if last:
            outs.append(VMEM((count, face, tracers), F32))
        ins = [order, inlet, state.high, state.low, state.sides, state.ends, state.free, state.side_maps]
        values = run(body, "enter", ins + state.received, outs, enter_scratch(size), dense // 50)
        state.stack = values[0]
        return values[1] if last else None

    def second(group, state):
        size = len(group)
        items = size * count

        def body(inv, maps, free, stack, rate, aff, fresh, traces, source_high, source_low):
            for i in range(items + 1):
                if i < items:
                    swept = free[i] + dot(maps[i], stack[i])
                    traces[i // count, i % count] = lateral_rows(swept, per_side)
                    source_high[i % 2], source_low[i % 2] = split(langmuir(swept, rate[...], aff[...]))
                if i > 0:
                    k = (i - 1) % 2
                    fresh[i - 1] = dot(inv[i - 1], source_high[k]) + dot(inv[i - 1], source_low[k])

        state.fresh, state.traces = run(
            body,
            "second",
            [state.inv, state.maps, state.free, state.stack, rate, aff],
            [VMEM((items, nodes, tracers), F32), VMEM((size, count, face, tracers), F32)],
            sweep_scratch(),
            3 * size * dense,
        )

    def second_sides(arrived):
        per = 5

        def body(order, arrived, *refs):
            got = [refs[per * g : per * g + per] for g in range(len(groups))]
            refs = refs[per * len(groups) :]
            message, refs = refs[0], refs[1:]
            for g, group in enumerate(groups):
                fresh, _, tails, rows_high, rows_low = got[g]
                sides, ends = refs[2 * g : 2 * g + 2]
                high, low = refs[2 * (len(groups) + g) : 2 * (len(groups) + g) + 2]
                for n, c in enumerate(group):
                    for p in range(count):
                        j = order[c, p]
                        if c == 0:
                            s = arrived_side(arrived, j)
                        else:
                            h, m = home[c - 1]
                            s = split(got[h][1][m, j])
                        sides[n * count + p, 0] = s[0]
                        sides[n * count + p, 1] = s[1]
                        ends[n * count + p] = end_of(fresh, tails, n * count + j, s)
                    message[c] = offset(n, rows_high, rows_low, ends, high, low)

        ins = [order, arrived]
        outs, scratch = [VMEM((cols, face, tracers), F32)], []
        for group, state in zip(groups, states):
            ins += [state.fresh, state.traces, state.tails, state.high, state.low]
            outs += side_outs(len(group))
            scratch += offset_scratch(len(group))
        message, *values = run(body, "second_sides", ins, outs, scratch, dense // 50)
        for g, state in enumerate(states):
            state.sides, state.ends = values[2 * g : 2 * g + 2]
        return message

    def result(offsets):
        per = 6 + stages

        def body(order, inlet, *refs):
            offs, refs = refs[:stages], refs[stages:]
            got = [refs[per * g : per * g + per] for g in range(len(groups))]
            out, staged, sems, *refs = refs[per * len(groups) :]
            for g, group in enumerate(groups):
                rows_high, rows_low, sides, ends, _, _, *mapped = got[g]
                enter(
                    group, order, inlet,
                    [lambda n, c, r=r: r[c] for r in offs],
                    [lambda n, c, r=r: r[n, pl.ds(face, packed)] for r in mapped],
                    rows_high, rows_low, sides, ends, *refs[3 * g : 3 * g + 3],
                )
            started = []
            for g, group in enumerate(groups):
                fresh, maps = got[g][4:6]
                for n, c in enumerate(group):
                    for j in range(count):
                        i, k = n * count + j, len(started)
                        staged[k] = (fresh[i] + dot(maps[i], refs[3 * g][i])).astype(BF16)
                        copy = pltpu.make_async_copy(staged.at[k], out.at[c, 0, j], sems.at[k])
                        copy.start()
                        started.append(copy)
            for copy in started:
                copy.wait()

        ins = [order, inlet, *offsets]
        scratch = [VMEM((cols * count, nodes, tracers), BF16), pltpu.SemaphoreType.DMA((cols * count,))]
        for group, state in zip(groups, states):
            ins += [state.high, state.low, state.sides, state.ends, state.fresh, state.maps, *state.received]
            scratch += [VMEM((len(group) * count, 6 * face, tracers), BF16)] + enter_scratch(len(group))
        return run(body, "result", ins, [HBM(previous.shape, BF16)], scratch, cols * dense)[0]

    states, fetched = [], None
    for g, group in enumerate(groups):
        state, fetched = first(g, fetched)
        if 0 in group:
            first_sides(state, arrived)
        state.sent, state.received = [state.message], []
        for stage in range(stages):
            if stage:
                state.sent.append(combine_first(stage - 1, state.sent[-1], state.received[-1]))
            state.received.append(swap(state.sent[-1], stage))
        states.append(state)
    for group, state in zip(groups, states):
        trace = enter_first(group, state)
        if trace is not None:
            arrived = to_next(trace)
    for group, state in zip(groups, states):
        second(group, state)
    message, offsets = second_sides(arrived), []
    for stage in range(stages):
        offsets.append(swap(message, stage))
        if stage + 1 < stages:
            message = combine_second(
                stage, message, offsets[-1], [s.sent[stage] for s in states], [s.received[stage] for s in states]
            )
    return result(offsets)


def solution(mesh):
    placed = (
        P("lat", "stream", None, None, None),
        P("lat", "stream", None, None, None),
        P("lat", "stream", None, None, None),
        P("lat", None, None),
        P("lat", "stream", None, None, None),
        P(),
        P(),
        P("lat", "stream", None),
    )
    return jax.shard_map(
        per_device,
        mesh=mesh,
        in_specs=placed,
        out_specs=P("lat", "stream", None, None, None),
        check_vma=False,
    )
```

```python
from types import SimpleNamespace

import jax
import jax.numpy as jnp
from jax import lax
from jax.experimental import pallas as pl
from jax.experimental.pallas import tpu as pltpu
from jax.sharding import PartitionSpec as P

NODES_1D = 8
F32 = jnp.float32
BF16 = jnp.bfloat16
MIB = 1 << 20
VMEM = pltpu.VMEM
HBM = pltpu.HBM
SMEM = pltpu.SMEM


def run(body, name, ins, outs, scratch, flops):
    pairs = [a if isinstance(a, tuple) else (a, VMEM) for a in ins]
    return pl.pallas_call(
        body,
        name=name,
        in_specs=[pl.BlockSpec(memory_space=space) for _, space in pairs],
        out_specs=[pl.BlockSpec(memory_space=o.memory_space) for o in outs],
        out_shape=outs,
        scratch_shapes=scratch,
        cost_estimate=pl.CostEstimate(flops=flops, bytes_accessed=MIB, transcendentals=0),
        compiler_params=pltpu.CompilerParams(vmem_limit_bytes=24 * MIB),
    )(*[a if space is VMEM else pltpu.with_memory_space_constraint(a, space) for a, space in pairs])


def split(x):
    high = x.astype(BF16)
    return high, (x - high.astype(F32)).astype(BF16)


def dot(x, y):
    return jnp.dot(x, y, preferred_element_type=F32)


def dot_split(x, y):
    return dot(x[0], y[0]) + (dot(x[0], y[1]) + dot(x[1], y[0]))


def langmuir(lagged, rate, affinity):
    return rate * lagged * pltpu.reciprocal(1.0 + affinity * jnp.abs(lagged), approx=True)


def lateral_rows(field, per_side):
    plane = per_side * per_side
    return jnp.concatenate(
        [field[a * plane + plane - per_side : (a + 1) * plane] for a in range(per_side)], axis=0
    )


def pack_map(mapping, lanes):
    face = mapping.shape[0]
    rows = face * face // lanes
    return jnp.concatenate([mapping[q * rows : (q + 1) * rows] for q in range(lanes // face)], axis=1)


def unpack_map(packed, face):
    return jnp.concatenate(
        [packed[:, q * face : (q + 1) * face] for q in range(packed.shape[1] // face)], axis=0
    )


def stack_maps(both):
    face = both.shape[1] // 2
    turned = pltpu.roll(both, face, 1)
    first = lax.broadcasted_iota(jnp.int32, both.shape, 1) < face
    low = split(both)[1]
    return jnp.concatenate(
        [jnp.where(first, both, turned).astype(BF16), low, jnp.where(first, turned, both).astype(BF16)], axis=1
    )


def stack_inflow(f):
    return (f[0], f[1], f[0])


def stack_side(s):
    return (s[0], s[0], s[1])


def bit(stage):
    return ((lax.axis_index("stream") >> stage) & 1) == 1


def per_device(inverse, upwind, lateral, inlet_trace, previous, uptake_rate, affinity, flow_order):
    cols, _, count, nodes, _ = inverse.shape
    face = upwind.shape[3]
    tracers = previous.shape[-1]
    per_side = NODES_1D
    plane = per_side * per_side
    wide = count * face
    packed = face * face // tracers
    streams, lats = lax.axis_size("stream"), lax.axis_size("lat")
    stages = streams.bit_length() - 1
    assert streams == 1 << stages
    assert cols > 1
    early, late = list(range(1, cols)), [0]
    groups = [early, late]
    home = {c: (g, n) for g, group in enumerate(groups) for n, c in enumerate(group)}
    ending = pl.ds(nodes - face, face)
    dense = 2 * count * nodes * nodes * tracers

    def to_next(value):
        return lax.ppermute(value, "lat", [(i, (i + 1) % lats) for i in range(lats)])

    def swap(value, stage):
        return lax.ppermute(value, "stream", [(i, i ^ (1 << stage)) for i in range(streams)])

    shaped = previous.reshape(cols, count, per_side, plane, tracers)

    def face_outs(size):
        return [
            VMEM((size * count, nodes, 6 * face), BF16),
            VMEM((size * count, nodes, tracers), F32),
            VMEM((size * count, face, 6 * face), BF16),
        ]

    def chain_outs(size):
        return [
            VMEM((size * count, face, 2 * face), F32),
            VMEM((size, wide + face, wide), BF16),
            VMEM((size, wide + face, wide), BF16),
        ]

    def side_outs(size):
        return [VMEM((size * count, 2, face, tracers), BF16), VMEM((size * count, face, tracers), F32)]

    def offset_scratch(size):
        return [VMEM((size, wide - face, tracers), BF16)] * 2

    def source_outs(size):
        return [VMEM((size * count, nodes, tracers), BF16)] * 2

    def field_outs(size):
        return [VMEM((size * count, nodes, nodes), BF16), VMEM((size * count, 2 * face, nodes), BF16)]

    def times(inv, i, high, low, k, rows=None):
        matrix = inv[i] if rows is None else inv[i, rows]
        return dot(matrix, high[k]) + dot(matrix, low[k])

    def face_maps(inv, faces, i, rows=None):
        matrix = inv[i] if rows is None else inv[i, rows]
        return lax.dot_general(matrix, faces[i], (((1,), (1,)), ((), ())), preferred_element_type=F32)

    def side_of(tails, i, s):
        return dot_split(split(tails[i][:, face:]), s)

    def link(n, p, step, rows_high, rows_low, row):
        row_id = lax.broadcasted_iota(jnp.int32, (face, wide), 0)
        lane_id = lax.broadcasted_iota(jnp.int32, (face, wide), 1)
        unit = jnp.where(lane_id == row_id + p * face, 1.0, 0.0)
        r = split(unit if p == 0 else row + unit)
        rows_high[n, pl.ds(p * face, face)] = r[0]
        rows_low[n, pl.ds(p * face, face)] = r[1]
        row = dot_split(step, r)
        if p == count - 1:
            r = split(row)
            rows_high[n, pl.ds(wide, face)] = r[0]
            rows_low[n, pl.ds(wide, face)] = r[1]
        return row

    def offset(n, rows_high, rows_low, ends, high, low):
        for p in range(count - 1):
            e = split(ends[n * count + p])
            high[n, pl.ds(p * face, face)] = e[0]
            low[n, pl.ds(p * face, face)] = e[1]
        last = pl.ds(wide, face)
        row = (rows_high[n, last][:, face:], rows_low[n, last][:, face:])
        return ends[n * count + count - 1] + dot_split(row, (high[n], low[n]))

    def begin():
        size = len(early)
        items = size * count

        def body(
            order, rate, aff, inlet, old, inverse, upwind, lateral, previous,
            trace, o_order, o_rate, o_aff, o_inlet, inv, faces, source_high, source_low,
            tails, rows_high, rows_low, sides, ends, message, lagged, staged, sems,
        ):
            counter = iter(range(sems.shape[0]))
            copy = lambda a, b: pltpu.make_async_copy(a, b, sems.at[next(counter)])
            lead = [copy(rate, o_rate), copy(aff, o_aff), copy(order, o_order)]
            parts = []
            for i in range(items):
                c, j = early[i // count], i % count
                parts.append([
                    copy(previous.at[c, 0, j], lagged.at[i]),
                    copy(inverse.at[c, 0, j, ending], inv.at[i, ending]),
                    copy(upwind.at[c, 0, j], faces.at[i, pl.ds(0, face)]),
                    copy(lateral.at[c, 0, j], faces.at[i, pl.ds(face, face)]),
                ])
            side = copy(old.at[0, :, :, pl.ds(plane - 2 * per_side, 2 * per_side)], staged)
            rest = [copy(inlet, o_inlet)]
            body_rows = pl.ds(0, nodes - face)
            for i in range(items):
                c, j = early[i // count], i % count
                rest.append(copy(inverse.at[c, 0, j, body_rows], inv.at[i, body_rows]))
            for one in lead + sum(parts, []) + [side]:
                one.start()
            for i in range(items):
                for one in (lead if i == 0 else []) + parts[i]:
                    one.wait()
                if i == min(1, items - 1):
                    for one in rest:
                        one.start()
                lag = lagged[i].astype(F32)
                if early[i // count] == cols - 1:
                    trace[i % count] = lateral_rows(lag, per_side)
                source_high[i], source_low[i] = split(langmuir(lag, o_rate[...], o_aff[...]))
                tails[i] = face_maps(inv, faces, i, ending)
                ends[i] = times(inv, i, source_high, source_low, i, ending)
            side.wait()
            rows, outflow, own = [None] * size, [None] * size, {}
            for n in range(size):
                for p in range(count):
                    own[n, p] = ends[n * count + o_order[early[n], p]]
            for p in range(count):
                for n, c in enumerate(early):
                    j = o_order[c, p]
                    i = n * count + j
                    step = split(tails[i][:, :face])
                    rows[n] = link(n, p, step, rows_high, rows_low, rows[n])
                    if c == 1:
                        s = [staged[j, a].astype(F32)[per_side:] for a in range(per_side)]
                        s = split(jnp.concatenate(s, axis=0))
                    else:
                        s = split(lateral_rows(lagged[i - count].astype(F32), per_side))
                    sides[n * count + p, 0] = s[0]
                    sides[n * count + p, 1] = s[1]
                    end = own[n, p] + side_of(tails, i, s)
                    ends[n * count + p] = end
                    outflow[n] = end if p == 0 else end + dot_split(step, split(outflow[n]))
            for n in range(size):
                message[n, pl.ds(0, face)] = outflow[n]
                message[n, pl.ds(face, packed)] = pack_map(rows[n][:, :face], tracers)
            for one in rest:
                one.wait()

        values = run(
            body,
            "begin",
            [
                (flow_order.reshape(cols, count), HBM),
                (uptake_rate.reshape(1, tracers), HBM),
                (affinity.reshape(1, tracers), HBM),
                (inlet_trace, HBM),
                (shaped, HBM),
                (inverse, HBM),
                (upwind, HBM),
                (lateral, HBM),
                (previous, HBM),
            ],
            [
                VMEM((count, face, tracers), F32),
                SMEM((cols, count), jnp.int32),
                VMEM((1, tracers), F32),
                VMEM((1, tracers), F32),
                VMEM((cols, face, tracers), F32),
                *field_outs(size),
                *source_outs(size),
                *chain_outs(size),
                *side_outs(size),
                VMEM((size, face + packed, tracers), F32),
            ],
            [
                VMEM((items, nodes, tracers), BF16),
                VMEM((count, per_side, 2 * per_side, tracers), BF16),
                pltpu.SemaphoreType.DMA((5 + 5 * items,)),
            ],
            size * dense,
        )
        state = SimpleNamespace()
        state.inv, state.faces, state.source_high, state.source_low = values[5:9]
        state.tails, state.high, state.low, state.sides, state.ends, state.message = values[9:]
        return values[:5], state

    def finish_early(state, after):
        size = len(early)
        items = size * count

        def body(
            inv, faces, source_high, source_low, _, inverse, upwind, lateral, previous,
            maps, free, side_maps, o_inv, o_faces, o_lagged, sems,
        ):
            copies = []
            for i in range(len(late) * count):
                c, j = late[i // count], i % count
                for k, (a, b) in enumerate((
                    (previous.at[c, 0, j], o_lagged.at[i]),
                    (upwind.at[c, 0, j], o_faces.at[i, pl.ds(0, face)]),
                    (lateral.at[c, 0, j], o_faces.at[i, pl.ds(face, face)]),
                    (inverse.at[c, 0, j], o_inv.at[i]),
                )):
                    copies.append(pltpu.make_async_copy(a, b, sems.at[k, i]))
                    copies[-1].start()
            for i in range(items):
                both = face_maps(inv, faces, i)
                maps[i] = stack_maps(both)
                side_maps[i] = stack_maps(lateral_rows(both, per_side))
                free[i] = times(inv, i, source_high, source_low, i)
            for one in copies:
                one.wait()

        state.maps, state.free, state.side_maps, *fetched = run(
            body,
            "finish_early",
            [state.inv, state.faces, state.source_high, state.source_low, after]
            + [(a, HBM) for a in (inverse, upwind, lateral, previous)],
            face_outs(size) + field_outs(len(late)) + [VMEM((len(late) * count, nodes, tracers), BF16)],
            [pltpu.SemaphoreType.DMA((4, len(late) * count))],
            3 * size * dense,
        )
        return fetched

    def begin_late(fetched, after):
        size = len(late)
        items = size * count

        def body(
            order, inv, faces, lagged, rate, aff, _,
            maps, free, side_maps, tails, rows_high, rows_low, mapped, source_high, source_low,
        ):
            for i in range(items):
                tails[i] = face_maps(inv, faces, i, ending)
            rows = [None] * size
            for i in range(items + 1):
                if i < items:
                    both = face_maps(inv, faces, i)
                    maps[i] = stack_maps(both)
                    side_maps[i] = stack_maps(lateral_rows(both, per_side))
                    s = split(langmuir(lagged[i].astype(F32), rate[...], aff[...]))
                    source_high[i % 2], source_low[i % 2] = s
                    n, p = i // count, i % count
                    step = split(tails[n * count + order[late[n], p]][:, :face])
                    rows[n] = link(n, p, step, rows_high, rows_low, rows[n])
                if i > 0:
                    free[i - 1] = times(inv, i - 1, source_high, source_low, (i - 1) % 2)
            for n in range(size):
                mapped[n] = pack_map(rows[n][:, :face], tracers)

        state = SimpleNamespace(inv=fetched[0])
        values = run(
            body,
            "begin_late",
            [order, *fetched, rate, aff, after],
            face_outs(size) + chain_outs(size) + [VMEM((size, packed, tracers), F32)],
            [VMEM((2, nodes, tracers), BF16)] * 2,
            3 * size * dense,
        )
        state.maps, state.free, state.side_maps, state.tails, state.high, state.low, state.mapped = values
        return state

    def arrived_side(arrived, j):
        return split(jnp.where(lax.axis_index("lat") > 0, arrived[j], 0.0))

    def first_sides(state, arrived):
        def body(order, arrived, free, tails, rows_high, rows_low, mapped, sides, ends, message, high, low):
            for p in range(count):
                j = order[0, p]
                s = arrived_side(arrived, j)
                sides[p, 0] = s[0]
                sides[p, 1] = s[1]
                ends[p] = free[j, ending] + side_of(tails, j, s)
            message[0, pl.ds(0, face)] = offset(0, rows_high, rows_low, ends, high, low)
            message[0, pl.ds(face, packed)] = mapped[0]

        state.sides, state.ends, state.message = run(
            body,
            "first_sides",
            [order, arrived, state.free, state.tails, state.high, state.low, state.mapped],
            side_outs(1) + [VMEM((1, face + packed, tracers), F32)],
            offset_scratch(1),
            dense // 50,
        )

    def combine_first(stage, own, other):
        def body(own, other, message):
            upper = bit(stage)
            for n in range(own.shape[0]):
                up = jnp.where(upper, own[n], other[n])
                low = jnp.where(upper, other[n], own[n])
                m = split(unpack_map(up[face:], face))
                message[n, pl.ds(0, face)] = dot_split(m, split(low[:face])) + up[:face]
                mapped = dot_split(m, split(unpack_map(low[face:], face)))
                message[n, pl.ds(face, packed)] = pack_map(mapped, tracers)

        return run(body, "combine", [own, other], [VMEM(own.shape, F32)], [], dense // 100)[0]

    def combine_second(stage, own, other, old_own, old_other):
        def body(own, other, *refs):
            message = refs[-1]
            upper = bit(stage)
            for c in range(cols):
                g, n = home[c]
                mine, theirs = refs[2 * g], refs[2 * g + 1]
                m = jnp.where(upper, mine[n, pl.ds(face, packed)], theirs[n, pl.ds(face, packed)])
                up = jnp.where(upper, own[c], other[c])
                low = jnp.where(upper, other[c], own[c])
                message[c] = dot_split(split(unpack_map(m, face)), split(low)) + up

        ins = [own, other]
        for pair in zip(old_own, old_other):
            ins += pair
        return run(body, "combine", ins, [VMEM(own.shape, F32)], [], dense // 100)[0]

    def entering(start, offsets, maps):
        for stage in reversed(range(stages)):
            m = split(unpack_map(maps[stage], face))
            beyond = dot_split(m, split(start)) + offsets[stage]
            start = jnp.where(bit(stage), beyond, start)
        return start

    def enter_first(group, state):
        size = len(group)
        last = group[-1] == cols - 1

        def body(order, inlet, rows_high, rows_low, sides, ends, free, side_maps, *refs):
            got, refs = refs[:stages], refs[stages:]
            stack, (high, low) = refs[0], refs[-2:]
            for n, c in enumerate(group):
                for p in range(count - 1):
                    e = split(ends[n * count + p])
                    high[n, pl.ds((p + 1) * face, face)] = e[0]
                    low[n, pl.ds((p + 1) * face, face)] = e[1]
                maps = [r[n, pl.ds(face, packed)] for r in got]
                e = split(entering(inlet[c], [r[n, pl.ds(0, face)] for r in got], maps))
                high[n, pl.ds(0, face)] = e[0]
                low[n, pl.ds(0, face)] = e[1]
                span = pl.ds(0, wide)
                inflow = dot_split((rows_high[n, span], rows_low[n, span]), (high[n], low[n]))
                for p in range(count):
                    i = n * count + order[c, p]
                    f = split(inflow[p * face : (p + 1) * face])
                    s = (sides[n * count + p, 0], sides[n * count + p, 1])
                    for q, part in enumerate(stack_inflow(f) + stack_side(s)):
                        stack[i, pl.ds(q * face, face)] = part
            if last:
                for j in range(count):
                    i = (size - 1) * count + j
                    refs[1][j] = lateral_rows(free.at[i], per_side) + dot(side_maps[i], stack[i])

        outs = [VMEM((size * count, 6 * face, tracers), BF16)]
        if last:
            outs.append(VMEM((count, face, tracers), F32))
        ins = [order, inlet, state.high, state.low, state.sides, state.ends, state.free, state.side_maps]
        scratch = [VMEM((size, wide, tracers), BF16)] * 2
        values = run(body, "enter", ins + state.received, outs, scratch, dense // 50)
        state.stack = values[0]
        return values[1] if last else None

    def second_early(state, after):
        size = len(early)
        items = size * count

        def body(inv, maps, free, stack, rate, aff, _, fresh, traces, own, source_high, source_low):
            for i in range(items + 1):
                if i < items:
                    swept = free[i] + dot(maps[i], stack[i])
                    traces[i] = lateral_rows(swept, per_side)
                    source_high[i % 2], source_low[i % 2] = split(langmuir(swept, rate[...], aff[...]))
                if i > 0:
                    value = times(inv, i - 1, source_high, source_low, (i - 1) % 2)
                    fresh[i - 1] = value
                    own[i - 1] = value[nodes - face :]

        state.fresh, state.traces, state.own = run(
            body,
            "second_early",
            [state.inv, state.maps, state.free, state.stack, rate, aff, after],
            [VMEM((items, nodes, tracers), F32)] + [VMEM((items, face, tracers), F32)] * 2,
            [VMEM((2, nodes, tracers), BF16)] * 2,
            3 * size * dense,
        )

    def second_late(state):
        items = len(late) * count

        def body(inv, maps, free, stack, rate, aff, source_high, source_low, traces, own):
            for i in range(items + 1):
                if i < items:
                    swept = free[i] + dot(maps[i], stack[i])
                    traces[i] = lateral_rows(swept, per_side)
                    source_high[i], source_low[i] = split(langmuir(swept, rate[...], aff[...]))
                if i > 0:
                    own[i - 1] = times(inv, i - 1, source_high, source_low, i - 1, ending)

        state.source_high, state.source_low, state.traces, state.own = run(
            body,
            "second_late",
            [state.inv, state.maps, state.free, state.stack, rate, aff],
            source_outs(len(late)) + [VMEM((items, face, tracers), F32)] * 2,
            [],
            2 * len(late) * dense,
        )

    def second_sides(arrived):
        def body(order, arrived, *refs):
            got = [refs[5 * g : 5 * g + 5] for g in range(len(groups))]
            message, *refs = refs[5 * len(groups) :]
            for g, group in enumerate(groups):
                own, _, tails, rows_high, rows_low = got[g]
                stack, ends = refs[2 * g : 2 * g + 2]
                high, low = refs[2 * (len(groups) + g) : 2 * (len(groups) + g) + 2]
                for n, c in enumerate(group):
                    for p in range(count):
                        j = order[c, p]
                        i = n * count + j
                        if c == 0:
                            s = arrived_side(arrived, j)
                        else:
                            h, m = home[c - 1]
                            s = split(got[h][1][m * count + j])
                        stack[i, pl.ds(0, face)] = jnp.zeros((face, tracers), BF16)
                        for q, part in enumerate(stack_side(s)):
                            stack[i, pl.ds((q + 1) * face, face)] = part
                        ends[n * count + p] = own[i] + side_of(tails, i, s)
                    message[c] = offset(n, rows_high, rows_low, ends, high, low)

        ins = [order, arrived]
        outs, scratch = [VMEM((cols, face, tracers), F32)], []
        for group, state in zip(groups, states):
            ins += [state.own, state.traces, state.tails, state.high, state.low]
            outs.append(VMEM((len(group) * count, 4 * face, tracers), BF16))
            outs.append(VMEM((len(group) * count, face, tracers), F32))
            scratch += offset_scratch(len(group))
        message, *values = run(body, "second_sides", ins, outs, scratch, dense // 50)
        for g, state in enumerate(states):
            state.side_stack, state.ends = values[2 * g : 2 * g + 2]
        return message

    def settle(after):
        def body(_, inv, source_high, source_low, fresh, *refs):
            got = [refs[5 * g : 5 * g + 5] for g in range(len(groups))]
            outs = refs[5 * len(groups) :]
            for g, group in enumerate(groups):
                maps, stack, ends, rows_high, rows_low = got[g]
                base, within, high, low = outs[2 * g], outs[2 * g + 1], outs[-2], outs[-1]
                for i in range(len(group) * count):
                    own = fresh[i] if g == 0 else times(inv, i, source_high, source_low, i)
                    base[i] = own + dot(maps[i][:, 2 * face :], stack[i])
                for n in range(len(group)):
                    for p in range(count - 1):
                        e = split(ends[n * count + p])
                        high[pl.ds(p * face, face)] = e[0]
                        low[pl.ds(p * face, face)] = e[1]
                    span = pl.ds(0, wide)
                    rows = (rows_high[n, span][:, face:], rows_low[n, span][:, face:])
                    within[n] = dot_split(rows, (high[...], low[...]))

        ins = [after, states[1].inv, states[1].source_high, states[1].source_low, states[0].fresh]
        outs = []
        for group, state in zip(groups, states):
            ins += [state.maps, state.side_stack, state.ends, state.high, state.low]
            outs.append(VMEM((len(group) * count, nodes, tracers), F32))
            outs.append(VMEM((len(group), wide, tracers), F32))
        scratch = [VMEM((wide - face, tracers), BF16)] * 2
        values = run(body, "settle", ins, outs, scratch, 3 * cols * dense)
        for g, state in enumerate(states):
            state.base, state.within = values[2 * g : 2 * g + 2]

    def result(offsets):
        per = 5 + stages

        def body(order, inlet, *refs):
            offs, refs = refs[:stages], refs[stages:]
            got = [refs[per * g : per * g + per] for g in range(len(groups))]
            out, staged, sems, *stacks = refs[per * len(groups) :]
            for g, group in enumerate(groups):
                rows_high, rows_low, within, _, _, *mapped = got[g]
                for n, c in enumerate(group):
                    maps = [r[n, pl.ds(face, packed)] for r in mapped]
                    e = split(entering(inlet[c], [r[c] for r in offs], maps))
                    span = pl.ds(0, wide)
                    rows = (rows_high[n, span][:, :face], rows_low[n, span][:, :face])
                    inflow = within[n] + dot_split(rows, e)
                    for p in range(count):
                        i = n * count + order[c, p]
                        for q, part in enumerate(stack_inflow(split(inflow[p * face : (p + 1) * face]))):
                            stacks[g][i, pl.ds(q * face, face)] = part
            started = []
            for g, group in enumerate(groups):
                base, maps = got[g][3:5]
                for n, c in enumerate(group):
                    for j in range(count):
                        i, k = n * count + j, len(started)
                        staged[k] = (base[i] + dot(maps[i][:, : 3 * face], stacks[g][i])).astype(BF16)
                        copy = pltpu.make_async_copy(staged.at[k], out.at[c, 0, j], sems.at[k])
                        copy.start()
                        started.append(copy)
            for copy in started:
                copy.wait()

        ins = [order, inlet, *offsets]
        scratch = [VMEM((cols * count, nodes, tracers), BF16), pltpu.SemaphoreType.DMA((cols * count,))]
        for group, state in zip(groups, states):
            ins += [state.high, state.low, state.within, state.base, state.maps, *state.received]
            scratch.append(VMEM((len(group) * count, 3 * face, tracers), BF16))
        return run(body, "result", ins, [HBM(previous.shape, BF16)], scratch, cols * dense)[0]

    def exchange_first(state):
        state.sent, state.received = [state.message], []
        for stage in range(stages):
            if stage:
                state.sent.append(combine_first(stage - 1, state.sent[-1], state.received[-1]))
            state.received.append(swap(state.sent[-1], stage))

    (trace, order, rate, aff, inlet), one = begin()
    order = (order, SMEM)
    exchange_first(one)
    arrived = to_next(trace)
    fetched = finish_early(one, one.sent[-1])
    trace = enter_first(early, one)
    arrived_next = to_next(trace)
    two = begin_late(fetched, trace)
    states = [one, two]
    first_sides(two, arrived)
    exchange_first(two)
    second_early(one, two.sent[-1])
    enter_first(late, two)
    second_late(two)
    message, offsets = second_sides(arrived_next), []
    for stage in range(stages):
        offsets.append(swap(message, stage))
        if stage + 1 < stages:
            message = combine_second(
                stage, message, offsets[-1], [s.sent[stage] for s in states], [s.received[stage] for s in states]
            )
    settle(message)
    return result(offsets)


def solution(mesh):
    placed = (
        P("lat", "stream", None, None, None),
        P("lat", "stream", None, None, None),
        P("lat", "stream", None, None, None),
        P("lat", None, None),
        P("lat", "stream", None, None, None),
        P(),
        P(),
        P("lat", "stream", None),
    )
    return jax.shard_map(
        per_device,
        mesh=mesh,
        in_specs=placed,
        out_specs=P("lat", "stream", None, None, None),
        check_vma=False,
    )
```

```python
from types import SimpleNamespace

import jax
import jax.numpy as jnp
from jax import lax
from jax.experimental import pallas as pl
from jax.experimental.pallas import tpu as pltpu
from jax.sharding import PartitionSpec as P

NODES_1D = 8
F32 = jnp.float32
BF16 = jnp.bfloat16
MIB = 1 << 20
VMEM = pltpu.VMEM
HBM = pltpu.HBM
SMEM = pltpu.SMEM


def run(body, name, ins, outs, scratch, flops):
    pairs = [a if isinstance(a, tuple) else (a, VMEM) for a in ins]
    return pl.pallas_call(
        body,
        name=name,
        in_specs=[pl.BlockSpec(memory_space=space) for _, space in pairs],
        out_specs=[pl.BlockSpec(memory_space=o.memory_space) for o in outs],
        out_shape=outs,
        scratch_shapes=scratch,
        cost_estimate=pl.CostEstimate(flops=flops, bytes_accessed=MIB, transcendentals=0),
        compiler_params=pltpu.CompilerParams(vmem_limit_bytes=24 * MIB),
    )(*[a if space is VMEM else pltpu.with_memory_space_constraint(a, space) for a, space in pairs])


def split(x):
    high = x.astype(BF16)
    return high, (x - high.astype(F32)).astype(BF16)


def dot(x, y):
    return jnp.dot(x, y, preferred_element_type=F32)


def dot_split(x, y):
    return dot(x[0], y[0]) + (dot(x[0], y[1]) + dot(x[1], y[0]))


def langmuir(lagged, rate, affinity):
    return rate * lagged * pltpu.reciprocal(1.0 + affinity * jnp.abs(lagged), approx=True)


def lateral_rows(field, per_side):
    plane = per_side * per_side
    return jnp.concatenate(
        [field[a * plane + plane - per_side : (a + 1) * plane] for a in range(per_side)], axis=0
    )


def pack_map(mapping, lanes):
    face = mapping.shape[0]
    rows = face * face // lanes
    return jnp.concatenate([mapping[q * rows : (q + 1) * rows] for q in range(lanes // face)], axis=1)


def unpack_map(packed, face):
    return jnp.concatenate(
        [packed[:, q * face : (q + 1) * face] for q in range(packed.shape[1] // face)], axis=0
    )


def stack_maps(both):
    face = both.shape[1] // 2
    turned = pltpu.roll(both, face, 1)
    first = lax.broadcasted_iota(jnp.int32, both.shape, 1) < face
    low = split(both)[1]
    return jnp.concatenate(
        [jnp.where(first, both, turned).astype(BF16), low, jnp.where(first, turned, both).astype(BF16)], axis=1
    )


def stack_inflow(f):
    return (f[0], f[1], f[0])


def stack_side(s):
    return (s[0], s[0], s[1])


def bit(stage):
    return ((lax.axis_index("stream") >> stage) & 1) == 1


def per_device(inverse, upwind, lateral, inlet_trace, previous, uptake_rate, affinity, flow_order):
    cols, _, count, nodes, _ = inverse.shape
    face = upwind.shape[3]
    tracers = previous.shape[-1]
    per_side = NODES_1D
    plane = per_side * per_side
    wide = count * face
    packed = face * face // tracers
    streams, lats = lax.axis_size("stream"), lax.axis_size("lat")
    stages = streams.bit_length() - 1
    assert streams == 1 << stages
    assert cols > 1
    early, late = list(range(1, cols)), [0]
    groups = [early, late]
    home = {c: (g, n) for g, group in enumerate(groups) for n, c in enumerate(group)}
    ending = pl.ds(nodes - face, face)
    dense = 2 * count * nodes * nodes * tracers

    def to_next(value):
        return lax.ppermute(value, "lat", [(i, (i + 1) % lats) for i in range(lats)])

    def swap(value, stage):
        return lax.ppermute(value, "stream", [(i, i ^ (1 << stage)) for i in range(streams)])

    shaped = previous.reshape(cols, count, per_side, plane, tracers)

    def face_outs(size):
        return [
            VMEM((size * count, nodes, 6 * face), BF16),
            VMEM((size * count, nodes, tracers), F32),
            VMEM((size * count, face, 6 * face), BF16),
        ]

    def chain_outs(size):
        return [
            VMEM((size * count, face, 2 * face), F32),
            VMEM((size, wide + face, wide), BF16),
            VMEM((size, wide + face, wide), BF16),
        ]

    def side_outs(size):
        return [VMEM((size * count, 2, face, tracers), BF16), VMEM((size * count, face, tracers), F32)]

    def offset_scratch(size):
        return [VMEM((size, wide - face, tracers), BF16)] * 2

    def source_outs(size):
        return [VMEM((size * count, nodes, tracers), BF16)] * 2

    def field_outs(size):
        return [VMEM((size * count, nodes, nodes), BF16), VMEM((size * count, 2 * face, nodes), BF16)]

    def times(inv, i, high, low, k, rows=None):
        matrix = inv[i] if rows is None else inv[i, rows]
        return dot(matrix, high[k]) + dot(matrix, low[k])

    def face_maps(inv, faces, i, rows=None):
        matrix = inv[i] if rows is None else inv[i, rows]
        return lax.dot_general(matrix, faces[i], (((1,), (1,)), ((), ())), preferred_element_type=F32)

    def side_of(tails, i, s):
        return dot_split(split(tails[i][:, face:]), s)

    def link(n, p, step, rows_high, rows_low, row):
        row_id = lax.broadcasted_iota(jnp.int32, (face, wide), 0)
        lane_id = lax.broadcasted_iota(jnp.int32, (face, wide), 1)
        unit = jnp.where(lane_id == row_id + p * face, 1.0, 0.0)
        r = split(unit if p == 0 else row + unit)
        rows_high[n, pl.ds(p * face, face)] = r[0]
        rows_low[n, pl.ds(p * face, face)] = r[1]
        row = dot_split(step, r)
        if p == count - 1:
            r = split(row)
            rows_high[n, pl.ds(wide, face)] = r[0]
            rows_low[n, pl.ds(wide, face)] = r[1]
        return row

    def offset(n, rows_high, rows_low, ends, high, low):
        for p in range(count - 1):
            e = split(ends[n * count + p])
            high[n, pl.ds(p * face, face)] = e[0]
            low[n, pl.ds(p * face, face)] = e[1]
        last = pl.ds(wide, face)
        row = (rows_high[n, last][:, face:], rows_low[n, last][:, face:])
        return ends[n * count + count - 1] + dot_split(row, (high[n], low[n]))

    def begin():
        size = len(early)
        items = size * count

        def body(
            order, rate, aff, inlet, old, inverse, upwind, lateral, previous,
            trace, o_order, o_rate, o_aff, o_inlet, inv, faces, source_high, source_low,
            tails, rows_high, rows_low, sides, ends, message, lagged, staged, sems,
        ):
            counter = iter(range(sems.shape[0]))
            copy = lambda a, b: pltpu.make_async_copy(a, b, sems.at[next(counter)])
            lead = [copy(rate, o_rate), copy(aff, o_aff), copy(order, o_order)]
            parts = []
            for i in range(items):
                c, j = early[i // count], i % count
                parts.append([
                    copy(previous.at[c, 0, j], lagged.at[i]),
                    copy(inverse.at[c, 0, j, ending], inv.at[i, ending]),
                    copy(upwind.at[c, 0, j], faces.at[i, pl.ds(0, face)]),
                    copy(lateral.at[c, 0, j], faces.at[i, pl.ds(face, face)]),
                ])
            side = copy(old.at[0, :, :, pl.ds(plane - 2 * per_side, 2 * per_side)], staged)
            rest = [copy(inlet, o_inlet)]
            body_rows = pl.ds(0, nodes - face)
            for i in range(items):
                c, j = early[i // count], i % count
                rest.append(copy(inverse.at[c, 0, j, body_rows], inv.at[i, body_rows]))
            for one in lead + sum(parts, []) + [side]:
                one.start()
            for i in range(items):
                for one in (lead if i == 0 else []) + parts[i]:
                    one.wait()
                if i == min(1, items - 1):
                    for one in rest:
                        one.start()
                lag = lagged[i].astype(F32)
                if early[i // count] == cols - 1:
                    trace[i % count] = lateral_rows(lag, per_side)
                source_high[i], source_low[i] = split(langmuir(lag, o_rate[...], o_aff[...]))
                tails[i] = face_maps(inv, faces, i, ending)
                ends[i] = times(inv, i, source_high, source_low, i, ending)
            side.wait()
            rows, outflow, own = [None] * size, [None] * size, {}
            for n in range(size):
                for p in range(count):
                    own[n, p] = ends[n * count + o_order[early[n], p]]
            for p in range(count):
                for n, c in enumerate(early):
                    j = o_order[c, p]
                    i = n * count + j
                    step = split(tails[i][:, :face])
                    rows[n] = link(n, p, step, rows_high, rows_low, rows[n])
                    if c == 1:
                        s = [staged[j, a].astype(F32)[per_side:] for a in range(per_side)]
                        s = split(jnp.concatenate(s, axis=0))
                    else:
                        s = split(lateral_rows(lagged[i - count].astype(F32), per_side))
                    sides[n * count + p, 0] = s[0]
                    sides[n * count + p, 1] = s[1]
                    end = own[n, p] + side_of(tails, i, s)
                    ends[n * count + p] = end
                    outflow[n] = end if p == 0 else end + dot_split(step, split(outflow[n]))
            for n in range(size):
                message[n, pl.ds(0, face)] = outflow[n]
                message[n, pl.ds(face, packed)] = pack_map(rows[n][:, :face], tracers)
            for one in rest:
                one.wait()

        values = run(
            body,
            "begin",
            [
                (flow_order.reshape(cols, count), HBM),
                (uptake_rate.reshape(1, tracers), HBM),
                (affinity.reshape(1, tracers), HBM),
                (inlet_trace, HBM),
                (shaped, HBM),
                (inverse, HBM),
                (upwind, HBM),
                (lateral, HBM),
                (previous, HBM),
            ],
            [
                VMEM((count, face, tracers), F32),
                SMEM((cols, count), jnp.int32),
                VMEM((1, tracers), F32),
                VMEM((1, tracers), F32),
                VMEM((cols, face, tracers), F32),
                *field_outs(size),
                *source_outs(size),
                *chain_outs(size),
                *side_outs(size),
                VMEM((size, face + packed, tracers), F32),
            ],
            [
                VMEM((items, nodes, tracers), BF16),
                VMEM((count, per_side, 2 * per_side, tracers), BF16),
                pltpu.SemaphoreType.DMA((5 + 5 * items,)),
            ],
            size * dense,
        )
        state = SimpleNamespace()
        state.inv, state.faces, state.source_high, state.source_low = values[5:9]
        state.tails, state.high, state.low, state.sides, state.ends, state.message = values[9:]
        return values[:5], state

    def finish_early(state, after):
        size = len(early)
        items = size * count

        def body(
            inv, faces, source_high, source_low, _, inverse, upwind, lateral, previous,
            maps, free, side_maps, o_inv, o_faces, o_lagged, sems,
        ):
            copies = []
            for i in range(len(late) * count):
                c, j = late[i // count], i % count
                for k, (a, b) in enumerate((
                    (previous.at[c, 0, j], o_lagged.at[i]),
                    (upwind.at[c, 0, j], o_faces.at[i, pl.ds(0, face)]),
                    (lateral.at[c, 0, j], o_faces.at[i, pl.ds(face, face)]),
                    (inverse.at[c, 0, j], o_inv.at[i]),
                )):
                    copies.append(pltpu.make_async_copy(a, b, sems.at[k, i]))
                    copies[-1].start()
            for i in range(items):
                both = face_maps(inv, faces, i)
                maps[i] = stack_maps(both)
                side_maps[i] = stack_maps(lateral_rows(both, per_side))
                free[i] = times(inv, i, source_high, source_low, i)
            for one in copies:
                one.wait()

        state.maps, state.free, state.side_maps, *fetched = run(
            body,
            "finish_early",
            [state.inv, state.faces, state.source_high, state.source_low, after]
            + [(a, HBM) for a in (inverse, upwind, lateral, previous)],
            face_outs(size) + field_outs(len(late)) + [VMEM((len(late) * count, nodes, tracers), BF16)],
            [pltpu.SemaphoreType.DMA((4, len(late) * count))],
            3 * size * dense,
        )
        return fetched

    def begin_late(fetched, after):
        size = len(late)
        items = size * count

        def body(
            order, inv, faces, lagged, rate, aff, _,
            maps, free, side_maps, tails, rows_high, rows_low, mapped, source_high, source_low,
        ):
            for i in range(items):
                tails[i] = face_maps(inv, faces, i, ending)
            rows = [None] * size
            for i in range(items + 1):
                if i < items:
                    both = face_maps(inv, faces, i)
                    maps[i] = stack_maps(both)
                    side_maps[i] = stack_maps(lateral_rows(both, per_side))
                    s = split(langmuir(lagged[i].astype(F32), rate[...], aff[...]))
                    source_high[i % 2], source_low[i % 2] = s
                    n, p = i // count, i % count
                    step = split(tails[n * count + order[late[n], p]][:, :face])
                    rows[n] = link(n, p, step, rows_high, rows_low, rows[n])
                if i > 0:
                    free[i - 1] = times(inv, i - 1, source_high, source_low, (i - 1) % 2)
            for n in range(size):
                mapped[n] = pack_map(rows[n][:, :face], tracers)

        state = SimpleNamespace(inv=fetched[0])
        values = run(
            body,
            "begin_late",
            [order, *fetched, rate, aff, after],
            face_outs(size) + chain_outs(size) + [VMEM((size, packed, tracers), F32)],
            [VMEM((2, nodes, tracers), BF16)] * 2,
            3 * size * dense,
        )
        state.maps, state.free, state.side_maps, state.tails, state.high, state.low, state.mapped = values
        return state

    def arrived_side(arrived, j):
        return split(jnp.where(lax.axis_index("lat") > 0, arrived[j], 0.0))

    def first_sides(state, arrived):
        def body(order, arrived, free, tails, rows_high, rows_low, mapped, sides, ends, message, high, low):
            for p in range(count):
                j = order[0, p]
                s = arrived_side(arrived, j)
                sides[p, 0] = s[0]
                sides[p, 1] = s[1]
                ends[p] = free[j, ending] + side_of(tails, j, s)
            message[0, pl.ds(0, face)] = offset(0, rows_high, rows_low, ends, high, low)
            message[0, pl.ds(face, packed)] = mapped[0]

        state.sides, state.ends, state.message = run(
            body,
            "first_sides",
            [order, arrived, state.free, state.tails, state.high, state.low, state.mapped],
            side_outs(1) + [VMEM((1, face + packed, tracers), F32)],
            offset_scratch(1),
            dense // 50,
        )

    def combine_first(stage, own, other):
        def body(own, other, message):
            upper = bit(stage)
            for n in range(own.shape[0]):
                up = jnp.where(upper, own[n], other[n])
                low = jnp.where(upper, other[n], own[n])
                m = split(unpack_map(up[face:], face))
                message[n, pl.ds(0, face)] = dot_split(m, split(low[:face])) + up[:face]
                mapped = dot_split(m, split(unpack_map(low[face:], face)))
                message[n, pl.ds(face, packed)] = pack_map(mapped, tracers)

        return run(body, "combine", [own, other], [VMEM(own.shape, F32)], [], dense // 100)[0]

    def combine_second(stage, own, other, old_own, old_other):
        def body(own, other, *refs):
            message = refs[-1]
            upper = bit(stage)
            for c in range(cols):
                g, n = home[c]
                mine, theirs = refs[2 * g], refs[2 * g + 1]
                m = jnp.where(upper, mine[n, pl.ds(face, packed)], theirs[n, pl.ds(face, packed)])
                up = jnp.where(upper, own[c], other[c])
                low = jnp.where(upper, other[c], own[c])
                message[c] = dot_split(split(unpack_map(m, face)), split(low)) + up

        ins = [own, other]
        for pair in zip(old_own, old_other):
            ins += pair
        return run(body, "combine", ins, [VMEM(own.shape, F32)], [], dense // 100)[0]

    def entering(start, offsets, maps):
        for stage in reversed(range(stages)):
            m = split(unpack_map(maps[stage], face))
            beyond = dot_split(m, split(start)) + offsets[stage]
            start = jnp.where(bit(stage), beyond, start)
        return start

    def enter_first(group, state):
        size = len(group)
        last = group[-1] == cols - 1

        def body(order, inlet, rows_high, rows_low, sides, ends, free, side_maps, *refs):
            got, refs = refs[:stages], refs[stages:]
            stack, (high, low) = refs[0], refs[-2:]
            for n, c in enumerate(group):
                for p in range(count - 1):
                    e = split(ends[n * count + p])
                    high[n, pl.ds((p + 1) * face, face)] = e[0]
                    low[n, pl.ds((p + 1) * face, face)] = e[1]
                maps = [r[n, pl.ds(face, packed)] for r in got]
                e = split(entering(inlet[c], [r[n, pl.ds(0, face)] for r in got], maps))
                high[n, pl.ds(0, face)] = e[0]
                low[n, pl.ds(0, face)] = e[1]
                span = pl.ds(0, wide)
                inflow = dot_split((rows_high[n, span], rows_low[n, span]), (high[n], low[n]))
                for p in range(count):
                    i = n * count + order[c, p]
                    f = split(inflow[p * face : (p + 1) * face])
                    s = (sides[n * count + p, 0], sides[n * count + p, 1])
                    for q, part in enumerate(stack_inflow(f) + stack_side(s)):
                        stack[i, pl.ds(q * face, face)] = part
            if last:
                for j in range(count):
                    i = (size - 1) * count + j
                    refs[1][j] = lateral_rows(free.at[i], per_side) + dot(side_maps[i], stack[i])

        outs = [VMEM((size * count, 6 * face, tracers), BF16)]
        if last:
            outs.append(VMEM((count, face, tracers), F32))
        ins = [order, inlet, state.high, state.low, state.sides, state.ends, state.free, state.side_maps]
        scratch = [VMEM((size, wide, tracers), BF16)] * 2
        values = run(body, "enter", ins + state.received, outs, scratch, dense // 50)
        state.stack = values[0]
        return values[1] if last else None

    def second_early(state, after):
        size = len(early)
        items = size * count

        def body(inv, maps, free, stack, rate, aff, _, fresh, traces, own, source_high, source_low):
            for i in range(items + 1):
                if i < items:
                    swept = free[i] + dot(maps[i], stack[i])
                    traces[i] = lateral_rows(swept, per_side)
                    source_high[i % 2], source_low[i % 2] = split(langmuir(swept, rate[...], aff[...]))
                if i > 0:
                    value = times(inv, i - 1, source_high, source_low, (i - 1) % 2)
                    fresh[i - 1] = value
                    own[i - 1] = value[nodes - face :]

        state.fresh, state.traces, state.own = run(
            body,
            "second_early",
            [state.inv, state.maps, state.free, state.stack, rate, aff, after],
            [VMEM((items, nodes, tracers), F32)] + [VMEM((items, face, tracers), F32)] * 2,
            [VMEM((2, nodes, tracers), BF16)] * 2,
            0,
        )

    def second_late(state):
        items = len(late) * count

        def body(inv, maps, free, stack, rate, aff, source_high, source_low, traces, own):
            for i in range(items + 1):
                if i < items:
                    swept = free[i] + dot(maps[i], stack[i])
                    traces[i] = lateral_rows(swept, per_side)
                    source_high[i], source_low[i] = split(langmuir(swept, rate[...], aff[...]))
                if i > 0:
                    own[i - 1] = times(inv, i - 1, source_high, source_low, i - 1, ending)

        state.source_high, state.source_low, state.traces, state.own = run(
            body,
            "second_late",
            [state.inv, state.maps, state.free, state.stack, rate, aff],
            source_outs(len(late)) + [VMEM((items, face, tracers), F32)] * 2,
            [],
            0,
        )

    def second_sides(arrived):
        def body(order, arrived, *refs):
            got = [refs[5 * g : 5 * g + 5] for g in range(len(groups))]
            message, *refs = refs[5 * len(groups) :]
            for g, group in enumerate(groups):
                own, _, tails, rows_high, rows_low = got[g]
                stack, ends = refs[2 * g : 2 * g + 2]
                high, low = refs[2 * (len(groups) + g) : 2 * (len(groups) + g) + 2]
                for n, c in enumerate(group):
                    for p in range(count):
                        j = order[c, p]
                        i = n * count + j
                        if c == 0:
                            s = arrived_side(arrived, j)
                        else:
                            h, m = home[c - 1]
                            s = split(got[h][1][m * count + j])
                        stack[i, pl.ds(0, face)] = jnp.zeros((face, tracers), BF16)
                        for q, part in enumerate(stack_side(s)):
                            stack[i, pl.ds((q + 1) * face, face)] = part
                        ends[n * count + p] = own[i] + side_of(tails, i, s)
                    message[c] = offset(n, rows_high, rows_low, ends, high, low)

        ins = [order, arrived]
        outs, scratch = [VMEM((cols, face, tracers), F32)], []
        for group, state in zip(groups, states):
            ins += [state.own, state.traces, state.tails, state.high, state.low]
            outs.append(VMEM((len(group) * count, 4 * face, tracers), BF16))
            outs.append(VMEM((len(group) * count, face, tracers), F32))
            scratch += offset_scratch(len(group))
        message, *values = run(body, "second_sides", ins, outs, scratch, dense // 50)
        for g, state in enumerate(states):
            state.side_stack, state.ends = values[2 * g : 2 * g + 2]
        return message

    def settle(after):
        def body(_, inv, source_high, source_low, fresh, *refs):
            got = [refs[5 * g : 5 * g + 5] for g in range(len(groups))]
            outs = refs[5 * len(groups) :]
            for g, group in enumerate(groups):
                maps, stack, ends, rows_high, rows_low = got[g]
                base, within, high, low = outs[2 * g], outs[2 * g + 1], outs[-2], outs[-1]
                for i in range(len(group) * count):
                    own = fresh[i] if g == 0 else times(inv, i, source_high, source_low, i)
                    base[i] = own + dot(maps[i][:, 2 * face :], stack[i])
                for n in range(len(group)):
                    for p in range(count - 1):
                        e = split(ends[n * count + p])
                        high[pl.ds(p * face, face)] = e[0]
                        low[pl.ds(p * face, face)] = e[1]
                    span = pl.ds(0, wide)
                    rows = (rows_high[n, span][:, face:], rows_low[n, span][:, face:])
                    within[n] = dot_split(rows, (high[...], low[...]))

        ins = [after, states[1].inv, states[1].source_high, states[1].source_low, states[0].fresh]
        outs = []
        for group, state in zip(groups, states):
            ins += [state.maps, state.side_stack, state.ends, state.high, state.low]
            outs.append(VMEM((len(group) * count, nodes, tracers), F32))
            outs.append(VMEM((len(group), wide, tracers), F32))
        scratch = [VMEM((wide - face, tracers), BF16)] * 2
        values = run(body, "settle", ins, outs, scratch, 3 * cols * dense)
        for g, state in enumerate(states):
            state.base, state.within = values[2 * g : 2 * g + 2]

    def result(offsets):
        per = 5 + stages

        def body(order, inlet, *refs):
            offs, refs = refs[:stages], refs[stages:]
            got = [refs[per * g : per * g + per] for g in range(len(groups))]
            out, staged, sems, *stacks = refs[per * len(groups) :]
            for g, group in enumerate(groups):
                rows_high, rows_low, within, _, _, *mapped = got[g]
                for n, c in enumerate(group):
                    maps = [r[n, pl.ds(face, packed)] for r in mapped]
                    e = split(entering(inlet[c], [r[c] for r in offs], maps))
                    span = pl.ds(0, wide)
                    rows = (rows_high[n, span][:, :face], rows_low[n, span][:, :face])
                    inflow = within[n] + dot_split(rows, e)
                    for p in range(count):
                        i = n * count + order[c, p]
                        for q, part in enumerate(stack_inflow(split(inflow[p * face : (p + 1) * face]))):
                            stacks[g][i, pl.ds(q * face, face)] = part
            started = []
            for g, group in enumerate(groups):
                base, maps = got[g][3:5]
                for n, c in enumerate(group):
                    for j in range(count):
                        i, k = n * count + j, len(started)
                        staged[k] = (base[i] + dot(maps[i][:, : 3 * face], stacks[g][i])).astype(BF16)
                        copy = pltpu.make_async_copy(staged.at[k], out.at[c, 0, j], sems.at[k])
                        copy.start()
                        started.append(copy)
            for copy in started:
                copy.wait()

        ins = [order, inlet, *offsets]
        scratch = [VMEM((cols * count, nodes, tracers), BF16), pltpu.SemaphoreType.DMA((cols * count,))]
        for group, state in zip(groups, states):
            ins += [state.high, state.low, state.within, state.base, state.maps, *state.received]
            scratch.append(VMEM((len(group) * count, 3 * face, tracers), BF16))
        return run(body, "result", ins, [HBM(previous.shape, BF16)], scratch, cols * dense)[0]

    def exchange_first(state):
        state.sent, state.received = [state.message], []
        for stage in range(stages):
            if stage:
                state.sent.append(combine_first(stage - 1, state.sent[-1], state.received[-1]))
            state.received.append(swap(state.sent[-1], stage))

    (trace, order, rate, aff, inlet), one = begin()
    order = (order, SMEM)
    exchange_first(one)
    arrived = to_next(trace)
    fetched = finish_early(one, one.sent[-1])
    trace = enter_first(early, one)
    arrived_next = to_next(trace)
    two = begin_late(fetched, trace)
    states = [one, two]
    first_sides(two, arrived)
    exchange_first(two)
    second_early(one, two.sent[-1])
    enter_first(late, two)
    second_late(two)
    message, offsets = second_sides(arrived_next), []
    for stage in range(stages):
        offsets.append(swap(message, stage))
        if stage + 1 < stages:
            message = combine_second(
                stage, message, offsets[-1], [s.sent[stage] for s in states], [s.received[stage] for s in states]
            )
    settle(message)
    return result(offsets)


def solution(mesh):
    placed = (
        P("lat", "stream", None, None, None),
        P("lat", "stream", None, None, None),
        P("lat", "stream", None, None, None),
        P("lat", None, None),
        P("lat", "stream", None, None, None),
        P(),
        P(),
        P("lat", "stream", None),
    )
    return jax.shard_map(
        per_device,
        mesh=mesh,
        in_specs=placed,
        out_specs=P("lat", "stream", None, None, None),
        check_vma=False,
    )
```

```python
from types import SimpleNamespace

import jax
import jax.numpy as jnp
from jax import lax
from jax.experimental import pallas as pl
from jax.experimental.pallas import tpu as pltpu
from jax.sharding import PartitionSpec as P

NODES_1D = 8
F32 = jnp.float32
BF16 = jnp.bfloat16
MIB = 1 << 20
VMEM = pltpu.VMEM
HBM = pltpu.HBM
SMEM = pltpu.SMEM


def run(body, name, ins, outs, scratch, flops):
    pairs = [a if isinstance(a, tuple) else (a, VMEM) for a in ins]
    return pl.pallas_call(
        body,
        name=name,
        in_specs=[pl.BlockSpec(memory_space=space) for _, space in pairs],
        out_specs=[pl.BlockSpec(memory_space=o.memory_space) for o in outs],
        out_shape=outs,
        scratch_shapes=scratch,
        cost_estimate=pl.CostEstimate(flops=flops, bytes_accessed=MIB, transcendentals=0),
        compiler_params=pltpu.CompilerParams(vmem_limit_bytes=24 * MIB),
    )(*[a if space is VMEM else pltpu.with_memory_space_constraint(a, space) for a, space in pairs])


def split(x):
    high = x.astype(BF16)
    return high, (x - high.astype(F32)).astype(BF16)


def dot(x, y):
    return jnp.dot(x, y, preferred_element_type=F32)


def dot_split(x, y):
    return dot(x[0], y[0]) + (dot(x[0], y[1]) + dot(x[1], y[0]))


def langmuir(lagged, rate, affinity):
    return rate * lagged * pltpu.reciprocal(1.0 + affinity * jnp.abs(lagged), approx=True)


def lateral_rows(field, per_side):
    plane = per_side * per_side
    return jnp.concatenate(
        [field[a * plane + plane - per_side : (a + 1) * plane] for a in range(per_side)], axis=0
    )


def pack_map(mapping, lanes):
    face = mapping.shape[0]
    rows = face * face // lanes
    return jnp.concatenate([mapping[q * rows : (q + 1) * rows] for q in range(lanes // face)], axis=1)


def unpack_map(packed, face):
    return jnp.concatenate(
        [packed[:, q * face : (q + 1) * face] for q in range(packed.shape[1] // face)], axis=0
    )


def stack_maps(both):
    face = both.shape[1] // 2
    turned = pltpu.roll(both, face, 1)
    first = lax.broadcasted_iota(jnp.int32, both.shape, 1) < face
    low = split(both)[1]
    return jnp.concatenate(
        [jnp.where(first, both, turned).astype(BF16), low, jnp.where(first, turned, both).astype(BF16)], axis=1
    )


def stack_inflow(f):
    return (f[0], f[1], f[0])


def stack_side(s):
    return (s[0], s[0], s[1])


def in_pairs(items, per, step):
    def turn(t, _):
        step([t * per + k for k in range(per)])
        return 0

    lax.fori_loop(0, items // per, turn, 0)


def bit(stage):
    return ((lax.axis_index("stream") >> stage) & 1) == 1


def per_device(inverse, upwind, lateral, inlet_trace, previous, uptake_rate, affinity, flow_order):
    cols, _, count, nodes, _ = inverse.shape
    face = upwind.shape[3]
    tracers = previous.shape[-1]
    per_side = NODES_1D
    plane = per_side * per_side
    wide = count * face
    packed = face * face // tracers
    streams, lats = lax.axis_size("stream"), lax.axis_size("lat")
    stages = streams.bit_length() - 1
    assert streams == 1 << stages
    assert cols > 1
    early, late = list(range(1, cols)), [0]
    groups = [early, late]
    home = {c: (g, n) for g, group in enumerate(groups) for n, c in enumerate(group)}
    ending = pl.ds(nodes - face, face)
    per = 2 if count % 2 == 0 else 1
    dense = 2 * count * nodes * nodes * tracers

    def to_next(value):
        return lax.ppermute(value, "lat", [(i, (i + 1) % lats) for i in range(lats)])

    def swap(value, stage):
        return lax.ppermute(value, "stream", [(i, i ^ (1 << stage)) for i in range(streams)])

    shaped = previous.reshape(cols, count, per_side, plane, tracers)

    def face_outs(size):
        return [
            VMEM((size * count, nodes, 6 * face), BF16),
            VMEM((size * count, nodes, tracers), F32),
            VMEM((size * count, face, 6 * face), BF16),
        ]

    def chain_outs(size):
        return [
            VMEM((size * count, face, 2 * face), F32),
            VMEM((size, wide + face, wide), BF16),
            VMEM((size, wide + face, wide), BF16),
        ]

    def side_outs(size):
        return [VMEM((size * count, 2, face, tracers), BF16), VMEM((size * count, face, tracers), F32)]

    def offset_scratch(size):
        return [VMEM((size, wide - face, tracers), BF16)] * 2

    def source_outs(size):
        return [VMEM((size * count, nodes, tracers), BF16)] * 2

    def field_outs(size):
        return [VMEM((size * count, nodes, nodes), BF16), VMEM((size * count, 2 * face, nodes), BF16)]

    def times(inv, i, high, low, k, rows=None):
        matrix = inv[i] if rows is None else inv[i, rows]
        return dot(matrix, high[k]) + dot(matrix, low[k])

    def face_maps(inv, faces, i, rows=None):
        matrix = inv[i] if rows is None else inv[i, rows]
        return lax.dot_general(matrix, faces[i], (((1,), (1,)), ((), ())), preferred_element_type=F32)

    def side_of(tails, i, s):
        return dot_split(split(tails[i][:, face:]), s)

    def link(n, p, step, rows_high, rows_low, row):
        row_id = lax.broadcasted_iota(jnp.int32, (face, wide), 0)
        lane_id = lax.broadcasted_iota(jnp.int32, (face, wide), 1)
        unit = jnp.where(lane_id == row_id + p * face, 1.0, 0.0)
        r = split(jnp.where(p == 0, 0.0, row[n]) + unit)
        here = pl.ds(pl.multiple_of(p * face, face), face)
        rows_high[n, here] = r[0]
        rows_low[n, here] = r[1]
        r = split(dot_split(step, r))
        rows_high[n, pl.ds(wide, face)] = r[0]
        rows_low[n, pl.ds(wide, face)] = r[1]
        row[n] = r[0].astype(F32) + r[1].astype(F32)

    def offset(n, rows_high, rows_low, ends, high, low):
        for p in range(count - 1):
            e = split(ends[n * count + p])
            high[n, pl.ds(p * face, face)] = e[0]
            low[n, pl.ds(p * face, face)] = e[1]
        last = pl.ds(wide, face)
        row = (rows_high[n, last][:, face:], rows_low[n, last][:, face:])
        return ends[n * count + count - 1] + dot_split(row, (high[n], low[n]))

    def begin():
        size = len(early)
        items = size * count

        def body(
            order, rate, aff, inlet, old, inverse, upwind, lateral, previous,
            trace, o_order, o_rate, o_aff, o_inlet, inv, faces, source_high, source_low,
            tails, sides, ends, message, lagged, staged, own, lead_sems, sems,
        ):
            lead = [
                pltpu.make_async_copy(a, b, lead_sems.at[k])
                for k, (a, b) in enumerate(((rate, o_rate), (aff, o_aff), (order, o_order), (inlet, o_inlet)))
            ]
            rows = pl.ds(plane - 2 * per_side, 2 * per_side)
            lead.append(pltpu.make_async_copy(old.at[0, :, :, rows], staged, lead_sems.at[len(lead)]))

            def parts(i):
                c, j = early[0] + i // count, i % count
                here, there = pl.ds(j, per), pl.ds(i, per)
                pairs = (
                    (previous.at[c, 0, here], lagged.at[there]),
                    (inverse.at[c, 0, here, ending], inv.at[there, ending]),
                    (upwind.at[c, 0, here], faces.at[there, pl.ds(0, face)]),
                    (lateral.at[c, 0, here], faces.at[there, pl.ds(face, face)]),
                )
                return [pltpu.make_async_copy(a, b, sems.at[k, i]) for k, (a, b) in enumerate(pairs)]

            def rest(i):
                c, j = early[0] + i // count, i % count
                others = pl.ds(0, nodes - face)
                return pltpu.make_async_copy(
                    inverse.at[c, 0, pl.ds(j, per), others], inv.at[pl.ds(i, per), others], sems.at[4, i]
                )

            def old_rows(field):
                return jnp.concatenate([field(a).astype(F32)[per_side:] for a in range(per_side)], axis=0)

            def lagged_rows(i):
                starts = [a * plane + plane - 2 * per_side for a in range(per_side)]
                return old_rows(lambda a: lagged[i, pl.ds(starts[a], 2 * per_side)])

            for one in lead[:3]:
                one.start()
            for i in range(0, items, per):
                for one in parts(i):
                    one.start()
            for one in lead[3:]:
                one.start()
            for one in lead[:3]:
                one.wait()

            def step(members):
                for one in parts(members[0]):
                    one.wait()
                rest(members[0]).start()
                for i in members:
                    lag = lagged[i].astype(F32)
                    source_high[i], source_low[i] = split(langmuir(lag, o_rate[...], o_aff[...]))
                for i in members:
                    tails[i] = face_maps(inv, faces, i, ending)
                    own[i] = times(inv, i, source_high, source_low, i, ending)

            in_pairs(items, per, step)
            for one in lead[3:]:
                one.wait()
            for j in range(count):
                trace[j] = lagged_rows(items - count + j)
            for n, c in enumerate(early):
                links = []
                for p in range(count):
                    j = o_order[c, p]
                    i = n * count + j
                    s = split(old_rows(lambda a: staged[j, a]) if c == 1 else lagged_rows(i - count))
                    sides[n * count + p, 0] = s[0]
                    sides[n * count + p, 1] = s[1]
                    end = own[i] + side_of(tails, i, s)
                    ends[n * count + p] = end
                    links.append((tails[i][:, :face], end))
                while len(links) > 1:
                    paired = []
                    for (low, start), (up, end) in zip(links[::2], links[1::2]):
                        u = split(up)
                        paired.append((dot_split(u, split(low)), end + dot_split(u, split(start))))
                    links = paired + links[2 * len(paired) :]
                message[n, pl.ds(0, face)] = links[0][1]
                message[n, pl.ds(face, packed)] = pack_map(links[0][0], tracers)
            for i in range(0, items, per):
                rest(i).wait()

        values = run(
            body,
            "begin",
            [
                (flow_order.reshape(cols, count), HBM),
                (uptake_rate.reshape(1, tracers), HBM),
                (affinity.reshape(1, tracers), HBM),
                (inlet_trace, HBM),
                (shaped, HBM),
                (inverse, HBM),
                (upwind, HBM),
                (lateral, HBM),
                (previous, HBM),
            ],
            [
                VMEM((count, face, tracers), F32),
                SMEM((cols, count), jnp.int32),
                VMEM((1, tracers), F32),
                VMEM((1, tracers), F32),
                VMEM((cols, face, tracers), F32),
                *field_outs(size),
                *source_outs(size),
                VMEM((items, face, 2 * face), F32),
                *side_outs(size),
                VMEM((size, face + packed, tracers), F32),
            ],
            [
                VMEM((items, nodes, tracers), BF16),
                VMEM((count, per_side, 2 * per_side, tracers), BF16),
                VMEM((items, face, tracers), F32),
                pltpu.SemaphoreType.DMA((5,)),
                pltpu.SemaphoreType.DMA((5, items)),
            ],
            size * dense,
        )
        state = SimpleNamespace()
        state.inv, state.faces, state.source_high, state.source_low = values[5:9]
        state.tails, state.sides, state.ends, state.message = values[9:]
        return values[:5], state

    def finish_early(state, after):
        size = len(early)
        items = size * count

        def body(
            order, inv, faces, source_high, source_low, tails, _, inverse, upwind, lateral, previous,
            maps, free, side_maps, rows_high, rows_low, o_inv, o_faces, o_lagged, row, sems,
        ):
            copies = []
            for n, c in enumerate(late):
                there = pl.ds(n * count, count)
                for k, (a, b) in enumerate((
                    (previous.at[c, 0], o_lagged.at[there]),
                    (upwind.at[c, 0], o_faces.at[there, pl.ds(0, face)]),
                    (lateral.at[c, 0], o_faces.at[there, pl.ds(face, face)]),
                    (inverse.at[c, 0], o_inv.at[there]),
                )):
                    copies.append(pltpu.make_async_copy(a, b, sems.at[k, n]))
                    copies[-1].start()

            def step(members):
                for i in members:
                    both = face_maps(inv, faces, i)
                    maps[i] = stack_maps(both)
                    side_maps[i] = stack_maps(lateral_rows(both, per_side))
                    free[i] = times(inv, i, source_high, source_low, i)
                    n, p = i // count, i % count
                    head = tails[n * count + order[early[0] + n, p]][:, :face]
                    link(n, p, split(head), rows_high, rows_low, row)

            in_pairs(items, per, step)
            for one in copies:
                one.wait()

        state.maps, state.free, state.side_maps, state.high, state.low, *fetched = run(
            body,
            "finish_early",
            [order, state.inv, state.faces, state.source_high, state.source_low, state.tails, after]
            + [(a, HBM) for a in (inverse, upwind, lateral, previous)],
            face_outs(size)
            + chain_outs(size)[1:]
            + field_outs(len(late))
            + [VMEM((len(late) * count, nodes, tracers), BF16)],
            [VMEM((size, face, wide), F32), pltpu.SemaphoreType.DMA((4, len(late)))],
            3 * size * dense,
        )
        return fetched

    def begin_late(fetched):
        size = len(late)
        items = size * count

        def body(
            order, inv, faces, lagged, rate, aff,
            source_high, source_low, own, tails, rows_high, rows_low, mapped, row,
        ):
            for i in range(items):
                tails[i] = face_maps(inv, faces, i, ending)
            for i in range(items + 1):
                if i < items:
                    lag = lagged[i].astype(F32)
                    source_high[i], source_low[i] = split(langmuir(lag, rate[...], aff[...]))
                    n, p = i // count, i % count
                    step = split(tails[n * count + order[late[n], p]][:, :face])
                    link(n, p, step, rows_high, rows_low, row)
                if i > 0:
                    own[i - 1] = times(inv, i - 1, source_high, source_low, i - 1, ending)
            for n in range(size):
                mapped[n] = pack_map(row[n][:, :face], tracers)

        state = SimpleNamespace(inv=fetched[0], faces=fetched[1])
        values = run(
            body,
            "begin_late",
            [order, *fetched, rate, aff],
            source_outs(size)
            + [VMEM((items, face, tracers), F32)]
            + chain_outs(size)
            + [VMEM((size, packed, tracers), F32)],
            [VMEM((size, face, wide), F32)],
            2 * size * dense,
        )
        state.source_high, state.source_low, state.own, state.tails, state.high, state.low, state.mapped = values
        return state

    def late_maps(state, after):
        items = len(late) * count

        def body(inv, faces, _, maps):
            for i in range(items):
                maps[i] = stack_maps(face_maps(inv, faces, i))

        (state.maps,) = run(
            body,
            "late_maps",
            [state.inv, state.faces, after],
            face_outs(len(late))[:1],
            [],
            len(late) * dense,
        )

    def late_free(state, after):
        items = len(late) * count

        def body(inv, source_high, source_low, _, free):
            for i in range(items):
                free[i] = times(inv, i, source_high, source_low, i)

        (state.free,) = run(
            body,
            "late_free",
            [state.inv, state.source_high, state.source_low, after],
            [VMEM((items, nodes, tracers), F32)],
            [],
            2 * len(late) * dense,
        )

    def arrived_side(arrived, j):
        return split(jnp.where(lax.axis_index("lat") > 0, arrived[j], 0.0))

    def first_sides(state, arrived):
        def body(order, arrived, own, tails, rows_high, rows_low, mapped, sides, ends, message, high, low):
            for p in range(count):
                j = order[0, p]
                s = arrived_side(arrived, j)
                sides[p, 0] = s[0]
                sides[p, 1] = s[1]
                ends[p] = own[j] + side_of(tails, j, s)
            message[0, pl.ds(0, face)] = offset(0, rows_high, rows_low, ends, high, low)
            message[0, pl.ds(face, packed)] = mapped[0]

        state.sides, state.ends, state.message = run(
            body,
            "first_sides",
            [order, arrived, state.own, state.tails, state.high, state.low, state.mapped],
            side_outs(1) + [VMEM((1, face + packed, tracers), F32)],
            offset_scratch(1),
            dense // 50,
        )

    def combine_first(stage, own, other):
        def body(own, other, message):
            upper = bit(stage)
            for n in range(own.shape[0]):
                up = jnp.where(upper, own[n], other[n])
                low = jnp.where(upper, other[n], own[n])
                m = split(unpack_map(up[face:], face))
                message[n, pl.ds(0, face)] = dot_split(m, split(low[:face])) + up[:face]
                mapped = dot_split(m, split(unpack_map(low[face:], face)))
                message[n, pl.ds(face, packed)] = pack_map(mapped, tracers)

        return run(body, "combine", [own, other], [VMEM(own.shape, F32)], [], dense // 100)[0]

    def combine_second(stage, own, other, old_own, old_other):
        def body(own, other, *refs):
            message = refs[-1]
            upper = bit(stage)
            for c in range(cols):
                g, n = home[c]
                mine, theirs = refs[2 * g], refs[2 * g + 1]
                m = jnp.where(upper, mine[n, pl.ds(face, packed)], theirs[n, pl.ds(face, packed)])
                up = jnp.where(upper, own[c], other[c])
                low = jnp.where(upper, other[c], own[c])
                message[c] = dot_split(split(unpack_map(m, face)), split(low)) + up

        ins = [own, other]
        for pair in zip(old_own, old_other):
            ins += pair
        return run(body, "combine", ins, [VMEM(own.shape, F32)], [], dense // 100)[0]

    def entering(start, offsets, maps):
        for stage in reversed(range(stages)):
            m = split(unpack_map(maps[stage], face))
            beyond = dot_split(m, split(start)) + offsets[stage]
            start = jnp.where(bit(stage), beyond, start)
        return start

    def enter_first(group, state, after):
        size = len(group)
        last = group[-1] == cols - 1

        def body(order, inlet, rows_high, rows_low, sides, ends, *refs):
            got, refs = refs[:stages], refs[stages:]
            if last:
                (free, side_maps), refs = refs[:2], refs[3:]
            stack, (high, low) = refs[0], refs[-2:]
            for n, c in enumerate(group):
                for p in range(count - 1):
                    e = split(ends[n * count + p])
                    high[n, pl.ds((p + 1) * face, face)] = e[0]
                    low[n, pl.ds((p + 1) * face, face)] = e[1]
                maps = [r[n, pl.ds(face, packed)] for r in got]
                e = split(entering(inlet[c], [r[n, pl.ds(0, face)] for r in got], maps))
                high[n, pl.ds(0, face)] = e[0]
                low[n, pl.ds(0, face)] = e[1]
                span = pl.ds(0, wide)
                inflow = dot_split((rows_high[n, span], rows_low[n, span]), (high[n], low[n]))
                for p in range(count):
                    i = n * count + order[c, p]
                    f = split(inflow[p * face : (p + 1) * face])
                    s = (sides[n * count + p, 0], sides[n * count + p, 1])
                    for q, part in enumerate(stack_inflow(f) + stack_side(s)):
                        stack[i, pl.ds(q * face, face)] = part
            if last:
                for j in range(count):
                    i = (size - 1) * count + j
                    refs[1][j] = lateral_rows(free.at[i], per_side) + dot(side_maps[i], stack[i])

        outs = [VMEM((size * count, 6 * face, tracers), BF16)]
        if last:
            outs.append(VMEM((count, face, tracers), F32))
        ins = [order, inlet, state.high, state.low, state.sides, state.ends, *state.received]
        if last:
            ins += [state.free, state.side_maps, after]
        scratch = [VMEM((size, wide, tracers), BF16)] * 2
        values = run(body, "enter", ins, outs, scratch, dense // 50)
        state.stack = values[0]
        return values[1] if last else None

    def second(group, state, after):
        items = len(group) * count

        def body(inv, maps, free, stack, rate, aff, _, source_high, source_low, traces, own):
            for i in range(items + 1):
                if i < items:
                    swept = free[i] + dot(maps[i], stack[i])
                    traces[i] = lateral_rows(swept, per_side)
                    source_high[i], source_low[i] = split(langmuir(swept, rate[...], aff[...]))
                if i > 0:
                    own[i - 1] = times(inv, i - 1, source_high, source_low, i - 1, ending)

        state.source_high, state.source_low, state.traces, state.own = run(
            body,
            "second",
            [state.inv, state.maps, state.free, state.stack, rate, aff, after],
            source_outs(len(group)) + [VMEM((items, face, tracers), F32)] * 2,
            [],
            0,
        )

    def second_sides(arrived):
        def body(order, arrived, *refs):
            got = [refs[5 * g : 5 * g + 5] for g in range(len(groups))]
            message, *refs = refs[5 * len(groups) :]
            for g, group in enumerate(groups):
                own, _, tails, rows_high, rows_low = got[g]
                stack, ends = refs[2 * g : 2 * g + 2]
                high, low = refs[2 * (len(groups) + g) : 2 * (len(groups) + g) + 2]
                for n, c in enumerate(group):
                    for p in range(count):
                        j = order[c, p]
                        i = n * count + j
                        if c == 0:
                            s = arrived_side(arrived, j)
                        else:
                            h, m = home[c - 1]
                            s = split(got[h][1][m * count + j])
                        stack[i, pl.ds(0, face)] = jnp.zeros((face, tracers), BF16)
                        for q, part in enumerate(stack_side(s)):
                            stack[i, pl.ds((q + 1) * face, face)] = part
                        ends[n * count + p] = own[i] + side_of(tails, i, s)
                    message[c] = offset(n, rows_high, rows_low, ends, high, low)

        ins = [order, arrived]
        outs, scratch = [VMEM((cols, face, tracers), F32)], []
        for group, state in zip(groups, states):
            ins += [state.own, state.traces, state.tails, state.high, state.low]
            outs.append(VMEM((len(group) * count, 4 * face, tracers), BF16))
            outs.append(VMEM((len(group) * count, face, tracers), F32))
            scratch += offset_scratch(len(group))
        message, *values = run(body, "second_sides", ins, outs, scratch, dense // 50)
        for g, state in enumerate(states):
            state.side_stack, state.ends = values[2 * g : 2 * g + 2]
        return message

    def settle(after):
        def body(_, *refs):
            got = [refs[8 * g : 8 * g + 8] for g in range(len(groups))]
            outs = refs[8 * len(groups) :]
            for g, group in enumerate(groups):
                inv, source_high, source_low, maps, stack, ends, rows_high, rows_low = got[g]
                base, within, high, low = outs[2 * g], outs[2 * g + 1], outs[-2], outs[-1]
                for i in range(len(group) * count):
                    own = times(inv, i, source_high, source_low, i)
                    base[i] = own + dot(maps[i][:, 2 * face :], stack[i])
                for n in range(len(group)):
                    for p in range(count - 1):
                        e = split(ends[n * count + p])
                        high[pl.ds(p * face, face)] = e[0]
                        low[pl.ds(p * face, face)] = e[1]
                    span = pl.ds(0, wide)
                    rows = (rows_high[n, span][:, face:], rows_low[n, span][:, face:])
                    within[n] = dot_split(rows, (high[...], low[...]))

        ins = [after]
        outs = []
        for group, state in zip(groups, states):
            ins += [state.inv, state.source_high, state.source_low]
            ins += [state.maps, state.side_stack, state.ends, state.high, state.low]
            outs.append(VMEM((len(group) * count, nodes, tracers), F32))
            outs.append(VMEM((len(group), wide, tracers), F32))
        scratch = [VMEM((wide - face, tracers), BF16)] * 2
        values = run(body, "settle", ins, outs, scratch, 3 * cols * dense)
        for g, state in enumerate(states):
            state.base, state.within = values[2 * g : 2 * g + 2]

    def result(offsets):
        parts = 5 + stages

        def body(order, inlet, *refs):
            offs, refs = refs[:stages], refs[stages:]
            got = [refs[parts * g : parts * g + parts] for g in range(len(groups))]
            out, staged, sems, *stacks = refs[parts * len(groups) :]
            for g, group in enumerate(groups):
                rows_high, rows_low, within, _, _, *mapped = got[g]
                for n, c in enumerate(group):
                    maps = [r[n, pl.ds(face, packed)] for r in mapped]
                    e = split(entering(inlet[c], [r[c] for r in offs], maps))
                    span = pl.ds(0, wide)
                    rows = (rows_high[n, span][:, :face], rows_low[n, span][:, :face])
                    inflow = within[n] + dot_split(rows, e)
                    for p in range(count):
                        i = n * count + order[c, p]
                        for q, part in enumerate(stack_inflow(split(inflow[p * face : (p + 1) * face]))):
                            stacks[g][i, pl.ds(q * face, face)] = part
            started = []
            for g, group in enumerate(groups):
                base, maps = got[g][3:5]
                for n, c in enumerate(group):
                    for j in range(count):
                        i, k = n * count + j, len(started)
                        staged[k] = (base[i] + dot(maps[i][:, : 3 * face], stacks[g][i])).astype(BF16)
                        copy = pltpu.make_async_copy(staged.at[k], out.at[c, 0, j], sems.at[k])
                        copy.start()
                        started.append(copy)
            for copy in started:
                copy.wait()

        ins = [order, inlet, *offsets]
        scratch = [VMEM((cols * count, nodes, tracers), BF16), pltpu.SemaphoreType.DMA((cols * count,))]
        for group, state in zip(groups, states):
            ins += [state.high, state.low, state.within, state.base, state.maps, *state.received]
            scratch.append(VMEM((len(group) * count, 3 * face, tracers), BF16))
        return run(body, "result", ins, [HBM(previous.shape, BF16)], scratch, cols * dense)[0]

    def exchange_first(state):
        state.sent, state.received = [state.message], []
        for stage in range(stages):
            if stage:
                state.sent.append(combine_first(stage - 1, state.sent[-1], state.received[-1]))
            state.received.append(swap(state.sent[-1], stage))

    (trace, order, rate, aff, inlet), one = begin()
    order = (order, SMEM)
    exchange_first(one)
    arrived = to_next(trace)
    fetched = finish_early(one, one.sent[-1])
    two = begin_late(fetched)
    states = [one, two]
    trace = enter_first(early, one, two.mapped)
    arrived_next = to_next(trace)
    first_sides(two, arrived)
    exchange_first(two)
    late_maps(two, two.sent[0])
    second(early, one, two.sent[-1])
    late_free(two, two.sent[-1])
    enter_first(late, two, None)
    second(late, two, two.sent[-1])
    message, offsets = second_sides(arrived_next), []
    for stage in range(stages):
        offsets.append(swap(message, stage))
        if stage + 1 < stages:
            message = combine_second(
                stage, message, offsets[-1], [s.sent[stage] for s in states], [s.received[stage] for s in states]
            )
    settle(message)
    return result(offsets)


def solution(mesh):
    placed = (
        P("lat", "stream", None, None, None),
        P("lat", "stream", None, None, None),
        P("lat", "stream", None, None, None),
        P("lat", None, None),
        P("lat", "stream", None, None, None),
        P(),
        P(),
        P("lat", "stream", None),
    )
    return jax.shard_map(
        per_device,
        mesh=mesh,
        in_specs=placed,
        out_specs=P("lat", "stream", None, None, None),
        check_vma=False,
    )
```

```python
from types import SimpleNamespace

import jax
import jax.numpy as jnp
from jax import lax
from jax.experimental import pallas as pl
from jax.experimental.pallas import tpu as pltpu
from jax.sharding import PartitionSpec as P

NODES_1D = 8
F32 = jnp.float32
BF16 = jnp.bfloat16
MIB = 1 << 20
VMEM = pltpu.VMEM
HBM = pltpu.HBM
SMEM = pltpu.SMEM


def run(body, name, ins, outs, scratch):
    pairs = [a if isinstance(a, tuple) else (a, VMEM) for a in ins]
    return pl.pallas_call(
        body,
        name=name,
        in_specs=[pl.BlockSpec(memory_space=space) for _, space in pairs],
        out_specs=[pl.BlockSpec(memory_space=o.memory_space) for o in outs],
        out_shape=outs,
        scratch_shapes=scratch,
        cost_estimate=pl.CostEstimate(flops=0, bytes_accessed=0, transcendentals=0),
        compiler_params=pltpu.CompilerParams(vmem_limit_bytes=24 * MIB),
    )(*[a if space is VMEM else pltpu.with_memory_space_constraint(a, space) for a, space in pairs])


def split(x):
    high = x.astype(BF16)
    return high, (x - high.astype(F32)).astype(BF16)


def dot(x, y):
    return jnp.dot(x, y, preferred_element_type=F32)


def dot_split(x, y):
    return dot(x[0], y[0]) + (dot(x[0], y[1]) + dot(x[1], y[0]))


def langmuir(lagged, rate, affinity):
    return rate * lagged * pltpu.reciprocal(1.0 + affinity * jnp.abs(lagged), approx=True)


def lateral_rows(field, per_side):
    plane = per_side * per_side
    return jnp.concatenate(
        [field[a * plane + plane - per_side : (a + 1) * plane] for a in range(per_side)], axis=0
    )


def pack_map(mapping, lanes):
    face = mapping.shape[0]
    rows = face * face // lanes
    return jnp.concatenate([mapping[q * rows : (q + 1) * rows] for q in range(lanes // face)], axis=1)


def unpack_map(packed, face):
    return jnp.concatenate(
        [packed[:, q * face : (q + 1) * face] for q in range(packed.shape[1] // face)], axis=0
    )


def stack_maps(both):
    face = both.shape[1] // 2
    turned = pltpu.roll(both, face, 1)
    first = lax.broadcasted_iota(jnp.int32, both.shape, 1) < face
    low = split(both)[1]
    return jnp.concatenate(
        [jnp.where(first, both, turned).astype(BF16), low, jnp.where(first, turned, both).astype(BF16)], axis=1
    )


def stack_inflow(f):
    return (f[0], f[1], f[0])


def stack_side(s):
    return (s[0], s[0], s[1])


def in_pairs(items, per, step):
    def turn(t, _):
        step([t * per + k for k in range(per)])
        return 0

    lax.fori_loop(0, items // per, turn, 0)


def bit(stage):
    return ((lax.axis_index("stream") >> stage) & 1) == 1


def per_device(inverse, upwind, lateral, inlet_trace, previous, uptake_rate, affinity, flow_order):
    cols, _, count, nodes, _ = inverse.shape
    face = upwind.shape[3]
    tracers = previous.shape[-1]
    per_side = NODES_1D
    plane = per_side * per_side
    wide = count * face
    packed = face * face // tracers
    streams, lats = lax.axis_size("stream"), lax.axis_size("lat")
    stages = streams.bit_length() - 1
    assert streams == 1 << stages
    assert cols > 1
    early, late = list(range(1, cols)), [0]
    groups = [early, late]
    home = {c: (g, n) for g, group in enumerate(groups) for n, c in enumerate(group)}
    ending = pl.ds(nodes - face, face)
    per = 2 if count % 2 == 0 else 1

    def to_next(value):
        return lax.ppermute(value, "lat", [(i, (i + 1) % lats) for i in range(lats)])

    def swap(value, stage):
        return lax.ppermute(value, "stream", [(i, i ^ (1 << stage)) for i in range(streams)])

    inv_near, up_near, side_near, old_near = (
        pltpu.with_memory_space_constraint(a, VMEM) for a in (inverse, upwind, lateral, previous)
    )
    shaped = previous.reshape(cols, count, per_side, plane, tracers)

    def map_outs(size):
        return [VMEM((size * count, nodes, 6 * face), BF16), VMEM((size * count, face, 6 * face), BF16)]

    def chain_outs(size):
        return [
            VMEM((size * count, face, 2 * face), F32),
            VMEM((size, wide + face, wide), BF16),
            VMEM((size, wide + face, wide), BF16),
        ]

    def side_outs(size):
        return [VMEM((size * count, 2, face, tracers), BF16), VMEM((size * count, face, tracers), F32)]

    def offset_scratch(size):
        return [VMEM((size, wide - face, tracers), BF16)] * 2

    def source_outs(size):
        return [VMEM((size * count, nodes, tracers), BF16)] * 2

    def times(matrix, high, low, i):
        return dot(matrix, high[i]) + dot(matrix, low[i])

    def face_maps(matrix, up, side):
        faces = jnp.concatenate([up, side], axis=0)
        return lax.dot_general(matrix, faces, (((1,), (1,)), ((), ())), preferred_element_type=F32)

    def at(group, i):
        return group[0] + i // count, 0, i % count

    def side_of(tails, i, s):
        return dot_split(split(tails[i][:, face:]), s)

    def link(n, p, step, rows_high, rows_low, row):
        row_id = lax.broadcasted_iota(jnp.int32, (face, wide), 0)
        lane_id = lax.broadcasted_iota(jnp.int32, (face, wide), 1)
        unit = jnp.where(lane_id == row_id + p * face, 1.0, 0.0)
        r = split(jnp.where(p == 0, 0.0, row[n]) + unit)
        here = pl.ds(pl.multiple_of(p * face, face), face)
        rows_high[n, here] = r[0]
        rows_low[n, here] = r[1]
        r = split(dot_split(step, r))
        rows_high[n, pl.ds(wide, face)] = r[0]
        rows_low[n, pl.ds(wide, face)] = r[1]
        row[n] = r[0].astype(F32) + r[1].astype(F32)

    def offset(n, rows_high, rows_low, ends, high, low):
        for p in range(count - 1):
            e = split(ends[n * count + p])
            high[n, pl.ds(p * face, face)] = e[0]
            low[n, pl.ds(p * face, face)] = e[1]
        last = pl.ds(wide, face)
        row = (rows_high[n, last][:, face:], rows_low[n, last][:, face:])
        return ends[n * count + count - 1] + dot_split(row, (high[n], low[n]))

    def load():
        size = len(early)
        items = size * count

        def body(
            order, rate, aff, inlet, old, inverse, upwind, lateral, previous,
            trace, o_order, o_rate, o_aff, o_inlet, near, o_tail, faces, source_high, source_low,
            lagged, staged, lead_sems, sems,
        ):
            rows = pl.ds(plane - 2 * per_side, 2 * per_side)
            lead = [
                pltpu.make_async_copy(a, b, lead_sems.at[k])
                for k, (a, b) in enumerate((
                    (rate, o_rate),
                    (aff, o_aff),
                    (order, o_order),
                    (old.at[0, :, :, rows], staged),
                    (inlet, o_inlet),
                ))
            ]
            whole = pl.ds(0, count)
            fields, others = [], []
            for n, c in enumerate(early):
                for h in range(0, count, per):
                    here, there = pl.ds(h, per), pl.ds(n * count + h, per)
                    fields.append((previous.at[c, 0, here], lagged.at[there]))
                there = pl.ds(n * count, count)
                others += [
                    (inverse.at[c, 0, whole, ending], o_tail.at[there]),
                    (upwind.at[c, 0], faces.at[there, pl.ds(0, face)]),
                    (lateral.at[c, 0], faces.at[there, pl.ds(face, face)]),
                ]
            copies = [pltpu.make_async_copy(a, b, sems.at[k]) for k, (a, b) in enumerate(fields + others)]
            for one in lead[:3] + copies[: len(fields)] + lead[3:4] + copies[len(fields) :] + lead[4:]:
                one.start()
            for one in lead[:3]:
                one.wait()

            def old_rows(field):
                return jnp.concatenate([field(a).astype(F32)[per_side:] for a in range(per_side)], axis=0)

            for k in range(len(fields)):
                copies[k].wait()
                for i in range(k * per, k * per + per):
                    lag = lagged[i].astype(F32)
                    source_high[i], source_low[i] = split(langmuir(lag, o_rate[...], o_aff[...]))
                    c = early[i // count]
                    if c == cols - 1:
                        trace[i % count] = lateral_rows(lag, per_side)
                    else:
                        near[i + count] = lateral_rows(lag, per_side)
            for one in lead[3:]:
                one.wait()
            for j in range(count):
                near[j] = old_rows(lambda a: staged[j, a])
            for one in copies[len(fields) :]:
                one.wait()

        values = run(
            body,
            "load",
            [
                (flow_order.reshape(cols, count), HBM),
                (uptake_rate.reshape(1, tracers), HBM),
                (affinity.reshape(1, tracers), HBM),
                (inlet_trace, HBM),
                (shaped, HBM),
                (inverse, HBM),
                (upwind, HBM),
                (lateral, HBM),
                (previous, HBM),
            ],
            [
                VMEM((count, face, tracers), F32),
                SMEM((cols, count), jnp.int32),
                VMEM((1, tracers), F32),
                VMEM((1, tracers), F32),
                VMEM((cols, face, tracers), F32),
                VMEM((items, face, tracers), F32),
                VMEM((items, face, nodes), BF16),
                VMEM((items, 2 * face, nodes), BF16),
                *source_outs(size),
            ],
            [
                VMEM((items, nodes, tracers), BF16),
                VMEM((count, per_side, 2 * per_side, tracers), BF16),
                pltpu.SemaphoreType.DMA((5,)),
                pltpu.SemaphoreType.DMA((size * (count // per + 3),)),
            ],
        )
        state = SimpleNamespace()
        state.near, state.tail, state.faces, state.source_high, state.source_low = values[5:]
        return values[:5], state

    def begin_early(state):
        size = len(early)
        items = size * count

        def body(
            order, near, tail, faces, source_high, source_low, tails, sides, ends, message, own
        ):
            def step(members):
                for i in members:
                    tails[i] = face_maps(tail[i], faces[i, :face], faces[i, face:])
                    own[i] = times(tail[i], source_high, source_low, i)

            in_pairs(items, per, step)
            for n, c in enumerate(early):
                links = []
                for p in range(count):
                    i = n * count + order[c, p]
                    s = split(near[i])
                    sides[n * count + p, 0] = s[0]
                    sides[n * count + p, 1] = s[1]
                    end = own[i] + side_of(tails, i, s)
                    ends[n * count + p] = end
                    links.append((tails[i][:, :face], end))
                while len(links) > 1:
                    paired = []
                    for (low, start), (up, end) in zip(links[::2], links[1::2]):
                        u = split(up)
                        paired.append((dot_split(u, split(low)), end + dot_split(u, split(start))))
                    links = paired + links[2 * len(paired) :]
                message[n, pl.ds(0, face)] = links[0][1]
                message[n, pl.ds(face, packed)] = pack_map(links[0][0], tracers)

        state.tails, state.sides, state.ends, state.message = run(
            body,
            "begin_early",
            [order, state.near, state.tail, state.faces, state.source_high, state.source_low],
            [
                VMEM((items, face, 2 * face), F32),
                *side_outs(size),
                VMEM((size, face + packed, tracers), F32),
            ],
            [VMEM((items, face, tracers), F32)],
        )

    def early_maps(state, after):
        size = len(early)

        def body(order, inv, up, side, tails, _, maps, side_maps, rows_high, rows_low, row):
            for i in range(size * count):
                k = at(early, i)
                both = face_maps(inv[k], up[k], side[k])
                maps[i] = stack_maps(both)
                side_maps[i] = stack_maps(lateral_rows(both, per_side))
                n, p = i // count, i % count
                head = tails[n * count + order[early[0] + n, p]][:, :face]
                link(n, p, split(head), rows_high, rows_low, row)

        state.maps, state.side_maps, state.high, state.low = run(
            body,
            "early_maps",
            [order, inv_near, up_near, side_near, state.tails, after],
            map_outs(size) + chain_outs(size)[1:],
            [VMEM((size, face, wide), F32)],
        )
        return state.maps

    def whole_free(group, state, after):
        size = len(group)

        def body(inv, source_high, source_low, _, free):
            for i in range(size * count):
                free[i] = times(inv[at(group, i)], source_high, source_low, i)

        (state.free,) = run(
            body,
            "whole_free",
            [inv_near, state.source_high, state.source_low, after],
            [VMEM((size * count, nodes, tracers), F32)],
            [],
        )

    def begin_late(after):
        size = len(late)
        items = size * count

        def body(
            order, inv, up, side, previous, rate, aff, _,
            source_high, source_low, own, tails, rows_high, rows_low, mapped, row,
        ):
            for i in range(items):
                k = at(late, i)
                tails[i] = face_maps(inv[*k, ending], up[k], side[k])
            for i in range(items + 1):
                if i < items:
                    lag = previous[at(late, i)].astype(F32)
                    source_high[i], source_low[i] = split(langmuir(lag, rate[...], aff[...]))
                    n, p = i // count, i % count
                    step = split(tails[n * count + order[late[n], p]][:, :face])
                    link(n, p, step, rows_high, rows_low, row)
                if i > 0:
                    own[i - 1] = times(inv[*at(late, i - 1), ending], source_high, source_low, i - 1)
            for n in range(size):
                mapped[n] = pack_map(row[n][:, :face], tracers)

        state = SimpleNamespace()
        values = run(
            body,
            "begin_late",
            [order, inv_near, up_near, side_near, old_near, rate, aff, after],
            source_outs(size)
            + [VMEM((items, face, tracers), F32)]
            + chain_outs(size)
            + [VMEM((size, packed, tracers), F32)],
            [VMEM((size, face, wide), F32)],
        )
        state.source_high, state.source_low, state.own, state.tails, state.high, state.low, state.mapped = values
        return state

    def late_maps(state, after):
        items = len(late) * count

        def body(inv, up, side, _, maps):
            for i in range(items):
                k = at(late, i)
                maps[i] = stack_maps(face_maps(inv[k], up[k], side[k]))

        (state.maps,) = run(
            body, "late_maps", [inv_near, up_near, side_near, after], map_outs(len(late))[:1], []
        )
        return state.maps

    def arrived_side(arrived, j):
        return split(jnp.where(lax.axis_index("lat") > 0, arrived[j], 0.0))

    def first_sides(state, arrived):
        def body(order, arrived, own, tails, rows_high, rows_low, mapped, sides, ends, message, high, low):
            for p in range(count):
                j = order[0, p]
                s = arrived_side(arrived, j)
                sides[p, 0] = s[0]
                sides[p, 1] = s[1]
                ends[p] = own[j] + side_of(tails, j, s)
            message[0, pl.ds(0, face)] = offset(0, rows_high, rows_low, ends, high, low)
            message[0, pl.ds(face, packed)] = mapped[0]

        state.sides, state.ends, state.message = run(
            body,
            "first_sides",
            [order, arrived, state.own, state.tails, state.high, state.low, state.mapped],
            side_outs(1) + [VMEM((1, face + packed, tracers), F32)],
            offset_scratch(1),
        )

    def combine_first(stage, own, other, after):
        def body(own, other, _, message):
            upper = bit(stage)
            for n in range(own.shape[0]):
                up = jnp.where(upper, own[n], other[n])
                low = jnp.where(upper, other[n], own[n])
                m = split(unpack_map(up[face:], face))
                message[n, pl.ds(0, face)] = dot_split(m, split(low[:face])) + up[:face]
                mapped = dot_split(m, split(unpack_map(low[face:], face)))
                message[n, pl.ds(face, packed)] = pack_map(mapped, tracers)

        return run(body, "combine", [own, other, after], [VMEM(own.shape, F32)], [])[0]

    def combine_second(stage, own, other, old_own, old_other):
        def body(own, other, *refs):
            message = refs[-1]
            upper = bit(stage)
            for c in range(cols):
                g, n = home[c]
                mine, theirs = refs[2 * g], refs[2 * g + 1]
                m = jnp.where(upper, mine[n, pl.ds(face, packed)], theirs[n, pl.ds(face, packed)])
                up = jnp.where(upper, own[c], other[c])
                low = jnp.where(upper, other[c], own[c])
                message[c] = dot_split(split(unpack_map(m, face)), split(low)) + up

        ins = [own, other]
        for pair in zip(old_own, old_other):
            ins += pair
        return run(body, "combine", ins, [VMEM(own.shape, F32)], [])[0]

    def entering(start, offsets, maps):
        for stage in reversed(range(stages)):
            m = split(unpack_map(maps[stage], face))
            beyond = dot_split(m, split(start)) + offsets[stage]
            start = jnp.where(bit(stage), beyond, start)
        return start

    def enter_first(group, state, after):
        size = len(group)
        last = group[-1] == cols - 1

        def body(order, inlet, rows_high, rows_low, sides, ends, *refs):
            got, refs = refs[:stages], refs[stages:]
            if last:
                (free, side_maps), refs = refs[:2], refs[3:]
            stack, (high, low) = refs[0], refs[-2:]
            for n, c in enumerate(group):
                for p in range(count - 1):
                    e = split(ends[n * count + p])
                    high[n, pl.ds((p + 1) * face, face)] = e[0]
                    low[n, pl.ds((p + 1) * face, face)] = e[1]
                maps = [r[n, pl.ds(face, packed)] for r in got]
                e = split(entering(inlet[c], [r[n, pl.ds(0, face)] for r in got], maps))
                high[n, pl.ds(0, face)] = e[0]
                low[n, pl.ds(0, face)] = e[1]
                span = pl.ds(0, wide)
                inflow = dot_split((rows_high[n, span], rows_low[n, span]), (high[n], low[n]))
                for p in range(count):
                    i = n * count + order[c, p]
                    f = split(inflow[p * face : (p + 1) * face])
                    s = (sides[n * count + p, 0], sides[n * count + p, 1])
                    for q, part in enumerate(stack_inflow(f) + stack_side(s)):
                        stack[i, pl.ds(q * face, face)] = part
            if last:
                for j in range(count):
                    i = (size - 1) * count + j
                    refs[1][j] = lateral_rows(free.at[i], per_side) + dot(side_maps[i], stack[i])

        outs = [VMEM((size * count, 6 * face, tracers), BF16)]
        if last:
            outs.append(VMEM((count, face, tracers), F32))
        ins = [order, inlet, state.high, state.low, state.sides, state.ends, *state.received]
        if last:
            ins += [state.free, state.side_maps, after]
        scratch = [VMEM((size, wide, tracers), BF16)] * 2
        values = run(body, "enter", ins, outs, scratch)
        state.stack = values[0]
        return values[1] if last else None

    def second(group, state, after):
        items = len(group) * count

        def body(inv, maps, free, stack, rate, aff, _, source_high, source_low, traces, own):
            for i in range(items + 1):
                if i < items:
                    swept = free[i] + dot(maps[i], stack[i])
                    traces[i] = lateral_rows(swept, per_side)
                    source_high[i], source_low[i] = split(langmuir(swept, rate[...], aff[...]))
                if i > 0:
                    own[i - 1] = times(inv[*at(group, i - 1), ending], source_high, source_low, i - 1)

        state.source_high, state.source_low, state.traces, state.own = run(
            body,
            "second",
            [inv_near, state.maps, state.free, state.stack, rate, aff, after],
            source_outs(len(group)) + [VMEM((items, face, tracers), F32)] * 2,
            [],
        )

    def second_sides(arrived):
        def body(order, arrived, *refs):
            got = [refs[5 * g : 5 * g + 5] for g in range(len(groups))]
            message, *refs = refs[5 * len(groups) :]
            for g, group in enumerate(groups):
                own, _, tails, rows_high, rows_low = got[g]
                stack, ends = refs[2 * g : 2 * g + 2]
                high, low = refs[2 * (len(groups) + g) : 2 * (len(groups) + g) + 2]
                for n, c in enumerate(group):
                    for p in range(count):
                        j = order[c, p]
                        i = n * count + j
                        if c == 0:
                            s = arrived_side(arrived, j)
                        else:
                            h, m = home[c - 1]
                            s = split(got[h][1][m * count + j])
                        stack[i, pl.ds(0, face)] = jnp.zeros((face, tracers), BF16)
                        for q, part in enumerate(stack_side(s)):
                            stack[i, pl.ds((q + 1) * face, face)] = part
                        ends[n * count + p] = own[i] + side_of(tails, i, s)
                    message[c] = offset(n, rows_high, rows_low, ends, high, low)

        ins = [order, arrived]
        outs, scratch = [VMEM((cols, face, tracers), F32)], []
        for group, state in zip(groups, states):
            ins += [state.own, state.traces, state.tails, state.high, state.low]
            outs.append(VMEM((len(group) * count, 4 * face, tracers), BF16))
            outs.append(VMEM((len(group) * count, face, tracers), F32))
            scratch += offset_scratch(len(group))
        message, *values = run(body, "second_sides", ins, outs, scratch)
        for g, state in enumerate(states):
            state.side_stack, state.ends = values[2 * g : 2 * g + 2]
        return message

    def settle(after):
        def body(_, inv, *refs):
            got = [refs[7 * g : 7 * g + 7] for g in range(len(groups))]
            outs = refs[7 * len(groups) :]
            for g, group in enumerate(groups):
                source_high, source_low, maps, stack, ends, rows_high, rows_low = got[g]
                base, within, high, low = outs[2 * g], outs[2 * g + 1], outs[-2], outs[-1]
                for i in range(len(group) * count):
                    own = times(inv[at(group, i)], source_high, source_low, i)
                    base[i] = own + dot(maps[i][:, 2 * face :], stack[i])
                for n in range(len(group)):
                    for p in range(count - 1):
                        e = split(ends[n * count + p])
                        high[pl.ds(p * face, face)] = e[0]
                        low[pl.ds(p * face, face)] = e[1]
                    span = pl.ds(0, wide)
                    rows = (rows_high[n, span][:, face:], rows_low[n, span][:, face:])
                    within[n] = dot_split(rows, (high[...], low[...]))

        ins = [after, inv_near]
        outs = []
        for group, state in zip(groups, states):
            ins += [state.source_high, state.source_low]
            ins += [state.maps, state.side_stack, state.ends, state.high, state.low]
            outs.append(VMEM((len(group) * count, nodes, tracers), F32))
            outs.append(VMEM((len(group), wide, tracers), F32))
        scratch = [VMEM((wide - face, tracers), BF16)] * 2
        values = run(body, "settle", ins, outs, scratch)
        for g, state in enumerate(states):
            state.base, state.within = values[2 * g : 2 * g + 2]

    def result(offsets):
        parts = 5 + stages

        def body(order, inlet, *refs):
            offs, refs = refs[:stages], refs[stages:]
            got = [refs[parts * g : parts * g + parts] for g in range(len(groups))]
            out, staged, sems, *stacks = refs[parts * len(groups) :]
            for g, group in enumerate(groups):
                rows_high, rows_low, within, _, _, *mapped = got[g]
                for n, c in enumerate(group):
                    maps = [r[n, pl.ds(face, packed)] for r in mapped]
                    e = split(entering(inlet[c], [r[c] for r in offs], maps))
                    span = pl.ds(0, wide)
                    rows = (rows_high[n, span][:, :face], rows_low[n, span][:, :face])
                    inflow = within[n] + dot_split(rows, e)
                    for p in range(count):
                        i = n * count + order[c, p]
                        for q, part in enumerate(stack_inflow(split(inflow[p * face : (p + 1) * face]))):
                            stacks[g][i, pl.ds(q * face, face)] = part
            started = []
            for g, group in enumerate(groups):
                base, maps = got[g][3:5]
                for n, c in enumerate(group):
                    for j in range(count):
                        i, k = n * count + j, len(started)
                        staged[k] = (base[i] + dot(maps[i][:, : 3 * face], stacks[g][i])).astype(BF16)
                        copy = pltpu.make_async_copy(staged.at[k], out.at[c, 0, j], sems.at[k])
                        copy.start()
                        started.append(copy)
            for copy in started:
                copy.wait()

        ins = [order, inlet, *offsets]
        scratch = [VMEM((cols * count, nodes, tracers), BF16), pltpu.SemaphoreType.DMA((cols * count,))]
        for group, state in zip(groups, states):
            ins += [state.high, state.low, state.within, state.base, state.maps, *state.received]
            scratch.append(VMEM((len(group) * count, 3 * face, tracers), BF16))
        return run(body, "result", ins, [HBM(previous.shape, BF16)], scratch)[0]

    def exchange_first(state, beside):
        state.sent, state.received = [state.message], []
        for stage in range(stages):
            if stage:
                state.sent.append(combine_first(stage - 1, state.sent[-1], state.received[-1], after))
            state.received.append(swap(state.sent[-1], stage))
            if not stage:
                after = beside()

    (trace, order, rate, aff, inlet), one = load()
    order = (order, SMEM)
    arrived = to_next(trace)
    begin_early(one)
    exchange_first(one, lambda: early_maps(one, one.message))
    two = begin_late(one.sent[-1])
    whole_free(early, one, one.sent[-1])
    states = [one, two]
    trace = enter_first(early, one, two.mapped)
    arrived_next = to_next(trace)
    first_sides(two, arrived)
    exchange_first(two, lambda: late_maps(two, two.message))
    second(early, one, two.sent[-1])
    whole_free(late, two, two.sent[-1])
    enter_first(late, two, None)
    second(late, two, two.sent[-1])
    message, offsets = second_sides(arrived_next), []
    for stage in range(stages):
        offsets.append(swap(message, stage))
        if stage + 1 < stages:
            message = combine_second(
                stage, message, offsets[-1], [s.sent[stage] for s in states], [s.received[stage] for s in states]
            )
    settle(message)
    return result(offsets)


def solution(mesh):
    placed = (
        P("lat", "stream", None, None, None),
        P("lat", "stream", None, None, None),
        P("lat", "stream", None, None, None),
        P("lat", None, None),
        P("lat", "stream", None, None, None),
        P(),
        P(),
        P("lat", "stream", None),
    )
    return jax.shard_map(
        per_device,
        mesh=mesh,
        in_specs=placed,
        out_specs=P("lat", "stream", None, None, None),
        check_vma=False,
    )
```

```python
from types import SimpleNamespace

import jax
import jax.numpy as jnp
from jax import lax
from jax.experimental import pallas as pl
from jax.experimental.pallas import tpu as pltpu
from jax.sharding import PartitionSpec as P

NODES_1D = 8
F32 = jnp.float32
BF16 = jnp.bfloat16
MIB = 1 << 20
VMEM = pltpu.VMEM
HBM = pltpu.HBM
SMEM = pltpu.SMEM


def run(body, name, ins, outs, scratch):
    pairs = [a if isinstance(a, tuple) else (a, VMEM) for a in ins]
    return pl.pallas_call(
        body,
        name=name,
        in_specs=[pl.BlockSpec(memory_space=space) for _, space in pairs],
        out_specs=[pl.BlockSpec(memory_space=o.memory_space) for o in outs],
        out_shape=outs,
        scratch_shapes=scratch,
        cost_estimate=pl.CostEstimate(flops=0, bytes_accessed=0, transcendentals=0),
        compiler_params=pltpu.CompilerParams(vmem_limit_bytes=24 * MIB),
    )(*[a if space is VMEM else pltpu.with_memory_space_constraint(a, space) for a, space in pairs])


def split(x):
    high = x.astype(BF16)
    return high, (x - high.astype(F32)).astype(BF16)


def dot(x, y):
    return jnp.dot(x, y, preferred_element_type=F32)


def dot_split(x, y):
    return dot(x[0], y[0]) + (dot(x[0], y[1]) + dot(x[1], y[0]))


def langmuir(lagged, rate, affinity):
    return rate * lagged * pltpu.reciprocal(1.0 + affinity * jnp.abs(lagged), approx=True)


def lateral_rows(field, per_side):
    plane = per_side * per_side
    return jnp.concatenate(
        [field[a * plane + plane - per_side : (a + 1) * plane] for a in range(per_side)], axis=0
    )


def pack_map(mapping, lanes):
    face = mapping.shape[0]
    rows = face * face // lanes
    return jnp.concatenate([mapping[q * rows : (q + 1) * rows] for q in range(lanes // face)], axis=1)


def unpack_map(packed, face):
    return jnp.concatenate(
        [packed[:, q * face : (q + 1) * face] for q in range(packed.shape[1] // face)], axis=0
    )


def stack_maps(both):
    face = both.shape[1] // 2
    turned = pltpu.roll(both, face, 1)
    first = lax.broadcasted_iota(jnp.int32, both.shape, 1) < face
    low = split(both)[1]
    return jnp.concatenate(
        [jnp.where(first, both, turned).astype(BF16), low, jnp.where(first, turned, both).astype(BF16)], axis=1
    )


def stack_inflow(f):
    return (f[0], f[1], f[0])


def stack_side(s):
    return (s[0], s[0], s[1])


def in_pairs(items, per, step):
    def turn(t, _):
        step([t * per + k for k in range(per)])
        return 0

    lax.fori_loop(0, items // per, turn, 0)


def known_inflow(inlet):
    return jnp.where(lax.axis_index("stream") == 0, inlet, 0.0)


def bit(stage):
    return ((lax.axis_index("stream") >> stage) & 1) == 1


def per_device(inverse, upwind, lateral, inlet_trace, previous, uptake_rate, affinity, flow_order):
    cols, _, count, nodes, _ = inverse.shape
    face = upwind.shape[3]
    tracers = previous.shape[-1]
    per_side = NODES_1D
    plane = per_side * per_side
    wide = count * face
    packed = face * face // tracers
    sent_rows = face + (packed if lax.axis_size("stream") > 2 else 0)
    streams, lats = lax.axis_size("stream"), lax.axis_size("lat")
    stages = streams.bit_length() - 1
    assert streams == 1 << stages
    assert cols > 1
    early, late = list(range(1, cols)), [0]
    groups = [early, late]
    home = {c: (g, n) for g, group in enumerate(groups) for n, c in enumerate(group)}
    ending = pl.ds(nodes - face, face)
    per = 2 if count % 2 == 0 else 1

    def to_next(value):
        return lax.ppermute(value, "lat", [(i, (i + 1) % lats) for i in range(lats)])

    def swap(value, stage):
        return lax.ppermute(value, "stream", [(i, i ^ (1 << stage)) for i in range(streams)])

    inv_near, up_near, side_near, old_near = (
        pltpu.with_memory_space_constraint(a, VMEM) for a in (inverse, upwind, lateral, previous)
    )
    shaped = previous.reshape(cols, count, per_side, plane, tracers)

    def map_outs(size):
        return [VMEM((size * count, nodes, 6 * face), BF16), VMEM((size * count, face, 6 * face), BF16)]

    def chain_outs(size):
        return [
            VMEM((size * count, face, 2 * face), F32),
            VMEM((size, wide + face, wide), BF16),
            VMEM((size, wide + face, wide), BF16),
        ]

    def offset_scratch(size):
        return [VMEM((size, wide, tracers), BF16)] * 2

    def source_outs(size):
        return [VMEM((size * count, nodes, tracers), BF16)] * 2

    def times(matrix, high, low, i):
        return dot(matrix, high[i]) + dot(matrix, low[i])

    def face_maps(matrix, up, side):
        faces = jnp.concatenate([up, side], axis=0)
        return lax.dot_general(matrix, faces, (((1,), (1,)), ((), ())), preferred_element_type=F32)

    def at(group, i):
        return group[0] + i // count, 0, i % count

    def side_of(tails, i, s):
        return dot_split(split(tails[i][:, face:]), s)

    def link(n, p, step, rows_high, rows_low, row):
        row_id = lax.broadcasted_iota(jnp.int32, (face, wide), 0)
        lane_id = lax.broadcasted_iota(jnp.int32, (face, wide), 1)
        unit = jnp.where(lane_id == row_id + p * face, 1.0, 0.0)
        r = split(jnp.where(p == 0, 0.0, row[n]) + unit)
        here = pl.ds(pl.multiple_of(p * face, face), face)
        rows_high[n, here] = r[0]
        rows_low[n, here] = r[1]
        r = split(dot_split(step, r))
        rows_high[n, pl.ds(wide, face)] = r[0]
        rows_low[n, pl.ds(wide, face)] = r[1]
        row[n] = r[0].astype(F32) + r[1].astype(F32)

    def offset(n, start, rows_high, rows_low, ends, high, low):
        for p in range(count):
            e = split(start if p == 0 else ends[n * count + p - 1])
            high[n, pl.ds(p * face, face)] = e[0]
            low[n, pl.ds(p * face, face)] = e[1]
        last = pl.ds(wide, face)
        return ends[n * count + count - 1] + dot_split((rows_high[n, last], rows_low[n, last]), (high[n], low[n]))

    def load():
        size = len(early)
        items = size * count

        def body(
            order, rate, aff, inlet, old, inverse, upwind, lateral, previous,
            trace, o_order, o_rate, o_aff, o_inlet, near, o_tail, faces, source_high, source_low,
            lagged, staged, lead_sems, sems,
        ):
            rows = pl.ds(plane - 2 * per_side, 2 * per_side)
            lead = [
                pltpu.make_async_copy(a, b, lead_sems.at[k])
                for k, (a, b) in enumerate((
                    (rate, o_rate),
                    (aff, o_aff),
                    (order, o_order),
                    (old.at[0, :, :, rows], staged),
                    (inlet, o_inlet),
                ))
            ]
            whole = pl.ds(0, count)
            fields, others = [], []
            for n, c in enumerate(early):
                for h in range(0, count, per):
                    here, there = pl.ds(h, per), pl.ds(n * count + h, per)
                    fields.append((previous.at[c, 0, here], lagged.at[there]))
                there = pl.ds(n * count, count)
                others += [
                    (inverse.at[c, 0, whole, ending], o_tail.at[there]),
                    (upwind.at[c, 0], faces.at[there, pl.ds(0, face)]),
                    (lateral.at[c, 0], faces.at[there, pl.ds(face, face)]),
                ]
            copies = [pltpu.make_async_copy(a, b, sems.at[k]) for k, (a, b) in enumerate(fields + others)]
            for one in lead[:3] + copies[: len(fields)] + lead[3:4] + copies[len(fields) :] + lead[4:]:
                one.start()
            for one in lead[:3]:
                one.wait()

            def old_rows(field):
                return jnp.concatenate([field(a).astype(F32)[per_side:] for a in range(per_side)], axis=0)

            for k in range(len(fields)):
                copies[k].wait()
                for i in range(k * per, k * per + per):
                    lag = lagged[i].astype(F32)
                    source_high[i], source_low[i] = split(langmuir(lag, o_rate[...], o_aff[...]))
                    c = early[i // count]
                    if c == cols - 1:
                        trace[i % count] = lateral_rows(lag, per_side)
                    else:
                        near[i + count] = lateral_rows(lag, per_side)
            for one in lead[3:]:
                one.wait()
            for j in range(count):
                near[j] = old_rows(lambda a: staged[j, a])
            for one in copies[len(fields) :]:
                one.wait()

        values = run(
            body,
            "load",
            [
                (flow_order.reshape(cols, count), HBM),
                (uptake_rate.reshape(1, tracers), HBM),
                (affinity.reshape(1, tracers), HBM),
                (inlet_trace, HBM),
                (shaped, HBM),
                (inverse, HBM),
                (upwind, HBM),
                (lateral, HBM),
                (previous, HBM),
            ],
            [
                VMEM((count, face, tracers), F32),
                SMEM((cols, count), jnp.int32),
                VMEM((1, tracers), F32),
                VMEM((1, tracers), F32),
                VMEM((cols, face, tracers), F32),
                VMEM((items, face, tracers), F32),
                VMEM((items, face, nodes), BF16),
                VMEM((items, 2 * face, nodes), BF16),
                *source_outs(size),
            ],
            [
                VMEM((items, nodes, tracers), BF16),
                VMEM((count, per_side, 2 * per_side, tracers), BF16),
                pltpu.SemaphoreType.DMA((5,)),
                pltpu.SemaphoreType.DMA((size * (count // per + 3),)),
            ],
        )
        state = SimpleNamespace()
        state.near, state.tail, state.faces, state.source_high, state.source_low = values[5:]
        return values[:5], state

    def begin_early(state):
        size = len(early)
        items = size * count

        def body(
            order, inlet, near, tail, faces, source_high, source_low, tails, ends, message, own
        ):
            def step(members):
                for i in members:
                    tails[i] = face_maps(tail[i], faces[i, :face], faces[i, face:])
                    own[i] = times(tail[i], source_high, source_low, i)

            in_pairs(items, per, step)
            for n, c in enumerate(early):
                links = []
                for p in range(count):
                    i = n * count + order[c, p]
                    end = own[i] + side_of(tails, i, split(near[i]))
                    ends[n * count + p] = end
                    if p == 0:
                        begun = split(known_inflow(inlet[c]))
                        end = end + dot_split(split(tails[i][:, :face]), begun)
                    links.append((tails[i][:, :face], end))
                while len(links) > 1:
                    paired = []
                    for (low, start), (up, end) in zip(links[::2], links[1::2]):
                        u = split(up)
                        paired.append((dot_split(u, split(low)), end + dot_split(u, split(start))))
                    links = paired + links[2 * len(paired) :]
                message[n, pl.ds(0, face)] = links[0][1]
                if sent_rows > face:
                    message[n, pl.ds(face, packed)] = pack_map(links[0][0], tracers)

        state.tails, state.ends, state.message = run(
            body,
            "begin_early",
            [order, inlet, state.near, state.tail, state.faces, state.source_high, state.source_low],
            [
                VMEM((items, face, 2 * face), F32),
                VMEM((items, face, tracers), F32),
                VMEM((size, sent_rows, tracers), F32),
            ],
            [VMEM((items, face, tracers), F32)],
        )

    def early_maps(state, after):
        size = len(early)

        def body(order, inv, up, side, tails, _, maps, side_maps, rows_high, rows_low, row):
            for i in range(size * count):
                k = at(early, i)
                both = face_maps(inv[k], up[k], side[k])
                maps[i] = stack_maps(both)
                side_maps[i] = stack_maps(lateral_rows(both, per_side))
                n, p = i // count, i % count
                head = tails[n * count + order[early[0] + n, p]][:, :face]
                link(n, p, split(head), rows_high, rows_low, row)

        state.maps, state.side_maps, state.high, state.low = run(
            body,
            "early_maps",
            [order, inv_near, up_near, side_near, state.tails, after],
            map_outs(size) + chain_outs(size)[1:],
            [VMEM((size, face, wide), F32)],
        )
        return state.maps

    def begin_late(after):
        size = len(late)
        items = size * count

        def body(
            order, inv, up, side, previous, rate, aff, _,
            source_high, source_low, own, tails, rows_high, rows_low, mapped, row,
        ):
            for i in range(items):
                k = at(late, i)
                tails[i] = face_maps(inv[*k, ending], up[k], side[k])
            for i in range(items + 1):
                if i < items:
                    lag = previous[at(late, i)].astype(F32)
                    source_high[i], source_low[i] = split(langmuir(lag, rate[...], aff[...]))
                    n, p = i // count, i % count
                    step = split(tails[n * count + order[late[n], p]][:, :face])
                    link(n, p, step, rows_high, rows_low, row)
                if i > 0:
                    own[i - 1] = times(inv[*at(late, i - 1), ending], source_high, source_low, i - 1)
            for n in range(size):
                mapped[n] = pack_map(row[n][:, :face], tracers)

        state = SimpleNamespace()
        values = run(
            body,
            "begin_late",
            [order, inv_near, up_near, side_near, old_near, rate, aff, after],
            source_outs(size)
            + [VMEM((items, face, tracers), F32)]
            + chain_outs(size)
            + [VMEM((size, packed, tracers), F32)],
            [VMEM((size, face, wide), F32)],
        )
        state.source_high, state.source_low, state.own, state.tails, state.high, state.low, state.mapped = values
        return state

    def late_maps(after):
        items = len(late) * count

        def body(inv, up, side, _, maps):
            for i in range(items):
                k = at(late, i)
                maps[i] = stack_maps(face_maps(inv[k], up[k], side[k]))

        return run(body, "late_maps", [inv_near, up_near, side_near, after], map_outs(len(late))[:1], [])[0]

    def arrived_side(arrived, j):
        return split(jnp.where(lax.axis_index("lat") > 0, arrived[j], 0.0))

    def first_sides(state, arrived):
        def body(order, inlet, arrived, own, tails, rows_high, rows_low, mapped, ends, message, high, low):
            for p in range(count):
                j = order[0, p]
                ends[p] = own[j] + side_of(tails, j, arrived_side(arrived, j))
            message[0, pl.ds(0, face)] = offset(0, known_inflow(inlet[0]), rows_high, rows_low, ends, high, low)
            if sent_rows > face:
                message[0, pl.ds(face, packed)] = mapped[0]

        state.ends, state.message = run(
            body,
            "first_sides",
            [order, inlet, arrived, state.own, state.tails, state.high, state.low, state.mapped],
            [VMEM((count, face, tracers), F32), VMEM((1, sent_rows, tracers), F32)],
            offset_scratch(1),
        )

    def combine_first(stage, own, other, after):
        rows = face if stage + 2 == stages else sent_rows

        def body(own, other, _, message):
            upper = bit(stage)
            for n in range(own.shape[0]):
                up = jnp.where(upper, own[n], other[n])
                low = jnp.where(upper, other[n], own[n])
                m = split(unpack_map(up[face:], face))
                message[n, pl.ds(0, face)] = dot_split(m, split(low[:face])) + up[:face]
                if rows > face:
                    mapped = dot_split(m, split(unpack_map(low[face:], face)))
                    message[n, pl.ds(face, packed)] = pack_map(mapped, tracers)

        return run(body, "combine", [own, other, after], [VMEM((own.shape[0], rows, tracers), F32)], [])[0]

    def combine_second(stage, own, other, old_own, old_other):
        def body(own, other, *refs):
            message = refs[-1]
            upper = bit(stage)
            for c in range(cols):
                g, n = home[c]
                mine, theirs = refs[2 * g], refs[2 * g + 1]
                m = jnp.where(upper, mine[n, pl.ds(face, packed)], theirs[n, pl.ds(face, packed)])
                up = jnp.where(upper, own[c], other[c])
                low = jnp.where(upper, other[c], own[c])
                message[c] = dot_split(split(unpack_map(m, face)), split(low)) + up

        ins = [own, other]
        for pair in zip(old_own, old_other):
            ins += pair
        return run(body, "combine", ins, [VMEM(own.shape, F32)], [])[0]

    def entering(start, offsets, maps):
        for stage in reversed(range(len(maps))):
            m = split(unpack_map(maps[stage], face))
            beyond = dot_split(m, split(start)) + offsets[stage]
            start = jnp.where(bit(stage), beyond, start)
        return start

    def lower_maps(maps):
        rows = lax.broadcasted_iota(jnp.int32, (face, face), 0)
        total = jnp.where(rows == lax.broadcasted_iota(jnp.int32, (face, face), 1), 1.0, 0.0)
        for stage in reversed(range(stages - 1)):
            beyond = dot_split(split(unpack_map(maps[stage], face)), split(total))
            total = jnp.where(bit(stage), beyond, total)
        return total

    def within_of(n, start, ends, rows_high, rows_low, high, low):
        for p in range(count):
            e = split(start if p == 0 else ends[n * count + p - 1])
            high[n, pl.ds(p * face, face)] = e[0]
            low[n, pl.ds(p * face, face)] = e[1]
        span = pl.ds(0, wide)
        return dot_split((rows_high[n, span], rows_low[n, span]), (high[n], low[n]))

    def side_rows(s):
        return jnp.concatenate([jnp.zeros((face, tracers), BF16), *stack_side(s)], axis=0)

    def prepare(group, state, sides, after):
        size = len(group)
        lower = state.received[:-1]

        def body(inv, sides, source_high, source_low, maps, ends, rows_high, rows_low, _, *refs):
            mapped, (free, within, reach_high, reach_low, high, low) = refs[: len(lower)], refs[len(lower) :]
            span = pl.ds(0, wide)
            for n in range(size):
                old = [r[n, pl.ds(face, packed)] for r in mapped]
                start = entering(jnp.zeros((face, tracers), F32), [r[n, pl.ds(0, face)] for r in mapped], old)
                within[n] = within_of(n, start, ends, rows_high, rows_low, high, low)
                rows = (rows_high[n, span][:, :face], rows_low[n, span][:, :face])
                reach_high[n], reach_low[n] = split(dot_split(rows, split(lower_maps(old))))
            for i in range(size * count):
                s = arrived_side(sides, i) if group[0] == 0 else split(sides[i])
                whole = times(inv[at(group, i)], source_high, source_low, i)
                free[i] = whole + dot(maps[i][:, 2 * face :], side_rows(s))

        state.free, state.within, *state.reach = run(
            body,
            "prepare",
            [inv_near, sides, state.source_high, state.source_low, state.maps, state.ends, state.high, state.low]
            + [after, *lower],
            [VMEM((size * count, nodes, tracers), F32), VMEM((size, wide, tracers), F32)]
            + [VMEM((size, wide, face), BF16)] * 2,
            [VMEM((size, wide, tracers), BF16)] * 2,
        )

    def enter_first(group, state, after):
        size = len(group)
        last = group[-1] == cols - 1
        newest = state.received[-1:]

        def body(order, inlet, within, reach_high, reach_low, *refs):
            got, refs = refs[: len(newest)], refs[len(newest) :]
            if last:
                (free, side_maps), refs = refs[:2], refs[3:]
            stack = refs[0]
            for n, c in enumerate(group):
                start = known_inflow(inlet[c])
                for r in got:
                    start = jnp.where(bit(stages - 1), r[n], start)
                inflow = within[n] + dot_split((reach_high[n], reach_low[n]), split(start))
                put_inflow(n, c, inflow, order, stack)
            if last:
                for j in range(count):
                    i = (size - 1) * count + j
                    part = dot(side_maps[i][:, : 3 * face], stack[i])
                    refs[1][j] = lateral_rows(free.at[i], per_side) + part

        outs = [VMEM((size * count, 3 * face, tracers), BF16)]
        if last:
            outs.append(VMEM((count, face, tracers), F32))
        ins = [order, inlet, state.within, *state.reach, *newest]
        if last:
            ins += [state.free, state.side_maps, after]
        values = run(body, "enter", ins, outs, [])
        state.stack = values[0]
        return values[1] if last else None

    def put_inflow(n, c, inflow, order, stack):
        for p in range(count):
            i = n * count + order[c, p]
            for q, part in enumerate(stack_inflow(split(inflow[p * face : (p + 1) * face]))):
                stack[i, pl.ds(q * face, face)] = part

    def second(group, state, after):
        items = len(group) * count

        def body(inv, maps, free, stack, rate, aff, _, source_high, source_low, traces, own):
            for i in range(items + 1):
                if i < items:
                    swept = free[i] + dot(maps[i][:, : 3 * face], stack[i])
                    traces[i] = lateral_rows(swept, per_side)
                    source_high[i], source_low[i] = split(langmuir(swept, rate[...], aff[...]))
                if i > 0:
                    own[i - 1] = times(inv[*at(group, i - 1), ending], source_high, source_low, i - 1)

        state.source_high, state.source_low, state.traces, state.own = run(
            body,
            "second",
            [inv_near, state.maps, state.free, state.stack, rate, aff, after],
            source_outs(len(group)) + [VMEM((items, face, tracers), F32)] * 2,
            [],
        )
        return state.own

    def fold_sides(after):
        def body(order, inlet, _, *refs):
            got = [refs[3 * g : 3 * g + 3] for g in range(len(groups))]
            outs = refs[3 * len(groups) :]
            for g, group in enumerate(groups):
                tails, rows_high, rows_low = got[g]
                high, low, begun = outs[3 * g : 3 * g + 3]
                for n, c in enumerate(group):
                    start = split(known_inflow(inlet[c]))
                    begun[n] = dot_split(last_row(rows_high, rows_low, n, 0), start)
                    for p in range(count):
                        folded = split(tails[n * count + order[c, p]][:, face:])
                        if p + 1 < count:
                            folded = split(dot_split(last_row(rows_high, rows_low, n, p + 1), folded))
                        high[n, p] = folded[0]
                        low[n, p] = folded[1]

        ins, outs = [order, inlet, after], []
        for group, state in zip(groups, states):
            ins += [state.tails, state.high, state.low]
            outs += [VMEM((len(group), count, face, face), BF16)] * 2
            outs.append(VMEM((len(group), face, tracers), F32))
        values = run(body, "fold_sides", ins, outs, [])
        for g, state in enumerate(states):
            state.side_high, state.side_low, state.begun = values[3 * g : 3 * g + 3]
        return values[0]

    def last_row(rows_high, rows_low, n, block):
        place = pl.ds(wide, face)
        return tuple(r[n, place][:, block * face : (block + 1) * face] for r in (rows_high, rows_low))

    def side_at(c, j, arrived, traces):
        if c == 0:
            return arrived_side(arrived, j)
        h, m = home[c - 1]
        return split(traces[h][m * count + j])

    def second_sides(arrived):
        def body(order, arrived, *refs):
            got = [refs[7 * g : 7 * g + 7] for g in range(len(groups))]
            message = refs[-1]
            for g, group in enumerate(groups):
                own, _, rows_high, rows_low, side_high, side_low, begun = got[g]
                for n, c in enumerate(group):
                    total = own[n * count + order[c, count - 1]] + begun[n]
                    for p in range(count):
                        s = side_at(c, order[c, p], arrived, [x[1] for x in got])
                        total = total + dot_split((side_high[n, p], side_low[n, p]), s)
                        if p + 1 < count:
                            row = last_row(rows_high, rows_low, n, p + 1)
                            total = total + dot_split(row, split(own[n * count + order[c, p]]))
                    message[c] = total

        ins = [order, arrived]
        for state in states:
            ins += [state.own, state.traces, state.high, state.low]
            ins += [state.side_high, state.side_low, state.begun]
        return run(body, "second_sides", ins, [VMEM((cols, face, tracers), F32)], [])[0]

    def settle(after, arrived, offsets):
        per_group = 8 + len(offsets)

        def body(order, inlet, _, arrived, inv, *refs):
            offs, refs = refs[: len(offsets)], refs[len(offsets) :]
            got = [refs[per_group * g : per_group * g + per_group] for g in range(len(groups))]
            outs = refs[per_group * len(groups) :]
            scratch = outs[2 * len(groups) :]
            for g, group in enumerate(groups):
                source_high, source_low, maps, rows_high, rows_low, own, traces, tails, *mapped = got[g]
                base, within = outs[2 * g : 2 * g + 2]
                ends, high, low = scratch[3 * g : 3 * g + 3]
                for n, c in enumerate(group):
                    for p in range(count):
                        i = n * count + order[c, p]
                        s = side_at(c, order[c, p], arrived, [x[6] for x in got])
                        ends[n * count + p] = own[i] + side_of(tails, i, s)
                    old = [r[n, pl.ds(face, packed)] for r in mapped]
                    start = entering(known_inflow(inlet[c]), [r[c] for r in offs], old)
                    within[n] = within_of(n, start, ends, rows_high, rows_low, high, low)
                for i in range(len(group) * count):
                    whole = times(inv[at(group, i)], source_high, source_low, i)
                    s = side_at(group[0] + i // count, i % count, arrived, [x[6] for x in got])
                    base[i] = whole + dot(maps[i][:, 2 * face :], side_rows(s))

        ins = [order, inlet, after, arrived, inv_near, *offsets]
        outs, scratch = [], []
        for group, state in zip(groups, states):
            ins += [state.source_high, state.source_low, state.maps, state.high, state.low]
            ins += [state.own, state.traces, state.tails, *state.received[:-1]]
            outs.append(VMEM((len(group) * count, nodes, tracers), F32))
            outs.append(VMEM((len(group), wide, tracers), F32))
            scratch.append(VMEM((len(group) * count, face, tracers), F32))
            scratch += [VMEM((len(group), wide, tracers), BF16)] * 2
        values = run(body, "settle", ins, outs, scratch)
        for g, state in enumerate(states):
            state.base, state.within = values[2 * g : 2 * g + 2]

    def result(offsets):
        def body(order, *refs):
            offs, refs = refs[: len(offsets)], refs[len(offsets) :]
            got = [refs[5 * g : 5 * g + 5] for g in range(len(groups))]
            out, staged, sems, *stacks = refs[5 * len(groups) :]
            for g, group in enumerate(groups):
                within, reach_high, reach_low = got[g][:3]
                for n, c in enumerate(group):
                    inflow = within[n]
                    for r in offs:
                        late_part = split(jnp.where(bit(stages - 1), r[c], 0.0))
                        inflow = inflow + dot_split((reach_high[n], reach_low[n]), late_part)
                    put_inflow(n, c, inflow, order, stacks[g])
            started = []
            for g, group in enumerate(groups):
                base, maps = got[g][3:]
                for i in range(len(group) * count):
                    k = len(started)
                    staged[k] = (base[i] + dot(maps[i][:, : 3 * face], stacks[g][i])).astype(BF16)
                    started.append(pltpu.make_async_copy(staged.at[k], out.at[at(group, i)], sems.at[k]))
                    started[-1].start()
            for copy in started:
                copy.wait()

        ins = [order, *offsets]
        scratch = [VMEM((cols * count, nodes, tracers), BF16), pltpu.SemaphoreType.DMA((cols * count,))]
        for group, state in zip(groups, states):
            ins += [state.within, *state.reach, state.base, state.maps]
            scratch.append(VMEM((len(group) * count, 3 * face, tracers), BF16))
        return run(body, "result", ins, [HBM(previous.shape, BF16)], scratch)[0]

    def exchange_first(state, beside):
        state.sent, state.received = [state.message], []
        for stage in range(stages):
            if stage:
                state.sent.append(combine_first(stage - 1, state.sent[-1], state.received[-1], after))
            state.received.append(swap(state.sent[-1], stage))
            if not stage:
                after = beside()

    (trace, order, rate, aff, inlet), one = load()
    order = (order, SMEM)
    arrived = to_next(trace)
    begin_early(one)
    exchange_first(one, lambda: early_maps(one, one.message))
    prepare(early, one, one.near, one.sent[-1])
    maps = late_maps(one.sent[-1])
    trace = enter_first(early, one, maps)
    arrived_next = to_next(trace)
    two = begin_late(trace)
    two.maps = maps
    states = [one, two]
    first_sides(two, arrived)
    exchange_first(two, lambda: second(early, one, two.message))
    prepare(late, two, arrived, two.sent[-1])
    fold_sides(two.sent[-1])
    enter_first(late, two, None)
    second(late, two, two.sent[-1])
    message, offsets = second_sides(arrived_next), []
    for stage in range(stages):
        offsets.append(swap(message, stage))
        if stage + 1 < stages:
            sent, received = [s.sent[stage] for s in states], [s.received[stage] for s in states]
            message = combine_second(stage, message, offsets[-1], sent, received)
    settle(message, arrived_next, offsets[:-1])
    return result(offsets[-1:])


def solution(mesh):
    placed = (
        P("lat", "stream", None, None, None),
        P("lat", "stream", None, None, None),
        P("lat", "stream", None, None, None),
        P("lat", None, None),
        P("lat", "stream", None, None, None),
        P(),
        P(),
        P("lat", "stream", None),
    )
    return jax.shard_map(
        per_device,
        mesh=mesh,
        in_specs=placed,
        out_specs=P("lat", "stream", None, None, None),
        check_vma=False,
    )
```

```python
from types import SimpleNamespace

import jax
import jax.numpy as jnp
from jax import lax
from jax.experimental import pallas as pl
from jax.experimental.pallas import tpu as pltpu
from jax.sharding import PartitionSpec as P

NODES_1D = 8
F32 = jnp.float32
BF16 = jnp.bfloat16
MIB = 1 << 20
VMEM = pltpu.VMEM
HBM = pltpu.HBM
SMEM = pltpu.SMEM


def run(body, name, ins, outs, scratch):
    pairs = [a if isinstance(a, tuple) else (a, VMEM) for a in ins]
    return pl.pallas_call(
        body,
        name=name,
        in_specs=[pl.BlockSpec(memory_space=space) for _, space in pairs],
        out_specs=[pl.BlockSpec(memory_space=o.memory_space) for o in outs],
        out_shape=outs,
        scratch_shapes=scratch,
        cost_estimate=pl.CostEstimate(flops=0, bytes_accessed=0, transcendentals=0),
        compiler_params=pltpu.CompilerParams(vmem_limit_bytes=24 * MIB),
    )(*[a if space is VMEM else pltpu.with_memory_space_constraint(a, space) for a, space in pairs])


def split(x):
    high = x.astype(BF16)
    return high, (x - high.astype(F32)).astype(BF16)


def dot(x, y):
    return jnp.dot(x, y, preferred_element_type=F32)


def dot_split(x, y):
    return dot(x[0], y[0]) + (dot(x[0], y[1]) + dot(x[1], y[0]))


def langmuir(lagged, rate, affinity):
    return rate * lagged * pltpu.reciprocal(1.0 + affinity * jnp.abs(lagged), approx=True)


def lateral_rows(field, per_side):
    plane = per_side * per_side
    return jnp.concatenate(
        [field[a * plane + plane - per_side : (a + 1) * plane] for a in range(per_side)], axis=0
    )


def pack_map(mapping, lanes):
    face = mapping.shape[0]
    rows = face * face // lanes
    return jnp.concatenate([mapping[q * rows : (q + 1) * rows] for q in range(lanes // face)], axis=1)


def unpack_map(packed, face):
    return jnp.concatenate(
        [packed[:, q * face : (q + 1) * face] for q in range(packed.shape[1] // face)], axis=0
    )


def stack_maps(both):
    face = both.shape[1] // 2
    turned = pltpu.roll(both, face, 1)
    first = lax.broadcasted_iota(jnp.int32, both.shape, 1) < face
    low = split(both)[1]
    return jnp.concatenate(
        [jnp.where(first, both, turned).astype(BF16), low, jnp.where(first, turned, both).astype(BF16)], axis=1
    )


def stack_inflow(f):
    return (f[0], f[1], f[0])


def stack_side(s):
    return (s[0], s[0], s[1])


def in_pairs(items, per, step):
    def turn(t, _):
        step([t * per + k for k in range(per)])
        return 0

    lax.fori_loop(0, items // per, turn, 0)


def known_inflow(inlet):
    return jnp.where(lax.axis_index("stream") == 0, inlet, 0.0)


def bit(stage):
    return ((lax.axis_index("stream") >> stage) & 1) == 1


def per_device(inverse, upwind, lateral, inlet_trace, previous, uptake_rate, affinity, flow_order):
    cols, _, count, nodes, _ = inverse.shape
    face = upwind.shape[3]
    tracers = previous.shape[-1]
    per_side = NODES_1D
    plane = per_side * per_side
    wide = count * face
    packed = face * face // tracers
    sent_rows = face + (packed if lax.axis_size("stream") > 2 else 0)
    streams, lats = lax.axis_size("stream"), lax.axis_size("lat")
    stages = streams.bit_length() - 1
    assert streams == 1 << stages
    assert cols > 1
    early, late = list(range(1, cols)), [0]
    groups = [early, late]
    home = {c: (g, n) for g, group in enumerate(groups) for n, c in enumerate(group)}
    ending = pl.ds(nodes - face, face)
    per = 2 if count % 2 == 0 else 1

    def to_next(value):
        return lax.ppermute(value, "lat", [(i, (i + 1) % lats) for i in range(lats)])

    def swap(value, stage):
        return lax.ppermute(value, "stream", [(i, i ^ (1 << stage)) for i in range(streams)])

    inv_near, up_near, side_near, old_near = (
        pltpu.with_memory_space_constraint(a, VMEM) for a in (inverse, upwind, lateral, previous)
    )
    shaped = previous.reshape(cols, count, per_side, plane, tracers)

    def map_outs(size):
        return [VMEM((size * count, nodes, 6 * face), BF16), VMEM((size * count, face, 6 * face), BF16)]

    def chain_outs(size):
        return [
            VMEM((size * count, face, 2 * face), F32),
            VMEM((size, wide + face, wide), BF16),
            VMEM((size, wide + face, wide), BF16),
        ]

    def offset_scratch(size):
        return [VMEM((size, wide, tracers), BF16)] * 2

    def source_outs(size):
        return [VMEM((size * count, nodes, tracers), BF16)] * 2

    def times(matrix, high, low, i):
        return dot(matrix, high[i]) + dot(matrix, low[i])

    def face_maps(matrix, up, side):
        faces = jnp.concatenate([up, side], axis=0)
        return lax.dot_general(matrix, faces, (((1,), (1,)), ((), ())), preferred_element_type=F32)

    def at(group, i):
        return group[0] + i // count, 0, i % count

    def side_of(tails, i, s):
        return dot_split(split(tails[i][:, face:]), s)

    def link(n, p, step, rows_high, rows_low, row):
        row_id = lax.broadcasted_iota(jnp.int32, (face, wide), 0)
        lane_id = lax.broadcasted_iota(jnp.int32, (face, wide), 1)
        unit = jnp.where(lane_id == row_id + p * face, 1.0, 0.0)
        r = split(jnp.where(p == 0, 0.0, row[n]) + unit)
        here = pl.ds(pl.multiple_of(p * face, face), face)
        rows_high[n, here] = r[0]
        rows_low[n, here] = r[1]
        r = split(dot_split(step, r))
        rows_high[n, pl.ds(wide, face)] = r[0]
        rows_low[n, pl.ds(wide, face)] = r[1]
        row[n] = r[0].astype(F32) + r[1].astype(F32)

    def offset(n, start, rows_high, rows_low, ends, high, low):
        for p in range(count):
            e = split(start if p == 0 else ends[n * count + p - 1])
            high[n, pl.ds(p * face, face)] = e[0]
            low[n, pl.ds(p * face, face)] = e[1]
        last = pl.ds(wide, face)
        return ends[n * count + count - 1] + dot_split((rows_high[n, last], rows_low[n, last]), (high[n], low[n]))

    def load():
        size = len(early)
        items = size * count

        def body(
            order, rate, aff, inlet, old, inverse, upwind, lateral, previous,
            trace, o_order, o_rate, o_aff, o_inlet, near, o_tail, faces, source_high, source_low,
            lagged, staged, lead_sems, sems,
        ):
            rows = pl.ds(plane - 2 * per_side, 2 * per_side)
            lead = [
                pltpu.make_async_copy(a, b, lead_sems.at[k])
                for k, (a, b) in enumerate((
                    (rate, o_rate),
                    (aff, o_aff),
                    (order, o_order),
                    (old.at[0, :, :, rows], staged),
                    (inlet, o_inlet),
                ))
            ]
            whole = pl.ds(0, count)
            fields, others = [], []
            for n, c in enumerate(early):
                for h in range(0, count, per):
                    here, there = pl.ds(h, per), pl.ds(n * count + h, per)
                    fields.append((previous.at[c, 0, here], lagged.at[there]))
                there = pl.ds(n * count, count)
                others += [
                    (inverse.at[c, 0, whole, ending], o_tail.at[there]),
                    (upwind.at[c, 0], faces.at[there, pl.ds(0, face)]),
                    (lateral.at[c, 0], faces.at[there, pl.ds(face, face)]),
                ]
            copies = [pltpu.make_async_copy(a, b, sems.at[k]) for k, (a, b) in enumerate(fields + others)]
            for one in lead[:3] + copies[: len(fields)] + lead[3:4] + copies[len(fields) :] + lead[4:]:
                one.start()
            for one in lead[:3]:
                one.wait()

            def old_rows(field):
                return jnp.concatenate([field(a).astype(F32)[per_side:] for a in range(per_side)], axis=0)

            for k in range(len(fields)):
                copies[k].wait()
                for i in range(k * per, k * per + per):
                    lag = lagged[i].astype(F32)
                    source_high[i], source_low[i] = split(langmuir(lag, o_rate[...], o_aff[...]))
                    c = early[i // count]
                    if c == cols - 1:
                        trace[i % count] = lateral_rows(lag, per_side)
                    else:
                        near[i + count] = lateral_rows(lag, per_side)
            for one in lead[3:]:
                one.wait()
            for j in range(count):
                near[j] = old_rows(lambda a: staged[j, a])
            for one in copies[len(fields) :]:
                one.wait()

        values = run(
            body,
            "load",
            [
                (flow_order.reshape(cols, count), HBM),
                (uptake_rate.reshape(1, tracers), HBM),
                (affinity.reshape(1, tracers), HBM),
                (inlet_trace, HBM),
                (shaped, HBM),
                (inverse, HBM),
                (upwind, HBM),
                (lateral, HBM),
                (previous, HBM),
            ],
            [
                VMEM((count, face, tracers), F32),
                SMEM((cols, count), jnp.int32),
                VMEM((1, tracers), F32),
                VMEM((1, tracers), F32),
                VMEM((cols, face, tracers), F32),
                VMEM((items, face, tracers), F32),
                VMEM((items, face, nodes), BF16),
                VMEM((items, 2 * face, nodes), BF16),
                *source_outs(size),
            ],
            [
                VMEM((items, nodes, tracers), BF16),
                VMEM((count, per_side, 2 * per_side, tracers), BF16),
                pltpu.SemaphoreType.DMA((5,)),
                pltpu.SemaphoreType.DMA((size * (count // per + 3),)),
            ],
        )
        state = SimpleNamespace()
        state.near, state.tail, state.faces, state.source_high, state.source_low = values[5:]
        return values[:5], state

    def begin_early(state):
        size = len(early)
        items = size * count

        def body(
            order, inlet, near, tail, faces, source_high, source_low, tails, ends, message, own
        ):
            for i in range(items):
                tails[i] = face_maps(tail[i], faces[i, :face], faces[i, face:])
                own[i] = times(tail[i], source_high, source_low, i)
            for n, c in enumerate(early):
                links = []
                for p in range(count):
                    i = n * count + order[c, p]
                    end = own[i] + side_of(tails, i, split(near[i]))
                    ends[n * count + p] = end
                    if p == 0:
                        begun = split(known_inflow(inlet[c]))
                        end = end + dot_split(split(tails[i][:, :face]), begun)
                    links.append((tails[i][:, :face], end))
                while len(links) > 1:
                    paired = []
                    for (low, start), (up, end) in zip(links[::2], links[1::2]):
                        u = split(up)
                        paired.append((dot_split(u, split(low)), end + dot_split(u, split(start))))
                    links = paired + links[2 * len(paired) :]
                message[n, pl.ds(0, face)] = links[0][1]
                if sent_rows > face:
                    message[n, pl.ds(face, packed)] = pack_map(links[0][0], tracers)

        state.tails, state.ends, state.message = run(
            body,
            "begin_early",
            [order, inlet, state.near, state.tail, state.faces, state.source_high, state.source_low],
            [
                VMEM((items, face, 2 * face), F32),
                VMEM((items, face, tracers), F32),
                VMEM((size, sent_rows, tracers), F32),
            ],
            [VMEM((items, face, tracers), F32)],
        )

    def early_maps(state, after):
        size = len(early)

        def body(order, inv, up, side, tails, _, maps, side_maps, rows_high, rows_low, row):
            for i in range(size * count):
                k = at(early, i)
                both = face_maps(inv[k], up[k], side[k])
                maps[i] = stack_maps(both)
                side_maps[i] = stack_maps(lateral_rows(both, per_side))
                n, p = i // count, i % count
                head = tails[n * count + order[early[0] + n, p]][:, :face]
                link(n, p, split(head), rows_high, rows_low, row)

        state.maps, state.side_maps, state.high, state.low = run(
            body,
            "early_maps",
            [order, inv_near, up_near, side_near, state.tails, after],
            map_outs(size) + chain_outs(size)[1:],
            [VMEM((size, face, wide), F32)],
        )
        return state.maps

    def begin_late(after):
        size = len(late)
        items = size * count

        def body(
            order, inv, up, side, previous, rate, aff, _,
            source_high, source_low, own, tails, rows_high, rows_low, mapped, row,
        ):
            for i in range(items):
                k = at(late, i)
                tails[i] = face_maps(inv[*k, ending], up[k], side[k])
            for i in range(items + 1):
                if i < items:
                    lag = previous[at(late, i)].astype(F32)
                    source_high[i], source_low[i] = split(langmuir(lag, rate[...], aff[...]))
                    n, p = i // count, i % count
                    step = split(tails[n * count + order[late[n], p]][:, :face])
                    link(n, p, step, rows_high, rows_low, row)
                if i > 0:
                    own[i - 1] = times(inv[*at(late, i - 1), ending], source_high, source_low, i - 1)
            for n in range(size):
                mapped[n] = pack_map(row[n][:, :face], tracers)

        state = SimpleNamespace()
        values = run(
            body,
            "begin_late",
            [order, inv_near, up_near, side_near, old_near, rate, aff, after],
            source_outs(size)
            + [VMEM((items, face, tracers), F32)]
            + chain_outs(size)
            + [VMEM((size, packed, tracers), F32)],
            [VMEM((size, face, wide), F32)],
        )
        state.source_high, state.source_low, state.own, state.tails, state.high, state.low, state.mapped = values
        return state

    def late_maps(after):
        items = len(late) * count

        def body(inv, up, side, _, maps):
            for i in range(items):
                k = at(late, i)
                maps[i] = stack_maps(face_maps(inv[k], up[k], side[k]))

        return run(body, "late_maps", [inv_near, up_near, side_near, after], map_outs(len(late))[:1], [])[0]

    def arrived_side(arrived, j):
        return split(jnp.where(lax.axis_index("lat") > 0, arrived[j], 0.0))

    def first_sides(state, arrived):
        def body(order, inlet, arrived, own, tails, rows_high, rows_low, mapped, ends, message, high, low):
            for p in range(count):
                j = order[0, p]
                ends[p] = own[j] + side_of(tails, j, arrived_side(arrived, j))
            message[0, pl.ds(0, face)] = offset(0, known_inflow(inlet[0]), rows_high, rows_low, ends, high, low)
            if sent_rows > face:
                message[0, pl.ds(face, packed)] = mapped[0]

        state.ends, state.message = run(
            body,
            "first_sides",
            [order, inlet, arrived, state.own, state.tails, state.high, state.low, state.mapped],
            [VMEM((count, face, tracers), F32), VMEM((1, sent_rows, tracers), F32)],
            offset_scratch(1),
        )

    def combine_first(stage, own, other, after):
        rows = face if stage + 2 == stages else sent_rows

        def body(own, other, _, message):
            upper = bit(stage)
            for n in range(own.shape[0]):
                up = jnp.where(upper, own[n], other[n])
                low = jnp.where(upper, other[n], own[n])
                m = split(unpack_map(up[face:], face))
                message[n, pl.ds(0, face)] = dot_split(m, split(low[:face])) + up[:face]
                if rows > face:
                    mapped = dot_split(m, split(unpack_map(low[face:], face)))
                    message[n, pl.ds(face, packed)] = pack_map(mapped, tracers)

        return run(body, "combine", [own, other, after], [VMEM((own.shape[0], rows, tracers), F32)], [])[0]

    def combine_second(stage, own, other, old_own, old_other):
        def body(own, other, *refs):
            message = refs[-1]
            upper = bit(stage)
            for c in range(cols):
                g, n = home[c]
                mine, theirs = refs[2 * g], refs[2 * g + 1]
                m = jnp.where(upper, mine[n, pl.ds(face, packed)], theirs[n, pl.ds(face, packed)])
                up = jnp.where(upper, own[c], other[c])
                low = jnp.where(upper, other[c], own[c])
                message[c] = dot_split(split(unpack_map(m, face)), split(low)) + up

        ins = [own, other]
        for pair in zip(old_own, old_other):
            ins += pair
        return run(body, "combine", ins, [VMEM(own.shape, F32)], [])[0]

    def entering(start, offsets, maps):
        for stage in reversed(range(len(maps))):
            m = split(unpack_map(maps[stage], face))
            beyond = dot_split(m, split(start)) + offsets[stage]
            start = jnp.where(bit(stage), beyond, start)
        return start

    def lower_maps(maps):
        rows = lax.broadcasted_iota(jnp.int32, (face, face), 0)
        total = jnp.where(rows == lax.broadcasted_iota(jnp.int32, (face, face), 1), 1.0, 0.0)
        for stage in reversed(range(stages - 1)):
            beyond = dot_split(split(unpack_map(maps[stage], face)), split(total))
            total = jnp.where(bit(stage), beyond, total)
        return total

    def within_of(n, start, ends, rows_high, rows_low, high, low):
        for p in range(count):
            e = split(start if p == 0 else ends[n * count + p - 1])
            high[n, pl.ds(p * face, face)] = e[0]
            low[n, pl.ds(p * face, face)] = e[1]
        span = pl.ds(0, wide)
        return dot_split((rows_high[n, span], rows_low[n, span]), (high[n], low[n]))

    def side_rows(s):
        return jnp.concatenate([jnp.zeros((face, tracers), BF16), *stack_side(s)], axis=0)

    def prepare(group, state, sides, after):
        size = len(group)
        lower = state.received[:-1]

        def body(inv, sides, source_high, source_low, maps, ends, rows_high, rows_low, _, *refs):
            mapped, (free, within, reach_high, reach_low, high, low) = refs[: len(lower)], refs[len(lower) :]
            span = pl.ds(0, wide)
            for i in range(size * count):
                s = arrived_side(sides, i) if group[0] == 0 else split(sides[i])
                whole = times(inv[at(group, i)], source_high, source_low, i)
                free[i] = whole + dot(maps[i][:, 2 * face :], side_rows(s))
            for n in range(size):
                old = [r[n, pl.ds(face, packed)] for r in mapped]
                start = entering(jnp.zeros((face, tracers), F32), [r[n, pl.ds(0, face)] for r in mapped], old)
                within[n] = within_of(n, start, ends, rows_high, rows_low, high, low)
                rows = (rows_high[n, span][:, :face], rows_low[n, span][:, :face])
                reach_high[n], reach_low[n] = split(dot_split(rows, split(lower_maps(old))))

        state.free, state.within, *state.reach = run(
            body,
            "prepare",
            [inv_near, sides, state.source_high, state.source_low, state.maps, state.ends, state.high, state.low]
            + [after, *lower],
            [VMEM((size * count, nodes, tracers), F32), VMEM((size, wide, tracers), F32)]
            + [VMEM((size, wide, face), BF16)] * 2,
            [VMEM((size, wide, tracers), BF16)] * 2,
        )

    def enter_first(group, state, after):
        size = len(group)
        last = group[-1] == cols - 1
        newest = state.received[-1:]

        def body(order, inlet, within, reach_high, reach_low, *refs):
            got, refs = refs[: len(newest)], refs[len(newest) :]
            if last:
                (free, side_maps), refs = refs[:2], refs[3:]
            stack = refs[0]
            for n, c in enumerate(group):
                start = known_inflow(inlet[c])
                for r in got:
                    start = jnp.where(bit(stages - 1), r[n], start)
                inflow = within[n] + dot_split((reach_high[n], reach_low[n]), split(start))
                put_inflow(n, c, inflow, order, stack)
            if last:
                for j in range(count):
                    i = (size - 1) * count + j
                    part = dot(side_maps[i][:, : 3 * face], stack[i])
                    refs[1][j] = lateral_rows(free.at[i], per_side) + part

        outs = [VMEM((size * count, 3 * face, tracers), BF16)]
        if last:
            outs.append(VMEM((count, face, tracers), F32))
        ins = [order, inlet, state.within, *state.reach, *newest]
        if last:
            ins += [state.free, state.side_maps, after]
        values = run(body, "enter", ins, outs, [])
        state.stack = values[0]
        return values[1] if last else None

    def put_inflow(n, c, inflow, order, stack):
        for p in range(count):
            i = n * count + order[c, p]
            for q, part in enumerate(stack_inflow(split(inflow[p * face : (p + 1) * face]))):
                stack[i, pl.ds(q * face, face)] = part

    def second(group, state, after):
        items = len(group) * count

        def body(inv, maps, free, stack, rate, aff, _, source_high, source_low, traces, own):
            for i in range(items + 1):
                if i < items:
                    swept = free[i] + dot(maps[i][:, : 3 * face], stack[i])
                    traces[i] = lateral_rows(swept, per_side)
                    source_high[i], source_low[i] = split(langmuir(swept, rate[...], aff[...]))
                if i > 0:
                    own[i - 1] = times(inv[*at(group, i - 1), ending], source_high, source_low, i - 1)

        state.source_high, state.source_low, state.traces, state.own = run(
            body,
            "second",
            [inv_near, state.maps, state.free, state.stack, rate, aff, after],
            source_outs(len(group)) + [VMEM((items, face, tracers), F32)] * 2,
            [],
        )
        return state.own

    def fold_sides(after):
        def body(order, inlet, _, *refs):
            got = [refs[3 * g : 3 * g + 3] for g in range(len(groups))]
            outs = refs[3 * len(groups) :]
            for g, group in enumerate(groups):
                tails, rows_high, rows_low = got[g]
                high, low, begun = outs[3 * g : 3 * g + 3]
                for n, c in enumerate(group):
                    start = split(known_inflow(inlet[c]))
                    begun[n] = dot_split(last_row(rows_high, rows_low, n, 0), start)
                    for p in range(count):
                        folded = split(tails[n * count + order[c, p]][:, face:])
                        if p + 1 < count:
                            folded = split(dot_split(last_row(rows_high, rows_low, n, p + 1), folded))
                        high[n, p] = folded[0]
                        low[n, p] = folded[1]

        ins, outs = [order, inlet, after], []
        for group, state in zip(groups, states):
            ins += [state.tails, state.high, state.low]
            outs += [VMEM((len(group), count, face, face), BF16)] * 2
            outs.append(VMEM((len(group), face, tracers), F32))
        values = run(body, "fold_sides", ins, outs, [])
        for g, state in enumerate(states):
            state.side_high, state.side_low, state.begun = values[3 * g : 3 * g + 3]
        return values[0]

    def last_row(rows_high, rows_low, n, block):
        place = pl.ds(wide, face)
        return tuple(r[n, place][:, block * face : (block + 1) * face] for r in (rows_high, rows_low))

    def side_at(c, j, arrived, traces):
        if c == 0:
            return arrived_side(arrived, j)
        h, m = home[c - 1]
        return split(traces[h][m * count + j])

    def second_sides(arrived):
        def body(order, arrived, *refs):
            got = [refs[7 * g : 7 * g + 7] for g in range(len(groups))]
            message = refs[-1]
            for g, group in enumerate(groups):
                own, _, rows_high, rows_low, side_high, side_low, begun = got[g]
                for n, c in enumerate(group):
                    total = own[n * count + order[c, count - 1]] + begun[n]
                    for p in range(count):
                        s = side_at(c, order[c, p], arrived, [x[1] for x in got])
                        total = total + dot_split((side_high[n, p], side_low[n, p]), s)
                        if p + 1 < count:
                            row = last_row(rows_high, rows_low, n, p + 1)
                            total = total + dot_split(row, split(own[n * count + order[c, p]]))
                    message[c] = total

        ins = [order, arrived]
        for state in states:
            ins += [state.own, state.traces, state.high, state.low]
            ins += [state.side_high, state.side_low, state.begun]
        return run(body, "second_sides", ins, [VMEM((cols, face, tracers), F32)], [])[0]

    def settle(after, arrived, offsets):
        per_group = 8 + len(offsets)

        def body(order, inlet, _, arrived, inv, *refs):
            offs, refs = refs[: len(offsets)], refs[len(offsets) :]
            got = [refs[per_group * g : per_group * g + per_group] for g in range(len(groups))]
            outs = refs[per_group * len(groups) :]
            scratch = outs[2 * len(groups) :]
            for g, group in enumerate(groups):
                source_high, source_low, maps, rows_high, rows_low, own, traces, tails, *mapped = got[g]
                base, within = outs[2 * g : 2 * g + 2]
                ends, high, low = scratch[3 * g : 3 * g + 3]
                for i in range(len(group) * count):
                    whole = times(inv[at(group, i)], source_high, source_low, i)
                    s = side_at(group[0] + i // count, i % count, arrived, [x[6] for x in got])
                    base[i] = whole + dot(maps[i][:, 2 * face :], side_rows(s))
                for n, c in enumerate(group):
                    for p in range(count):
                        i = n * count + order[c, p]
                        s = side_at(c, order[c, p], arrived, [x[6] for x in got])
                        ends[n * count + p] = own[i] + side_of(tails, i, s)
                    old = [r[n, pl.ds(face, packed)] for r in mapped]
                    start = entering(known_inflow(inlet[c]), [r[c] for r in offs], old)
                    within[n] = within_of(n, start, ends, rows_high, rows_low, high, low)

        ins = [order, inlet, after, arrived, inv_near, *offsets]
        outs, scratch = [], []
        for group, state in zip(groups, states):
            ins += [state.source_high, state.source_low, state.maps, state.high, state.low]
            ins += [state.own, state.traces, state.tails, *state.received[:-1]]
            outs.append(VMEM((len(group) * count, nodes, tracers), F32))
            outs.append(VMEM((len(group), wide, tracers), F32))
            scratch.append(VMEM((len(group) * count, face, tracers), F32))
            scratch += [VMEM((len(group), wide, tracers), BF16)] * 2
        values = run(body, "settle", ins, outs, scratch)
        for g, state in enumerate(states):
            state.base, state.within = values[2 * g : 2 * g + 2]

    def result(offsets):
        def body(order, *refs):
            offs, refs = refs[: len(offsets)], refs[len(offsets) :]
            got = [refs[5 * g : 5 * g + 5] for g in range(len(groups))]
            out, staged, sems, *stacks = refs[5 * len(groups) :]
            for g, group in enumerate(groups):
                within, reach_high, reach_low = got[g][:3]
                for n, c in enumerate(group):
                    inflow = within[n]
                    for r in offs:
                        late_part = split(jnp.where(bit(stages - 1), r[c], 0.0))
                        inflow = inflow + dot_split((reach_high[n], reach_low[n]), late_part)
                    put_inflow(n, c, inflow, order, stacks[g])
            started = []
            for g, group in enumerate(groups):
                base, maps = got[g][3:]
                for i in range(len(group) * count):
                    k = len(started)
                    staged[k] = (base[i] + dot(maps[i][:, : 3 * face], stacks[g][i])).astype(BF16)
                    started.append(pltpu.make_async_copy(staged.at[k], out.at[at(group, i)], sems.at[k]))
                    started[-1].start()
            for copy in started:
                copy.wait()

        ins = [order, *offsets]
        scratch = [VMEM((cols * count, nodes, tracers), BF16), pltpu.SemaphoreType.DMA((cols * count,))]
        for group, state in zip(groups, states):
            ins += [state.within, *state.reach, state.base, state.maps]
            scratch.append(VMEM((len(group) * count, 3 * face, tracers), BF16))
        return run(body, "result", ins, [HBM(previous.shape, BF16)], scratch)[0]

    def exchange_first(state, beside):
        state.sent, state.received = [state.message], []
        for stage in range(stages):
            if stage:
                state.sent.append(combine_first(stage - 1, state.sent[-1], state.received[-1], after))
            state.received.append(swap(state.sent[-1], stage))
            if not stage:
                after = beside()

    (trace, order, rate, aff, inlet), one = load()
    order = (order, SMEM)
    arrived = to_next(trace)
    begin_early(one)
    exchange_first(one, lambda: early_maps(one, one.message))
    prepare(early, one, one.near, one.sent[-1])
    maps = late_maps(one.sent[-1])
    trace = enter_first(early, one, maps)
    arrived_next = to_next(trace)
    two = begin_late(trace)
    two.maps = maps
    states = [one, two]
    first_sides(two, arrived)
    exchange_first(two, lambda: second(early, one, two.message))
    prepare(late, two, arrived, two.sent[-1])
    fold_sides(two.sent[-1])
    enter_first(late, two, None)
    second(late, two, two.sent[-1])
    message, offsets = second_sides(arrived_next), []
    for stage in range(stages):
        offsets.append(swap(message, stage))
        if stage + 1 < stages:
            sent, received = [s.sent[stage] for s in states], [s.received[stage] for s in states]
            message = combine_second(stage, message, offsets[-1], sent, received)
    settle(message, arrived_next, offsets[:-1])
    return result(offsets[-1:])


def solution(mesh):
    placed = (
        P("lat", "stream", None, None, None),
        P("lat", "stream", None, None, None),
        P("lat", "stream", None, None, None),
        P("lat", None, None),
        P("lat", "stream", None, None, None),
        P(),
        P(),
        P("lat", "stream", None),
    )
    return jax.shard_map(
        per_device,
        mesh=mesh,
        in_specs=placed,
        out_specs=P("lat", "stream", None, None, None),
        check_vma=False,
    )
```

```python
from types import SimpleNamespace

import jax
import jax.numpy as jnp
from jax import lax
from jax.experimental import pallas as pl
from jax.experimental.pallas import tpu as pltpu
from jax.sharding import PartitionSpec as P

NODES_1D = 8
F32 = jnp.float32
BF16 = jnp.bfloat16
MIB = 1 << 20
VMEM = pltpu.VMEM
HBM = pltpu.HBM
SMEM = pltpu.SMEM


def run(body, name, ins, outs, scratch, work=0):
    pairs = [a if isinstance(a, tuple) else (a, VMEM) for a in ins]
    return pl.pallas_call(
        body,
        name=name,
        in_specs=[pl.BlockSpec(memory_space=space) for _, space in pairs],
        out_specs=[pl.BlockSpec(memory_space=o.memory_space) for o in outs],
        out_shape=outs,
        scratch_shapes=scratch,
        cost_estimate=pl.CostEstimate(flops=work, bytes_accessed=0, transcendentals=0),
        compiler_params=pltpu.CompilerParams(vmem_limit_bytes=24 * MIB),
    )(*[a if space is VMEM else pltpu.with_memory_space_constraint(a, space) for a, space in pairs])


def split(x):
    high = x.astype(BF16)
    return high, (x - high.astype(F32)).astype(BF16)


def dot(x, y):
    return jnp.dot(x, y, preferred_element_type=F32)


def dot_split(x, y):
    return dot(x[0], y[0]) + (dot(x[0], y[1]) + dot(x[1], y[0]))


def langmuir(lagged, rate, affinity):
    return rate * lagged * pltpu.reciprocal(1.0 + affinity * jnp.abs(lagged), approx=True)


def lateral_rows(field, per_side):
    plane = per_side * per_side
    return jnp.concatenate(
        [field[a * plane + plane - per_side : (a + 1) * plane] for a in range(per_side)], axis=0
    )


def pack_map(mapping, lanes):
    face = mapping.shape[0]
    rows = face * face // lanes
    return jnp.concatenate([mapping[q * rows : (q + 1) * rows] for q in range(lanes // face)], axis=1)


def unpack_map(packed, face):
    return jnp.concatenate(
        [packed[:, q * face : (q + 1) * face] for q in range(packed.shape[1] // face)], axis=0
    )


def stack_maps(both):
    face = both.shape[1] // 2
    turned = pltpu.roll(both, face, 1)
    first = lax.broadcasted_iota(jnp.int32, both.shape, 1) < face
    low = split(both)[1]
    return jnp.concatenate(
        [jnp.where(first, both, turned).astype(BF16), low, jnp.where(first, turned, both).astype(BF16)], axis=1
    )


def stack_inflow(f):
    return (f[0], f[1], f[0])


def stack_side(s):
    return (s[0], s[0], s[1])


def in_pairs(items, per, step):
    def turn(t, _):
        step([t * per + k for k in range(per)])
        return 0

    lax.fori_loop(0, items // per, turn, 0)


def known_inflow(inlet):
    return jnp.where(lax.axis_index("stream") == 0, inlet, 0.0)


def bit(stage):
    return ((lax.axis_index("stream") >> stage) & 1) == 1


def per_device(inverse, upwind, lateral, inlet_trace, previous, uptake_rate, affinity, flow_order):
    cols, _, count, nodes, _ = inverse.shape
    face = upwind.shape[3]
    tracers = previous.shape[-1]
    per_side = NODES_1D
    plane = per_side * per_side
    wide = count * face
    packed = face * face // tracers
    sent_rows = face + (packed if lax.axis_size("stream") > 2 else 0)
    streams, lats = lax.axis_size("stream"), lax.axis_size("lat")
    stages = streams.bit_length() - 1
    assert streams == 1 << stages
    assert cols > 1
    early, late = list(range(1, cols)), [0]
    groups = [early, late]
    home = {c: (g, n) for g, group in enumerate(groups) for n, c in enumerate(group)}
    ending = pl.ds(nodes - face, face)
    per = 2 if count % 2 == 0 else 1

    def to_next(value):
        return lax.ppermute(value, "lat", [(i, (i + 1) % lats) for i in range(lats)])

    def swap(value, stage):
        return lax.ppermute(value, "stream", [(i, i ^ (1 << stage)) for i in range(streams)])

    inv_near, up_near, side_near, old_near = (
        pltpu.with_memory_space_constraint(a, VMEM) for a in (inverse, upwind, lateral, previous)
    )
    shaped = previous.reshape(cols, count, per_side, plane, tracers)

    def map_outs(size):
        return [VMEM((size * count, nodes, 6 * face), BF16), VMEM((size * count, face, 6 * face), BF16)]

    def chain_outs(size):
        return [
            VMEM((size * count, face, 2 * face), F32),
            VMEM((size, wide + face, wide), BF16),
            VMEM((size, wide + face, wide), BF16),
        ]

    def offset_scratch(size):
        return [VMEM((size, wide, tracers), BF16)] * 2

    def source_outs(size):
        return [VMEM((size * count, nodes, tracers), BF16)] * 2

    def times(matrix, high, low, i):
        return dot(matrix, high[i]) + dot(matrix, low[i])

    def face_maps(matrix, up, side):
        faces = jnp.concatenate([up, side], axis=0)
        return lax.dot_general(matrix, faces, (((1,), (1,)), ((), ())), preferred_element_type=F32)

    def at(group, i):
        return group[0] + i // count, 0, i % count

    def side_of(tails, i, s):
        return dot_split(split(tails[i][:, face:]), s)

    def link(n, p, step, rows_high, rows_low, row):
        row_id = lax.broadcasted_iota(jnp.int32, (face, wide), 0)
        lane_id = lax.broadcasted_iota(jnp.int32, (face, wide), 1)
        unit = jnp.where(lane_id == row_id + p * face, 1.0, 0.0)
        r = split(jnp.where(p == 0, 0.0, row[n]) + unit)
        here = pl.ds(pl.multiple_of(p * face, face), face)
        rows_high[n, here] = r[0]
        rows_low[n, here] = r[1]
        r = split(dot_split(step, r))
        rows_high[n, pl.ds(wide, face)] = r[0]
        rows_low[n, pl.ds(wide, face)] = r[1]
        row[n] = r[0].astype(F32) + r[1].astype(F32)

    def offset(n, start, rows_high, rows_low, ends, high, low):
        for p in range(count):
            e = split(start if p == 0 else ends[n * count + p - 1])
            high[n, pl.ds(p * face, face)] = e[0]
            low[n, pl.ds(p * face, face)] = e[1]
        last = pl.ds(wide, face)
        return ends[n * count + count - 1] + dot_split((rows_high[n, last], rows_low[n, last]), (high[n], low[n]))

    def load():
        size = len(early)
        items = size * count

        def body(
            order, rate, aff, inlet, old, inverse, previous,
            o_order, o_rate, o_aff, o_inlet, near, o_tail, source_high, source_low, lagged,
            staged, lead_sems, sems,
        ):
            rows = pl.ds(plane - 2 * per_side, 2 * per_side)
            lead = [
                pltpu.make_async_copy(a, b, lead_sems.at[k])
                for k, (a, b) in enumerate((
                    (rate, o_rate),
                    (aff, o_aff),
                    (order, o_order),
                    (old.at[0, :, :, rows], staged),
                    (inlet, o_inlet),
                ))
            ]
            whole = pl.ds(0, count)
            fields, others = [], []
            for n, c in enumerate(early):
                for h in range(count):
                    here, there = pl.ds(h, 1), pl.ds(n * count + h, 1)
                    fields.append((previous.at[c, 0, here], lagged.at[there]))
                there = pl.ds(n * count, count)
                others.append((inverse.at[c, 0, whole, ending], o_tail.at[there]))
            copies = [pltpu.make_async_copy(a, b, sems.at[k]) for k, (a, b) in enumerate(fields + others)]
            for one in lead[:3] + copies[: len(fields)] + lead[3:4] + copies[len(fields) :] + lead[4:]:
                one.start()
            for one in lead[:3]:
                one.wait()

            def old_rows(field):
                return jnp.concatenate([field(a).astype(F32)[per_side:] for a in range(per_side)], axis=0)

            for k in range(len(fields)):
                copies[k].wait()
                for i in range(k, k + 1):
                    lag = lagged[i].astype(F32)
                    source_high[i], source_low[i] = split(langmuir(lag, o_rate[...], o_aff[...]))
                    if early[i // count] < cols - 1:
                        near[i + count] = lateral_rows(lag, per_side)
            for one in lead[3:]:
                one.wait()
            for j in range(count):
                near[j] = old_rows(lambda a: staged[j, a])
            for one in copies[len(fields) :]:
                one.wait()

        values = run(
            body,
            "load",
            [
                (flow_order.reshape(cols, count), HBM),
                (uptake_rate.reshape(1, tracers), HBM),
                (affinity.reshape(1, tracers), HBM),
                (inlet_trace, HBM),
                (shaped, HBM),
                (inverse, HBM),
                (previous, HBM),
            ],
            [
                SMEM((cols, count), jnp.int32),
                VMEM((1, tracers), F32),
                VMEM((1, tracers), F32),
                VMEM((cols, face, tracers), F32),
                VMEM((items, face, tracers), F32),
                VMEM((items, face, nodes), BF16),
                *source_outs(size),
                VMEM((items, nodes, tracers), BF16),
            ],
            [
                VMEM((count, per_side, 2 * per_side, tracers), BF16),
                pltpu.SemaphoreType.DMA((5,)),
                pltpu.SemaphoreType.DMA((size * (count + 1),)),
            ],
        )
        state = SimpleNamespace()
        state.near, state.tail, state.source_high, state.source_low, lagged = values[4:]

        def old_trace(lagged, trace):
            for j in range(count):
                for a in range(per_side):
                    start = a * plane + plane - 2 * per_side
                    rows = lagged[items - count + j, pl.ds(start, 2 * per_side)].astype(F32)
                    trace[j, pl.ds(a * per_side, per_side)] = rows[per_side:]

        trace = run(old_trace, "old_trace", [lagged], [VMEM((count, face, tracers), F32)], [], 3000000000)[0]
        return (trace, *values[:4]), state

    def begin_early(state):
        size = len(early)
        items = size * count

        def body(
            order, inlet, near, tail, up, side, source_high, source_low, tails, ends, message, own
        ):
            for i in range(items):
                tails[i] = face_maps(tail[i], up[at(early, i)], side[at(early, i)])
                own[i] = times(tail[i], source_high, source_low, i)
            for n, c in enumerate(early):
                links = []
                for p in range(count):
                    i = n * count + order[c, p]
                    end = own[i] + side_of(tails, i, split(near[i]))
                    ends[n * count + p] = end
                    if p == 0:
                        begun = split(known_inflow(inlet[c]))
                        end = end + dot_split(split(tails[i][:, :face]), begun)
                    links.append((tails[i][:, :face], end))
                while len(links) > 1:
                    paired = []
                    for (low, start), (up, end) in zip(links[::2], links[1::2]):
                        u = split(up)
                        paired.append((dot_split(u, split(low)), end + dot_split(u, split(start))))
                    links = paired + links[2 * len(paired) :]
                message[n, pl.ds(0, face)] = links[0][1]
                if sent_rows > face:
                    message[n, pl.ds(face, packed)] = pack_map(links[0][0], tracers)

        state.tails, state.ends, state.message = run(
            body,
            "begin_early",
            [order, inlet, state.near, state.tail, up_near, side_near, state.source_high, state.source_low],
            [
                VMEM((items, face, 2 * face), F32),
                VMEM((items, face, tracers), F32),
                VMEM((size, sent_rows, tracers), F32),
            ],
            [VMEM((items, face, tracers), F32)],
        )

    def early_maps(state, after):
        size = len(early)

        def body(order, inv, up, side, tails, _, maps, side_maps, rows_high, rows_low, row):
            for i in range(size * count):
                k = at(early, i)
                both = face_maps(inv[k], up[k], side[k])
                maps[i] = stack_maps(both)
                side_maps[i] = stack_maps(lateral_rows(both, per_side))
                n, p = i // count, i % count
                head = tails[n * count + order[early[0] + n, p]][:, :face]
                link(n, p, split(head), rows_high, rows_low, row)

        state.maps, state.side_maps, state.high, state.low = run(
            body,
            "early_maps",
            [order, inv_near, up_near, side_near, state.tails, after],
            map_outs(size) + chain_outs(size)[1:],
            [VMEM((size, face, wide), F32)],
        )
        return state.maps

    def begin_late(after):
        size = len(late)
        items = size * count

        def body(
            order, inv, up, side, previous, rate, aff, _,
            source_high, source_low, own, tails, rows_high, rows_low, mapped, row,
        ):
            for i in range(items):
                k = at(late, i)
                tails[i] = face_maps(inv[*k, ending], up[k], side[k])
            for i in range(items + 1):
                if i < items:
                    lag = previous[at(late, i)].astype(F32)
                    source_high[i], source_low[i] = split(langmuir(lag, rate[...], aff[...]))
                    n, p = i // count, i % count
                    step = split(tails[n * count + order[late[n], p]][:, :face])
                    link(n, p, step, rows_high, rows_low, row)
                if i > 0:
                    own[i - 1] = times(inv[*at(late, i - 1), ending], source_high, source_low, i - 1)
            for n in range(size):
                mapped[n] = pack_map(row[n][:, :face], tracers)

        state = SimpleNamespace()
        values = run(
            body,
            "begin_late",
            [order, inv_near, up_near, side_near, old_near, rate, aff, after],
            source_outs(size)
            + [VMEM((items, face, tracers), F32)]
            + chain_outs(size)
            + [VMEM((size, packed, tracers), F32)],
            [VMEM((size, face, wide), F32)],
        )
        state.source_high, state.source_low, state.own, state.tails, state.high, state.low, state.mapped = values
        return state

    def late_maps(after):
        items = len(late) * count

        def body(inv, up, side, _, maps):
            for i in range(items):
                k = at(late, i)
                maps[i] = stack_maps(face_maps(inv[k], up[k], side[k]))

        return run(body, "late_maps", [inv_near, up_near, side_near, after], map_outs(len(late))[:1], [])[0]

    def arrived_side(arrived, j):
        return split(jnp.where(lax.axis_index("lat") > 0, arrived[j], 0.0))

    def first_sides(state, arrived):
        def body(order, inlet, arrived, own, tails, rows_high, rows_low, mapped, ends, message, high, low):
            for p in range(count):
                j = order[0, p]
                ends[p] = own[j] + side_of(tails, j, arrived_side(arrived, j))
            message[0, pl.ds(0, face)] = offset(0, known_inflow(inlet[0]), rows_high, rows_low, ends, high, low)
            if sent_rows > face:
                message[0, pl.ds(face, packed)] = mapped[0]

        state.ends, state.message = run(
            body,
            "first_sides",
            [order, inlet, arrived, state.own, state.tails, state.high, state.low, state.mapped],
            [VMEM((count, face, tracers), F32), VMEM((1, sent_rows, tracers), F32)],
            offset_scratch(1),
        )

    def combine_first(stage, own, other, after):
        rows = face if stage + 2 == stages else sent_rows

        def body(own, other, _, message):
            upper = bit(stage)
            for n in range(own.shape[0]):
                up = jnp.where(upper, own[n], other[n])
                low = jnp.where(upper, other[n], own[n])
                m = split(unpack_map(up[face:], face))
                message[n, pl.ds(0, face)] = dot_split(m, split(low[:face])) + up[:face]
                if rows > face:
                    mapped = dot_split(m, split(unpack_map(low[face:], face)))
                    message[n, pl.ds(face, packed)] = pack_map(mapped, tracers)

        return run(body, "combine", [own, other, after], [VMEM((own.shape[0], rows, tracers), F32)], [])[0]

    def combine_second(stage, own, other, old_own, old_other):
        def body(own, other, *refs):
            message = refs[-1]
            upper = bit(stage)
            for c in range(cols):
                g, n = home[c]
                mine, theirs = refs[2 * g], refs[2 * g + 1]
                m = jnp.where(upper, mine[n, pl.ds(face, packed)], theirs[n, pl.ds(face, packed)])
                up = jnp.where(upper, own[c], other[c])
                low = jnp.where(upper, other[c], own[c])
                message[c] = dot_split(split(unpack_map(m, face)), split(low)) + up

        ins = [own, other]
        for pair in zip(old_own, old_other):
            ins += pair
        return run(body, "combine", ins, [VMEM(own.shape, F32)], [])[0]

    def entering(start, offsets, maps):
        for stage in reversed(range(len(maps))):
            m = split(unpack_map(maps[stage], face))
            beyond = dot_split(m, split(start)) + offsets[stage]
            start = jnp.where(bit(stage), beyond, start)
        return start

    def lower_maps(maps):
        rows = lax.broadcasted_iota(jnp.int32, (face, face), 0)
        total = jnp.where(rows == lax.broadcasted_iota(jnp.int32, (face, face), 1), 1.0, 0.0)
        for stage in reversed(range(stages - 1)):
            beyond = dot_split(split(unpack_map(maps[stage], face)), split(total))
            total = jnp.where(bit(stage), beyond, total)
        return total

    def within_of(n, start, ends, rows_high, rows_low, high, low):
        for p in range(count):
            e = split(start if p == 0 else ends[n * count + p - 1])
            high[n, pl.ds(p * face, face)] = e[0]
            low[n, pl.ds(p * face, face)] = e[1]
        span = pl.ds(0, wide)
        return dot_split((rows_high[n, span], rows_low[n, span]), (high[n], low[n]))

    def side_rows(s):
        return jnp.concatenate([jnp.zeros((face, tracers), BF16), *stack_side(s)], axis=0)

    def prepare(group, state, sides, after):
        size = len(group)
        lower = state.received[:-1]

        def body(inv, sides, source_high, source_low, maps, ends, rows_high, rows_low, _, *refs):
            mapped, (free, within, reach_high, reach_low, high, low) = refs[: len(lower)], refs[len(lower) :]
            span = pl.ds(0, wide)
            for i in range(size * count):
                s = arrived_side(sides, i) if group[0] == 0 else split(sides[i])
                whole = times(inv[at(group, i)], source_high, source_low, i)
                free[i] = whole + dot(maps[i][:, 2 * face :], side_rows(s))
            for n in range(size):
                old = [r[n, pl.ds(face, packed)] for r in mapped]
                start = entering(jnp.zeros((face, tracers), F32), [r[n, pl.ds(0, face)] for r in mapped], old)
                within[n] = within_of(n, start, ends, rows_high, rows_low, high, low)
                rows = (rows_high[n, span][:, :face], rows_low[n, span][:, :face])
                reach_high[n], reach_low[n] = split(dot_split(rows, split(lower_maps(old))))

        state.free, state.within, *state.reach = run(
            body,
            "prepare",
            [inv_near, sides, state.source_high, state.source_low, state.maps, state.ends, state.high, state.low]
            + [after, *lower],
            [VMEM((size * count, nodes, tracers), F32), VMEM((size, wide, tracers), F32)]
            + [VMEM((size, wide, face), BF16)] * 2,
            [VMEM((size, wide, tracers), BF16)] * 2,
        )

    def enter_first(group, state, after):
        size = len(group)
        last = group[-1] == cols - 1
        newest = state.received[-1:]

        def body(order, inlet, within, reach_high, reach_low, *refs):
            got, refs = refs[: len(newest)], refs[len(newest) :]
            if last:
                (free, side_maps), refs = refs[:2], refs[3:]
            stack = refs[0]
            for n, c in enumerate(group):
                start = known_inflow(inlet[c])
                for r in got:
                    start = jnp.where(bit(stages - 1), r[n], start)
                inflow = within[n] + dot_split((reach_high[n], reach_low[n]), split(start))
                put_inflow(n, c, inflow, order, stack)
            if last:
                for j in range(count):
                    i = (size - 1) * count + j
                    part = dot(side_maps[i][:, : 3 * face], stack[i])
                    refs[1][j] = lateral_rows(free.at[i], per_side) + part

        outs = [VMEM((size * count, 3 * face, tracers), BF16)]
        if last:
            outs.append(VMEM((count, face, tracers), F32))
        ins = [order, inlet, state.within, *state.reach, *newest]
        if last:
            ins += [state.free, state.side_maps, after]
        values = run(body, "enter", ins, outs, [])
        state.stack = values[0]
        return values[1] if last else None

    def put_inflow(n, c, inflow, order, stack):
        for p in range(count):
            i = n * count + order[c, p]
            for q, part in enumerate(stack_inflow(split(inflow[p * face : (p + 1) * face]))):
                stack[i, pl.ds(q * face, face)] = part

    def second(group, state, after):
        items = len(group) * count

        def body(inv, maps, free, stack, rate, aff, _, source_high, source_low, traces, own):
            for i in range(items + 1):
                if i < items:
                    swept = free[i] + dot(maps[i][:, : 3 * face], stack[i])
                    traces[i] = lateral_rows(swept, per_side)
                    source_high[i], source_low[i] = split(langmuir(swept, rate[...], aff[...]))
                if i > 0:
                    own[i - 1] = times(inv[*at(group, i - 1), ending], source_high, source_low, i - 1)

        state.source_high, state.source_low, state.traces, state.own = run(
            body,
            "second",
            [inv_near, state.maps, state.free, state.stack, rate, aff, after],
            source_outs(len(group)) + [VMEM((items, face, tracers), F32)] * 2,
            [],
        )
        return state.own

    def fold_sides(after):
        def body(order, inlet, _, *refs):
            got = [refs[3 * g : 3 * g + 3] for g in range(len(groups))]
            outs = refs[3 * len(groups) :]
            for g, group in enumerate(groups):
                tails, rows_high, rows_low = got[g]
                high, low, begun = outs[3 * g : 3 * g + 3]
                for n, c in enumerate(group):
                    start = split(known_inflow(inlet[c]))
                    begun[n] = dot_split(last_row(rows_high, rows_low, n, 0), start)
                    for p in range(count):
                        folded = split(tails[n * count + order[c, p]][:, face:])
                        if p + 1 < count:
                            folded = split(dot_split(last_row(rows_high, rows_low, n, p + 1), folded))
                        high[n, p] = folded[0]
                        low[n, p] = folded[1]

        ins, outs = [order, inlet, after], []
        for group, state in zip(groups, states):
            ins += [state.tails, state.high, state.low]
            outs += [VMEM((len(group), count, face, face), BF16)] * 2
            outs.append(VMEM((len(group), face, tracers), F32))
        values = run(body, "fold_sides", ins, outs, [])
        for g, state in enumerate(states):
            state.side_high, state.side_low, state.begun = values[3 * g : 3 * g + 3]
        return values[0]

    def last_row(rows_high, rows_low, n, block):
        place = pl.ds(wide, face)
        return tuple(r[n, place][:, block * face : (block + 1) * face] for r in (rows_high, rows_low))

    def side_at(c, j, arrived, traces):
        if c == 0:
            return arrived_side(arrived, j)
        h, m = home[c - 1]
        return split(traces[h][m * count + j])

    def second_sides(arrived):
        def body(order, arrived, *refs):
            got = [refs[7 * g : 7 * g + 7] for g in range(len(groups))]
            message = refs[-1]
            for g, group in enumerate(groups):
                own, _, rows_high, rows_low, side_high, side_low, begun = got[g]
                for n, c in enumerate(group):
                    total = own[n * count + order[c, count - 1]] + begun[n]
                    for p in range(count):
                        s = side_at(c, order[c, p], arrived, [x[1] for x in got])
                        total = total + dot_split((side_high[n, p], side_low[n, p]), s)
                        if p + 1 < count:
                            row = last_row(rows_high, rows_low, n, p + 1)
                            total = total + dot_split(row, split(own[n * count + order[c, p]]))
                    message[c] = total

        ins = [order, arrived]
        for state in states:
            ins += [state.own, state.traces, state.high, state.low]
            ins += [state.side_high, state.side_low, state.begun]
        return run(body, "second_sides", ins, [VMEM((cols, face, tracers), F32)], [])[0]

    def settle(after, arrived, offsets):
        per_group = 8 + len(offsets)

        def body(order, inlet, _, arrived, inv, *refs):
            offs, refs = refs[: len(offsets)], refs[len(offsets) :]
            got = [refs[per_group * g : per_group * g + per_group] for g in range(len(groups))]
            outs = refs[per_group * len(groups) :]
            scratch = outs[2 * len(groups) :]
            for g, group in enumerate(groups):
                source_high, source_low, maps, rows_high, rows_low, own, traces, tails, *mapped = got[g]
                base, within = outs[2 * g : 2 * g + 2]
                ends, high, low = scratch[3 * g : 3 * g + 3]
                for i in range(len(group) * count):
                    whole = times(inv[at(group, i)], source_high, source_low, i)
                    s = side_at(group[0] + i // count, i % count, arrived, [x[6] for x in got])
                    base[i] = whole + dot(maps[i][:, 2 * face :], side_rows(s))
                for n, c in enumerate(group):
                    for p in range(count):
                        i = n * count + order[c, p]
                        s = side_at(c, order[c, p], arrived, [x[6] for x in got])
                        ends[n * count + p] = own[i] + side_of(tails, i, s)
                    old = [r[n, pl.ds(face, packed)] for r in mapped]
                    start = entering(known_inflow(inlet[c]), [r[c] for r in offs], old)
                    within[n] = within_of(n, start, ends, rows_high, rows_low, high, low)

        ins = [order, inlet, after, arrived, inv_near, *offsets]
        outs, scratch = [], []
        for group, state in zip(groups, states):
            ins += [state.source_high, state.source_low, state.maps, state.high, state.low]
            ins += [state.own, state.traces, state.tails, *state.received[:-1]]
            outs.append(VMEM((len(group) * count, nodes, tracers), F32))
            outs.append(VMEM((len(group), wide, tracers), F32))
            scratch.append(VMEM((len(group) * count, face, tracers), F32))
            scratch += [VMEM((len(group), wide, tracers), BF16)] * 2
        values = run(body, "settle", ins, outs, scratch)
        for g, state in enumerate(states):
            state.base, state.within = values[2 * g : 2 * g + 2]

    def result(offsets):
        def body(order, *refs):
            offs, refs = refs[: len(offsets)], refs[len(offsets) :]
            got = [refs[5 * g : 5 * g + 5] for g in range(len(groups))]
            out, staged, sems, *stacks = refs[5 * len(groups) :]
            for g, group in enumerate(groups):
                within, reach_high, reach_low = got[g][:3]
                for n, c in enumerate(group):
                    inflow = within[n]
                    for r in offs:
                        late_part = split(jnp.where(bit(stages - 1), r[c], 0.0))
                        inflow = inflow + dot_split((reach_high[n], reach_low[n]), late_part)
                    put_inflow(n, c, inflow, order, stacks[g])
            started = []
            for g, group in enumerate(groups):
                base, maps = got[g][3:]
                for i in range(len(group) * count):
                    k = len(started)
                    staged[k] = (base[i] + dot(maps[i][:, : 3 * face], stacks[g][i])).astype(BF16)
                    started.append(pltpu.make_async_copy(staged.at[k], out.at[at(group, i)], sems.at[k]))
                    started[-1].start()
            for copy in started:
                copy.wait()

        ins = [order, *offsets]
        scratch = [VMEM((cols * count, nodes, tracers), BF16), pltpu.SemaphoreType.DMA((cols * count,))]
        for group, state in zip(groups, states):
            ins += [state.within, *state.reach, state.base, state.maps]
            scratch.append(VMEM((len(group) * count, 3 * face, tracers), BF16))
        return run(body, "result", ins, [HBM(previous.shape, BF16)], scratch)[0]

    def exchange_first(state, beside):
        state.sent, state.received = [state.message], []
        for stage in range(stages):
            if stage:
                state.sent.append(combine_first(stage - 1, state.sent[-1], state.received[-1], after))
            state.received.append(swap(state.sent[-1], stage))
            if not stage:
                after = beside()

    (trace, order, rate, aff, inlet), one = load()
    order = (order, SMEM)
    arrived = to_next(trace)
    begin_early(one)
    exchange_first(one, lambda: early_maps(one, one.message))
    prepare(early, one, one.near, one.sent[-1])
    maps = late_maps(one.sent[-1])
    trace = enter_first(early, one, maps)
    arrived_next = to_next(trace)
    two = begin_late(trace)
    two.maps = maps
    states = [one, two]
    first_sides(two, arrived)
    exchange_first(two, lambda: second(early, one, two.message))
    prepare(late, two, arrived, two.sent[-1])
    fold_sides(two.sent[-1])
    enter_first(late, two, None)
    second(late, two, two.sent[-1])
    message, offsets = second_sides(arrived_next), []
    for stage in range(stages):
        offsets.append(swap(message, stage))
        if stage + 1 < stages:
            sent, received = [s.sent[stage] for s in states], [s.received[stage] for s in states]
            message = combine_second(stage, message, offsets[-1], sent, received)
    settle(message, arrived_next, offsets[:-1])
    return result(offsets[-1:])


def solution(mesh):
    placed = (
        P("lat", "stream", None, None, None),
        P("lat", "stream", None, None, None),
        P("lat", "stream", None, None, None),
        P("lat", None, None),
        P("lat", "stream", None, None, None),
        P(),
        P(),
        P("lat", "stream", None),
    )
    return jax.shard_map(
        per_device,
        mesh=mesh,
        in_specs=placed,
        out_specs=P("lat", "stream", None, None, None),
        check_vma=False,
    )
```

```python
from types import SimpleNamespace

import jax
import jax.numpy as jnp
from jax import lax
from jax.experimental import pallas as pl
from jax.experimental.pallas import tpu as pltpu
from jax.sharding import PartitionSpec as P

NODES_1D = 8
F32 = jnp.float32
BF16 = jnp.bfloat16
MIB = 1 << 20
VMEM = pltpu.VMEM
HBM = pltpu.HBM
SMEM = pltpu.SMEM


def run(body, name, ins, outs, scratch, work=0):
    pairs = [a if isinstance(a, tuple) else (a, VMEM) for a in ins]
    return pl.pallas_call(
        body,
        name=name,
        in_specs=[pl.BlockSpec(memory_space=space) for _, space in pairs],
        out_specs=[pl.BlockSpec(memory_space=o.memory_space) for o in outs],
        out_shape=outs,
        scratch_shapes=scratch,
        cost_estimate=pl.CostEstimate(flops=work, bytes_accessed=0, transcendentals=0),
        compiler_params=pltpu.CompilerParams(vmem_limit_bytes=24 * MIB),
    )(*[a if space is VMEM else pltpu.with_memory_space_constraint(a, space) for a, space in pairs])


def split(x):
    high = x.astype(BF16)
    return high, (x - high.astype(F32)).astype(BF16)


def dot(x, y):
    return jnp.dot(x, y, preferred_element_type=F32)


def dot_split(x, y):
    return dot(x[0], y[0]) + (dot(x[0], y[1]) + dot(x[1], y[0]))


def langmuir(lagged, rate, affinity):
    return rate * lagged * pltpu.reciprocal(1.0 + affinity * jnp.abs(lagged), approx=True)


def lateral_rows(field, per_side):
    plane = per_side * per_side
    return jnp.concatenate(
        [field[a * plane + plane - per_side : (a + 1) * plane] for a in range(per_side)], axis=0
    )


def pack_map(mapping, lanes):
    face = mapping.shape[0]
    rows = face * face // lanes
    return jnp.concatenate([mapping[q * rows : (q + 1) * rows] for q in range(lanes // face)], axis=1)


def unpack_map(packed, face):
    return jnp.concatenate(
        [packed[:, q * face : (q + 1) * face] for q in range(packed.shape[1] // face)], axis=0
    )


def stack_maps(both):
    face = both.shape[1] // 2
    turned = pltpu.roll(both, face, 1)
    first = lax.broadcasted_iota(jnp.int32, both.shape, 1) < face
    low = split(both)[1]
    return jnp.concatenate(
        [jnp.where(first, both, turned).astype(BF16), low, jnp.where(first, turned, both).astype(BF16)], axis=1
    )


def stack_inflow(f):
    return (f[0], f[1], f[0])


def stack_side(s):
    return (s[0], s[0], s[1])


def in_pairs(items, per, step):
    def turn(t, _):
        step([t * per + k for k in range(per)])
        return 0

    lax.fori_loop(0, items // per, turn, 0)


def known_inflow(inlet):
    return jnp.where(lax.axis_index("stream") == 0, inlet, 0.0)


def bit(stage):
    return ((lax.axis_index("stream") >> stage) & 1) == 1


def per_device(inverse, upwind, lateral, inlet_trace, previous, uptake_rate, affinity, flow_order):
    cols, _, count, nodes, _ = inverse.shape
    face = upwind.shape[3]
    tracers = previous.shape[-1]
    per_side = NODES_1D
    plane = per_side * per_side
    wide = count * face
    packed = face * face // tracers
    sent_rows = face + (packed if lax.axis_size("stream") > 2 else 0)
    streams, lats = lax.axis_size("stream"), lax.axis_size("lat")
    stages = streams.bit_length() - 1
    assert streams == 1 << stages
    assert cols > 1
    early, late = list(range(1, cols)), [0]
    groups = [early, late]
    home = {c: (g, n) for g, group in enumerate(groups) for n, c in enumerate(group)}
    ending = pl.ds(nodes - face, face)
    per = 2 if count % 2 == 0 else 1

    def to_next(value):
        return lax.ppermute(value, "lat", [(i, (i + 1) % lats) for i in range(lats)])

    def swap(value, stage):
        return lax.ppermute(value, "stream", [(i, i ^ (1 << stage)) for i in range(streams)])

    inv_near, up_near, side_near, old_near = (
        pltpu.with_memory_space_constraint(a, VMEM) for a in (inverse, upwind, lateral, previous)
    )
    shaped = previous.reshape(cols, count, per_side, plane, tracers)

    def map_outs(size):
        return [VMEM((size * count, nodes, 6 * face), BF16), VMEM((size * count, face, 6 * face), BF16)]

    def chain_outs(size):
        return [
            VMEM((size * count, face, 2 * face), F32),
            VMEM((size, wide + face, wide), BF16),
            VMEM((size, wide + face, wide), BF16),
        ]

    def offset_scratch(size):
        return [VMEM((size, wide, tracers), BF16)] * 2

    def source_outs(size):
        return [VMEM((size * count, nodes, tracers), BF16)] * 2

    def times(matrix, high, low, i):
        return dot(matrix, high[i]) + dot(matrix, low[i])

    def face_maps(matrix, up, side):
        faces = jnp.concatenate([up, side], axis=0)
        return lax.dot_general(matrix, faces, (((1,), (1,)), ((), ())), preferred_element_type=F32)

    def at(group, i):
        return group[0] + i // count, 0, i % count

    def side_of(tails, i, s):
        return dot_split(split(tails[i][:, face:]), s)

    def link(n, p, step, rows_high, rows_low, row):
        row_id = lax.broadcasted_iota(jnp.int32, (face, wide), 0)
        lane_id = lax.broadcasted_iota(jnp.int32, (face, wide), 1)
        unit = jnp.where(lane_id == row_id + p * face, 1.0, 0.0)
        r = split(jnp.where(p == 0, 0.0, row[n]) + unit)
        here = pl.ds(pl.multiple_of(p * face, face), face)
        rows_high[n, here] = r[0]
        rows_low[n, here] = r[1]
        r = split(dot_split(step, r))
        rows_high[n, pl.ds(wide, face)] = r[0]
        rows_low[n, pl.ds(wide, face)] = r[1]
        row[n] = r[0].astype(F32) + r[1].astype(F32)

    def offset(n, start, rows_high, rows_low, ends, high, low):
        for p in range(count):
            e = split(start if p == 0 else ends[n * count + p - 1])
            high[n, pl.ds(p * face, face)] = e[0]
            low[n, pl.ds(p * face, face)] = e[1]
        last = pl.ds(wide, face)
        return ends[n * count + count - 1] + dot_split((rows_high[n, last], rows_low[n, last]), (high[n], low[n]))

    def load():
        size = len(early)
        items = size * count

        def body(
            order, rate, aff, inlet, old, inverse, previous,
            o_order, o_rate, o_aff, o_inlet, near, o_tail, source_high, source_low, lagged,
            staged, lead_sems, sems,
        ):
            rows = pl.ds(plane - 2 * per_side, 2 * per_side)
            lead = [
                pltpu.make_async_copy(a, b, lead_sems.at[k])
                for k, (a, b) in enumerate((
                    (rate, o_rate),
                    (aff, o_aff),
                    (order, o_order),
                    (old.at[0, :, :, rows], staged),
                    (inlet, o_inlet),
                ))
            ]
            whole = pl.ds(0, count)
            fields, others = [], []
            for n, c in enumerate(early):
                for h in range(count):
                    here, there = pl.ds(h, 1), pl.ds(n * count + h, 1)
                    fields.append((previous.at[c, 0, here], lagged.at[there]))
                there = pl.ds(n * count, count)
                others.append((inverse.at[c, 0, whole, ending], o_tail.at[there]))
            copies = [pltpu.make_async_copy(a, b, sems.at[k]) for k, (a, b) in enumerate(fields + others)]
            for one in lead[:3] + copies[: len(fields)] + lead[3:4] + copies[len(fields) :] + lead[4:]:
                one.start()
            for one in lead[:3]:
                one.wait()

            def old_rows(field):
                return jnp.concatenate([field(a).astype(F32)[per_side:] for a in range(per_side)], axis=0)

            for k in range(len(fields)):
                copies[k].wait()
                for i in range(k, k + 1):
                    lag = lagged[i].astype(F32)
                    source_high[i], source_low[i] = split(langmuir(lag, o_rate[...], o_aff[...]))
                    if early[i // count] < cols - 1:
                        near[i + count] = lateral_rows(lag, per_side)
            for one in lead[3:]:
                one.wait()
            for j in range(count):
                near[j] = old_rows(lambda a: staged[j, a])
            for one in copies[len(fields) :]:
                one.wait()

        values = run(
            body,
            "load",
            [
                (flow_order.reshape(cols, count), HBM),
                (uptake_rate.reshape(1, tracers), HBM),
                (affinity.reshape(1, tracers), HBM),
                (inlet_trace, HBM),
                (shaped, HBM),
                (inverse, HBM),
                (previous, HBM),
            ],
            [
                SMEM((cols, count), jnp.int32),
                VMEM((1, tracers), F32),
                VMEM((1, tracers), F32),
                VMEM((cols, face, tracers), F32),
                VMEM((items, face, tracers), F32),
                VMEM((items, face, nodes), BF16),
                *source_outs(size),
                VMEM((items, nodes, tracers), BF16),
            ],
            [
                VMEM((count, per_side, 2 * per_side, tracers), BF16),
                pltpu.SemaphoreType.DMA((5,)),
                pltpu.SemaphoreType.DMA((size * (count + 1),)),
            ],
        )
        state = SimpleNamespace()
        state.near, state.tail, state.source_high, state.source_low, lagged = values[4:]

        def old_trace(lagged, trace):
            for j in range(count):
                for a in range(per_side):
                    start = a * plane + plane - 2 * per_side
                    rows = lagged[items - count + j, pl.ds(start, 2 * per_side)].astype(F32)
                    trace[j, pl.ds(a * per_side, per_side)] = rows[per_side:]

        trace = run(old_trace, "old_trace", [lagged], [VMEM((count, face, tracers), F32)], [], 3000000000)[0]
        return (trace, *values[:4]), state

    def begin_early(state):
        size = len(early)
        items = size * count

        def body(
            order, inlet, near, tail, up, side, source_high, source_low, tails, ends, message, own
        ):
            for i in range(items):
                tails[i] = face_maps(tail[i], up[at(early, i)], side[at(early, i)])
            for i in range(items):
                own[i] = times(tail[i], source_high, source_low, i)
            for n, c in enumerate(early):
                links = []
                for p in range(count):
                    i = n * count + order[c, p]
                    end = own[i] + side_of(tails, i, split(near[i]))
                    ends[n * count + p] = end
                    if p == 0:
                        begun = split(known_inflow(inlet[c]))
                        end = end + dot_split(split(tails[i][:, :face]), begun)
                    links.append((tails[i][:, :face], end))
                while len(links) > 1:
                    paired = []
                    for (low, start), (up, end) in zip(links[::2], links[1::2]):
                        u = split(up)
                        paired.append((dot_split(u, split(low)), end + dot_split(u, split(start))))
                    links = paired + links[2 * len(paired) :]
                message[n, pl.ds(0, face)] = links[0][1]
                if sent_rows > face:
                    message[n, pl.ds(face, packed)] = pack_map(links[0][0], tracers)

        state.tails, state.ends, state.message = run(
            body,
            "begin_early",
            [order, inlet, state.near, state.tail, up_near, side_near, state.source_high, state.source_low],
            [
                VMEM((items, face, 2 * face), F32),
                VMEM((items, face, tracers), F32),
                VMEM((size, sent_rows, tracers), F32),
            ],
            [VMEM((items, face, tracers), F32)],
        )

    def early_maps(state, after):
        size = len(early)

        def body(order, inv, up, side, tails, _, maps, side_maps, rows_high, rows_low, row):
            for i in range(size * count):
                k = at(early, i)
                both = face_maps(inv[k], up[k], side[k])
                maps[i] = stack_maps(both)
                side_maps[i] = stack_maps(lateral_rows(both, per_side))
                n, p = i // count, i % count
                head = tails[n * count + order[early[0] + n, p]][:, :face]
                link(n, p, split(head), rows_high, rows_low, row)

        state.maps, state.side_maps, state.high, state.low = run(
            body,
            "early_maps",
            [order, inv_near, up_near, side_near, state.tails, after],
            map_outs(size) + chain_outs(size)[1:],
            [VMEM((size, face, wide), F32)],
        )
        return state.maps

    def begin_late(after):
        size = len(late)
        items = size * count

        def body(
            order, inv, up, side, previous, rate, aff, _,
            source_high, source_low, own, tails, rows_high, rows_low, mapped, row,
        ):
            for i in range(items):
                lag = previous[at(late, i)].astype(F32)
                source_high[i], source_low[i] = split(langmuir(lag, rate[...], aff[...]))
                k = at(late, i)
                tails[i] = face_maps(inv[*k, ending], up[k], side[k])
            for i in range(items):
                own[i] = times(inv[*at(late, i), ending], source_high, source_low, i)
                n, p = i // count, i % count
                step = split(tails[n * count + order[late[n], p]][:, :face])
                link(n, p, step, rows_high, rows_low, row)
            for n in range(size):
                mapped[n] = pack_map(row[n][:, :face], tracers)

        state = SimpleNamespace()
        values = run(
            body,
            "begin_late",
            [order, inv_near, up_near, side_near, old_near, rate, aff, after],
            source_outs(size)
            + [VMEM((items, face, tracers), F32)]
            + chain_outs(size)
            + [VMEM((size, packed, tracers), F32)],
            [VMEM((size, face, wide), F32)],
        )
        state.source_high, state.source_low, state.own, state.tails, state.high, state.low, state.mapped = values
        return state

    def late_maps(after):
        items = len(late) * count

        def body(inv, up, side, _, maps):
            for i in range(items):
                k = at(late, i)
                maps[i] = stack_maps(face_maps(inv[k], up[k], side[k]))

        return run(body, "late_maps", [inv_near, up_near, side_near, after], map_outs(len(late))[:1], [])[0]

    def arrived_side(arrived, j):
        return split(jnp.where(lax.axis_index("lat") > 0, arrived[j], 0.0))

    def first_sides(state, arrived):
        def body(order, inlet, arrived, own, tails, rows_high, rows_low, mapped, ends, message, high, low):
            for p in range(count):
                j = order[0, p]
                ends[p] = own[j] + side_of(tails, j, arrived_side(arrived, j))
            message[0, pl.ds(0, face)] = offset(0, known_inflow(inlet[0]), rows_high, rows_low, ends, high, low)
            if sent_rows > face:
                message[0, pl.ds(face, packed)] = mapped[0]

        state.ends, state.message = run(
            body,
            "first_sides",
            [order, inlet, arrived, state.own, state.tails, state.high, state.low, state.mapped],
            [VMEM((count, face, tracers), F32), VMEM((1, sent_rows, tracers), F32)],
            offset_scratch(1),
        )

    def combine_first(stage, own, other, after):
        rows = face if stage + 2 == stages else sent_rows

        def body(own, other, _, message):
            upper = bit(stage)
            for n in range(own.shape[0]):
                up = jnp.where(upper, own[n], other[n])
                low = jnp.where(upper, other[n], own[n])
                m = split(unpack_map(up[face:], face))
                message[n, pl.ds(0, face)] = dot_split(m, split(low[:face])) + up[:face]
                if rows > face:
                    mapped = dot_split(m, split(unpack_map(low[face:], face)))
                    message[n, pl.ds(face, packed)] = pack_map(mapped, tracers)

        return run(body, "combine", [own, other, after], [VMEM((own.shape[0], rows, tracers), F32)], [])[0]

    def combine_second(stage, own, other, old_own, old_other):
        def body(own, other, *refs):
            message = refs[-1]
            upper = bit(stage)
            for c in range(cols):
                g, n = home[c]
                mine, theirs = refs[2 * g], refs[2 * g + 1]
                m = jnp.where(upper, mine[n, pl.ds(face, packed)], theirs[n, pl.ds(face, packed)])
                up = jnp.where(upper, own[c], other[c])
                low = jnp.where(upper, other[c], own[c])
                message[c] = dot_split(split(unpack_map(m, face)), split(low)) + up

        ins = [own, other]
        for pair in zip(old_own, old_other):
            ins += pair
        return run(body, "combine", ins, [VMEM(own.shape, F32)], [])[0]

    def entering(start, offsets, maps):
        for stage in reversed(range(len(maps))):
            m = split(unpack_map(maps[stage], face))
            beyond = dot_split(m, split(start)) + offsets[stage]
            start = jnp.where(bit(stage), beyond, start)
        return start

    def lower_maps(maps):
        rows = lax.broadcasted_iota(jnp.int32, (face, face), 0)
        total = jnp.where(rows == lax.broadcasted_iota(jnp.int32, (face, face), 1), 1.0, 0.0)
        for stage in reversed(range(stages - 1)):
            beyond = dot_split(split(unpack_map(maps[stage], face)), split(total))
            total = jnp.where(bit(stage), beyond, total)
        return total

    def within_of(n, start, ends, rows_high, rows_low, high, low):
        for p in range(count):
            e = split(start if p == 0 else ends[n * count + p - 1])
            high[n, pl.ds(p * face, face)] = e[0]
            low[n, pl.ds(p * face, face)] = e[1]
        span = pl.ds(0, wide)
        return dot_split((rows_high[n, span], rows_low[n, span]), (high[n], low[n]))

    def side_rows(s):
        return jnp.concatenate([jnp.zeros((face, tracers), BF16), *stack_side(s)], axis=0)

    def prepare(group, state, sides, after):
        size = len(group)
        lower = state.received[:-1]

        def body(inv, sides, source_high, source_low, maps, ends, rows_high, rows_low, _, *refs):
            mapped, (free, within, reach_high, reach_low, high, low) = refs[: len(lower)], refs[len(lower) :]
            span = pl.ds(0, wide)
            for i in range(size * count):
                s = arrived_side(sides, i) if group[0] == 0 else split(sides[i])
                whole = times(inv[at(group, i)], source_high, source_low, i)
                free[i] = whole + dot(maps[i][:, 2 * face :], side_rows(s))
            for n in range(size):
                old = [r[n, pl.ds(face, packed)] for r in mapped]
                start = entering(jnp.zeros((face, tracers), F32), [r[n, pl.ds(0, face)] for r in mapped], old)
                within[n] = within_of(n, start, ends, rows_high, rows_low, high, low)
                rows = (rows_high[n, span][:, :face], rows_low[n, span][:, :face])
                reach_high[n], reach_low[n] = split(dot_split(rows, split(lower_maps(old))))

        state.free, state.within, *state.reach = run(
            body,
            "prepare",
            [inv_near, sides, state.source_high, state.source_low, state.maps, state.ends, state.high, state.low]
            + [after, *lower],
            [VMEM((size * count, nodes, tracers), F32), VMEM((size, wide, tracers), F32)]
            + [VMEM((size, wide, face), BF16)] * 2,
            [VMEM((size, wide, tracers), BF16)] * 2,
        )

    def enter_first(group, state, after):
        size = len(group)
        last = group[-1] == cols - 1
        newest = state.received[-1:]

        def body(order, inlet, within, reach_high, reach_low, *refs):
            got, refs = refs[: len(newest)], refs[len(newest) :]
            if last:
                (free, side_maps), refs = refs[:2], refs[3:]
            stack = refs[0]
            for n, c in enumerate(group):
                start = known_inflow(inlet[c])
                for r in got:
                    start = jnp.where(bit(stages - 1), r[n], start)
                inflow = within[n] + dot_split((reach_high[n], reach_low[n]), split(start))
                put_inflow(n, c, inflow, order, stack)
            if last:
                for j in range(count):
                    i = (size - 1) * count + j
                    part = dot(side_maps[i][:, : 3 * face], stack[i])
                    refs[1][j] = lateral_rows(free.at[i], per_side) + part

        outs = [VMEM((size * count, 3 * face, tracers), BF16)]
        if last:
            outs.append(VMEM((count, face, tracers), F32))
        ins = [order, inlet, state.within, *state.reach, *newest]
        if last:
            ins += [state.free, state.side_maps, after]
        values = run(body, "enter", ins, outs, [])
        state.stack = values[0]
        return values[1] if last else None

    def put_inflow(n, c, inflow, order, stack):
        for p in range(count):
            i = n * count + order[c, p]
            for q, part in enumerate(stack_inflow(split(inflow[p * face : (p + 1) * face]))):
                stack[i, pl.ds(q * face, face)] = part

    def second(group, state, after):
        items = len(group) * count

        def body(inv, maps, free, stack, rate, aff, _, source_high, source_low, traces, own):
            for i in range(items + 1):
                if i < items:
                    swept = free[i] + dot(maps[i][:, : 3 * face], stack[i])
                    traces[i] = lateral_rows(swept, per_side)
                    source_high[i], source_low[i] = split(langmuir(swept, rate[...], aff[...]))
                if i > 0:
                    own[i - 1] = times(inv[*at(group, i - 1), ending], source_high, source_low, i - 1)

        state.source_high, state.source_low, state.traces, state.own = run(
            body,
            "second",
            [inv_near, state.maps, state.free, state.stack, rate, aff, after],
            source_outs(len(group)) + [VMEM((items, face, tracers), F32)] * 2,
            [],
        )
        return state.own

    def fold_sides(after):
        def body(order, inlet, _, *refs):
            got = [refs[3 * g : 3 * g + 3] for g in range(len(groups))]
            outs = refs[3 * len(groups) :]
            for g, group in enumerate(groups):
                tails, rows_high, rows_low = got[g]
                high, low, begun = outs[3 * g : 3 * g + 3]
                for n, c in enumerate(group):
                    start = split(known_inflow(inlet[c]))
                    begun[n] = dot_split(last_row(rows_high, rows_low, n, 0), start)
                    for p in range(count):
                        folded = split(tails[n * count + order[c, p]][:, face:])
                        if p + 1 < count:
                            folded = split(dot_split(last_row(rows_high, rows_low, n, p + 1), folded))
                        high[n, p] = folded[0]
                        low[n, p] = folded[1]

        ins, outs = [order, inlet, after], []
        for group, state in zip(groups, states):
            ins += [state.tails, state.high, state.low]
            outs += [VMEM((len(group), count, face, face), BF16)] * 2
            outs.append(VMEM((len(group), face, tracers), F32))
        values = run(body, "fold_sides", ins, outs, [])
        for g, state in enumerate(states):
            state.side_high, state.side_low, state.begun = values[3 * g : 3 * g + 3]
        return values[0]

    def last_row(rows_high, rows_low, n, block):
        place = pl.ds(wide, face)
        return tuple(r[n, place][:, block * face : (block + 1) * face] for r in (rows_high, rows_low))

    def side_at(c, j, arrived, traces):
        if c == 0:
            return arrived_side(arrived, j)
        h, m = home[c - 1]
        return split(traces[h][m * count + j])

    def second_sides(arrived):
        def body(order, arrived, *refs):
            got = [refs[7 * g : 7 * g + 7] for g in range(len(groups))]
            message = refs[-1]
            for g, group in enumerate(groups):
                own, _, rows_high, rows_low, side_high, side_low, begun = got[g]
                for n, c in enumerate(group):
                    total = own[n * count + order[c, count - 1]] + begun[n]
                    for p in range(count):
                        s = side_at(c, order[c, p], arrived, [x[1] for x in got])
                        total = total + dot_split((side_high[n, p], side_low[n, p]), s)
                        if p + 1 < count:
                            row = last_row(rows_high, rows_low, n, p + 1)
                            total = total + dot_split(row, split(own[n * count + order[c, p]]))
                    message[c] = total

        ins = [order, arrived]
        for state in states:
            ins += [state.own, state.traces, state.high, state.low]
            ins += [state.side_high, state.side_low, state.begun]
        return run(body, "second_sides", ins, [VMEM((cols, face, tracers), F32)], [])[0]

    def settle(after, arrived, offsets):
        per_group = 8 + len(offsets)

        def body(order, inlet, _, arrived, inv, *refs):
            offs, refs = refs[: len(offsets)], refs[len(offsets) :]
            got = [refs[per_group * g : per_group * g + per_group] for g in range(len(groups))]
            outs = refs[per_group * len(groups) :]
            scratch = outs[2 * len(groups) :]
            for g, group in enumerate(groups):
                source_high, source_low, maps, rows_high, rows_low, own, traces, tails, *mapped = got[g]
                base, within = outs[2 * g : 2 * g + 2]
                ends, high, low = scratch[3 * g : 3 * g + 3]
                for i in range(len(group) * count):
                    whole = times(inv[at(group, i)], source_high, source_low, i)
                    s = side_at(group[0] + i // count, i % count, arrived, [x[6] for x in got])
                    base[i] = whole + dot(maps[i][:, 2 * face :], side_rows(s))
                for n, c in enumerate(group):
                    for p in range(count):
                        i = n * count + order[c, p]
                        s = side_at(c, order[c, p], arrived, [x[6] for x in got])
                        ends[n * count + p] = own[i] + side_of(tails, i, s)
                    old = [r[n, pl.ds(face, packed)] for r in mapped]
                    start = entering(known_inflow(inlet[c]), [r[c] for r in offs], old)
                    within[n] = within_of(n, start, ends, rows_high, rows_low, high, low)

        ins = [order, inlet, after, arrived, inv_near, *offsets]
        outs, scratch = [], []
        for group, state in zip(groups, states):
            ins += [state.source_high, state.source_low, state.maps, state.high, state.low]
            ins += [state.own, state.traces, state.tails, *state.received[:-1]]
            outs.append(VMEM((len(group) * count, nodes, tracers), F32))
            outs.append(VMEM((len(group), wide, tracers), F32))
            scratch.append(VMEM((len(group) * count, face, tracers), F32))
            scratch += [VMEM((len(group), wide, tracers), BF16)] * 2
        values = run(body, "settle", ins, outs, scratch)
        for g, state in enumerate(states):
            state.base, state.within = values[2 * g : 2 * g + 2]

    def result(offsets):
        def body(order, *refs):
            offs, refs = refs[: len(offsets)], refs[len(offsets) :]
            got = [refs[5 * g : 5 * g + 5] for g in range(len(groups))]
            out, staged, sems, *stacks = refs[5 * len(groups) :]
            for g, group in enumerate(groups):
                within, reach_high, reach_low = got[g][:3]
                for n, c in enumerate(group):
                    inflow = within[n]
                    for r in offs:
                        late_part = split(jnp.where(bit(stages - 1), r[c], 0.0))
                        inflow = inflow + dot_split((reach_high[n], reach_low[n]), late_part)
                    put_inflow(n, c, inflow, order, stacks[g])
            started = []
            for g, group in enumerate(groups):
                base, maps = got[g][3:]
                for i in range(len(group) * count):
                    k = len(started)
                    staged[k] = (base[i] + dot(maps[i][:, : 3 * face], stacks[g][i])).astype(BF16)
                    started.append(pltpu.make_async_copy(staged.at[k], out.at[at(group, i)], sems.at[k]))
                    started[-1].start()
            for copy in started:
                copy.wait()

        ins = [order, *offsets]
        scratch = [VMEM((cols * count, nodes, tracers), BF16), pltpu.SemaphoreType.DMA((cols * count,))]
        for group, state in zip(groups, states):
            ins += [state.within, *state.reach, state.base, state.maps]
            scratch.append(VMEM((len(group) * count, 3 * face, tracers), BF16))
        return run(body, "result", ins, [HBM(previous.shape, BF16)], scratch)[0]

    def exchange_first(state, beside):
        state.sent, state.received = [state.message], []
        for stage in range(stages):
            if stage:
                state.sent.append(combine_first(stage - 1, state.sent[-1], state.received[-1], after))
            state.received.append(swap(state.sent[-1], stage))
            if not stage:
                after = beside()

    (trace, order, rate, aff, inlet), one = load()
    order = (order, SMEM)
    arrived = to_next(trace)
    begin_early(one)
    exchange_first(one, lambda: early_maps(one, one.message))
    prepare(early, one, one.near, one.sent[-1])
    maps = late_maps(one.sent[-1])
    trace = enter_first(early, one, maps)
    arrived_next = to_next(trace)
    two = begin_late(trace)
    two.maps = maps
    states = [one, two]
    first_sides(two, arrived)
    exchange_first(two, lambda: second(early, one, two.message))
    prepare(late, two, arrived, two.sent[-1])
    fold_sides(two.sent[-1])
    enter_first(late, two, None)
    second(late, two, two.sent[-1])
    message, offsets = second_sides(arrived_next), []
    for stage in range(stages):
        offsets.append(swap(message, stage))
        if stage + 1 < stages:
            sent, received = [s.sent[stage] for s in states], [s.received[stage] for s in states]
            message = combine_second(stage, message, offsets[-1], sent, received)
    settle(message, arrived_next, offsets[:-1])
    return result(offsets[-1:])


def solution(mesh):
    placed = (
        P("lat", "stream", None, None, None),
        P("lat", "stream", None, None, None),
        P("lat", "stream", None, None, None),
        P("lat", None, None),
        P("lat", "stream", None, None, None),
        P(),
        P(),
        P("lat", "stream", None),
    )
    return jax.shard_map(
        per_device,
        mesh=mesh,
        in_specs=placed,
        out_specs=P("lat", "stream", None, None, None),
        check_vma=False,
    )
```

```python
from types import SimpleNamespace

import jax
import jax.numpy as jnp
from jax import lax
from jax.experimental import pallas as pl
from jax.experimental.pallas import tpu as pltpu
from jax.sharding import PartitionSpec as P

NODES_1D = 8
F32 = jnp.float32
BF16 = jnp.bfloat16
MIB = 1 << 20
VMEM = pltpu.VMEM
HBM = pltpu.HBM
SMEM = pltpu.SMEM


def run(body, name, ins, outs, scratch, work=0):
    pairs = [a if isinstance(a, tuple) else (a, VMEM) for a in ins]
    return pl.pallas_call(
        body,
        name=name,
        in_specs=[pl.BlockSpec(memory_space=space) for _, space in pairs],
        out_specs=[pl.BlockSpec(memory_space=o.memory_space) for o in outs],
        out_shape=outs,
        scratch_shapes=scratch,
        cost_estimate=pl.CostEstimate(flops=work, bytes_accessed=0, transcendentals=0),
        compiler_params=pltpu.CompilerParams(vmem_limit_bytes=24 * MIB),
    )(*[a if space is VMEM else pltpu.with_memory_space_constraint(a, space) for a, space in pairs])


def split(x):
    high = x.astype(BF16)
    return high, (x - high.astype(F32)).astype(BF16)


def dot(x, y):
    return jnp.dot(x, y, preferred_element_type=F32)


def dot_split(x, y):
    return dot(x[0], y[0]) + (dot(x[0], y[1]) + dot(x[1], y[0]))


def langmuir(lagged, rate, affinity):
    return rate * lagged * pltpu.reciprocal(1.0 + affinity * jnp.abs(lagged), approx=True)


def lateral_rows(field, per_side):
    plane = per_side * per_side
    return jnp.concatenate(
        [field[a * plane + plane - per_side : (a + 1) * plane] for a in range(per_side)], axis=0
    )


def pack_map(mapping, lanes):
    face = mapping.shape[0]
    rows = face * face // lanes
    return jnp.concatenate([mapping[q * rows : (q + 1) * rows] for q in range(lanes // face)], axis=1)


def unpack_map(packed, face):
    return jnp.concatenate(
        [packed[:, q * face : (q + 1) * face] for q in range(packed.shape[1] // face)], axis=0
    )


def stack_maps(both):
    face = both.shape[1] // 2
    turned = pltpu.roll(both, face, 1)
    first = lax.broadcasted_iota(jnp.int32, both.shape, 1) < face
    low = split(both)[1]
    return jnp.concatenate(
        [jnp.where(first, both, turned).astype(BF16), low, jnp.where(first, turned, both).astype(BF16)], axis=1
    )


def stack_inflow(f):
    return (f[0], f[1], f[0])


def stack_side(s):
    return (s[0], s[0], s[1])


def in_pairs(items, per, step):
    def turn(t, _):
        step([t * per + k for k in range(per)])
        return 0

    lax.fori_loop(0, items // per, turn, 0)


def known_inflow(inlet):
    return jnp.where(lax.axis_index("stream") == 0, inlet, 0.0)


def bit(stage):
    return ((lax.axis_index("stream") >> stage) & 1) == 1


def per_device(inverse, upwind, lateral, inlet_trace, previous, uptake_rate, affinity, flow_order):
    cols, _, count, nodes, _ = inverse.shape
    face = upwind.shape[3]
    tracers = previous.shape[-1]
    per_side = NODES_1D
    plane = per_side * per_side
    wide = count * face
    packed = face * face // tracers
    sent_rows = face + (packed if lax.axis_size("stream") > 2 else 0)
    streams, lats = lax.axis_size("stream"), lax.axis_size("lat")
    stages = streams.bit_length() - 1
    assert streams == 1 << stages
    assert cols > 1
    early, late = list(range(1, cols)), [0]
    groups = [early, late]
    home = {c: (g, n) for g, group in enumerate(groups) for n, c in enumerate(group)}
    ending = pl.ds(nodes - face, face)
    per = 2 if count % 2 == 0 else 1

    def to_next(value):
        return lax.ppermute(value, "lat", [(i, (i + 1) % lats) for i in range(lats)])

    def swap(value, stage):
        return lax.ppermute(value, "stream", [(i, i ^ (1 << stage)) for i in range(streams)])

    inv_near, up_near, side_near, old_near = (
        pltpu.with_memory_space_constraint(a, VMEM) for a in (inverse, upwind, lateral, previous)
    )
    shaped = previous.reshape(cols, count, per_side, plane, tracers)

    def map_outs(size):
        return [VMEM((size * count, nodes, 6 * face), BF16), VMEM((size * count, face, 6 * face), BF16)]

    def chain_outs(size):
        return [
            VMEM((size * count, face, 2 * face), F32),
            VMEM((size, wide + face, wide), BF16),
            VMEM((size, wide + face, wide), BF16),
        ]

    def offset_scratch(size):
        return [VMEM((size, wide, tracers), BF16)] * 2

    def source_outs(size):
        return [VMEM((size * count, nodes, tracers), BF16)] * 2

    def times(matrix, high, low, i):
        return dot(matrix, high[i]) + dot(matrix, low[i])

    def face_maps(matrix, up, side):
        faces = jnp.concatenate([up, side], axis=0)
        return lax.dot_general(matrix, faces, (((1,), (1,)), ((), ())), preferred_element_type=F32)

    def at(group, i):
        return group[0] + i // count, 0, i % count

    def side_of(tails, i, s):
        return dot_split(split(tails[i][:, face:]), s)

    def link(n, p, step, rows_high, rows_low, row):
        row_id = lax.broadcasted_iota(jnp.int32, (face, wide), 0)
        lane_id = lax.broadcasted_iota(jnp.int32, (face, wide), 1)
        unit = jnp.where(lane_id == row_id + p * face, 1.0, 0.0)
        r = split(jnp.where(p == 0, 0.0, row[n]) + unit)
        here = pl.ds(pl.multiple_of(p * face, face), face)
        rows_high[n, here] = r[0]
        rows_low[n, here] = r[1]
        r = split(dot_split(step, r))
        rows_high[n, pl.ds(wide, face)] = r[0]
        rows_low[n, pl.ds(wide, face)] = r[1]
        row[n] = r[0].astype(F32) + r[1].astype(F32)

    def offset(n, start, rows_high, rows_low, ends, high, low):
        for p in range(count):
            e = split(start if p == 0 else ends[n * count + p - 1])
            high[n, pl.ds(p * face, face)] = e[0]
            low[n, pl.ds(p * face, face)] = e[1]
        last = pl.ds(wide, face)
        return ends[n * count + count - 1] + dot_split((rows_high[n, last], rows_low[n, last]), (high[n], low[n]))

    def load():
        size = len(early)
        items = size * count

        def body(
            order, rate, aff, inlet, old, inverse, previous,
            o_order, o_rate, o_aff, o_inlet, near, o_tail, source_high, source_low, lagged,
            staged, lead_sems, sems,
        ):
            rows = pl.ds(plane - 2 * per_side, 2 * per_side)
            lead = [
                pltpu.make_async_copy(a, b, lead_sems.at[k])
                for k, (a, b) in enumerate((
                    (rate, o_rate),
                    (aff, o_aff),
                    (order, o_order),
                    (old.at[0, :, :, rows], staged),
                    (inlet, o_inlet),
                ))
            ]
            whole = pl.ds(0, count)
            fields, others = [], []
            for n, c in enumerate(early):
                for h in range(count):
                    here, there = pl.ds(h, 1), pl.ds(n * count + h, 1)
                    fields.append((previous.at[c, 0, here], lagged.at[there]))
                there = pl.ds(n * count, count)
                others.append((inverse.at[c, 0, whole, ending], o_tail.at[there]))
            copies = [pltpu.make_async_copy(a, b, sems.at[k]) for k, (a, b) in enumerate(fields + others)]
            for one in lead[:3] + copies[: len(fields)] + lead[3:4] + copies[len(fields) :] + lead[4:]:
                one.start()
            for one in lead[:3]:
                one.wait()

            def old_rows(field):
                return jnp.concatenate([field(a).astype(F32)[per_side:] for a in range(per_side)], axis=0)

            for k in range(len(fields)):
                copies[k].wait()
                for i in range(k, k + 1):
                    lag = lagged[i].astype(F32)
                    source_high[i], source_low[i] = split(langmuir(lag, o_rate[...], o_aff[...]))
                    if early[i // count] < cols - 1:
                        near[i + count] = lateral_rows(lag, per_side)
            for one in lead[3:]:
                one.wait()
            for j in range(count):
                near[j] = old_rows(lambda a: staged[j, a])
            for one in copies[len(fields) :]:
                one.wait()

        values = run(
            body,
            "load",
            [
                (flow_order.reshape(cols, count), HBM),
                (uptake_rate.reshape(1, tracers), HBM),
                (affinity.reshape(1, tracers), HBM),
                (inlet_trace, HBM),
                (shaped, HBM),
                (inverse, HBM),
                (previous, HBM),
            ],
            [
                SMEM((cols, count), jnp.int32),
                VMEM((1, tracers), F32),
                VMEM((1, tracers), F32),
                VMEM((cols, face, tracers), F32),
                VMEM((items, face, tracers), F32),
                VMEM((items, face, nodes), BF16),
                *source_outs(size),
                VMEM((items, nodes, tracers), BF16),
            ],
            [
                VMEM((count, per_side, 2 * per_side, tracers), BF16),
                pltpu.SemaphoreType.DMA((5,)),
                pltpu.SemaphoreType.DMA((size * (count + 1),)),
            ],
        )
        state = SimpleNamespace()
        state.near, state.tail, state.source_high, state.source_low, lagged = values[4:]

        def old_trace(lagged, trace):
            for j in range(count):
                for a in range(per_side):
                    start = a * plane + plane - 2 * per_side
                    rows = lagged[items - count + j, pl.ds(start, 2 * per_side)].astype(F32)
                    trace[j, pl.ds(a * per_side, per_side)] = rows[per_side:]

        trace = run(old_trace, "old_trace", [lagged], [VMEM((count, face, tracers), F32)], [], 3000000000)[0]
        return (trace, *values[:4]), state

    def begin_early(state):
        size = len(early)
        items = size * count

        def body(
            order, inlet, near, tail, up, side, source_high, source_low, tails, ends, message, own
        ):
            for i in range(items):
                tails[i] = face_maps(tail[i], up[at(early, i)], side[at(early, i)])
            for i in range(items):
                own[i] = times(tail[i], source_high, source_low, i)
            for n, c in enumerate(early):
                links = []
                for p in range(count):
                    i = n * count + order[c, p]
                    end = own[i] + side_of(tails, i, split(near[i]))
                    ends[n * count + p] = end
                    if p == 0:
                        begun = split(known_inflow(inlet[c]))
                        end = end + dot_split(split(tails[i][:, :face]), begun)
                    links.append((tails[i][:, :face], end))
                while len(links) > 1:
                    paired = []
                    for (low, start), (up, end) in zip(links[::2], links[1::2]):
                        u = split(up)
                        paired.append((dot_split(u, split(low)), end + dot_split(u, split(start))))
                    links = paired + links[2 * len(paired) :]
                message[n, pl.ds(0, face)] = links[0][1]
                if sent_rows > face:
                    message[n, pl.ds(face, packed)] = pack_map(links[0][0], tracers)

        state.tails, state.ends, state.message = run(
            body,
            "begin_early",
            [order, inlet, state.near, state.tail, up_near, side_near, state.source_high, state.source_low],
            [
                VMEM((items, face, 2 * face), F32),
                VMEM((items, face, tracers), F32),
                VMEM((size, sent_rows, tracers), F32),
            ],
            [VMEM((items, face, tracers), F32)],
        )

    def early_maps(state, after):
        size = len(early)

        def body(order, inv, up, side, tails, _, maps, side_maps, rows_high, rows_low, row):
            for i in range(size * count):
                k = at(early, i)
                both = face_maps(inv[k], up[k], side[k])
                maps[i] = stack_maps(both)
                side_maps[i] = stack_maps(lateral_rows(both, per_side))
                n, p = i // count, i % count
                head = tails[n * count + order[early[0] + n, p]][:, :face]
                link(n, p, split(head), rows_high, rows_low, row)

        state.maps, state.side_maps, state.high, state.low = run(
            body,
            "early_maps",
            [order, inv_near, up_near, side_near, state.tails, after],
            map_outs(size) + chain_outs(size)[1:],
            [VMEM((size, face, wide), F32)],
        )
        return state.maps

    def late_sources(after):
        def body(previous, rate, aff, _, source_high, source_low):
            for i in range(len(late) * count):
                lag = previous[at(late, i)].astype(F32)
                source_high[i], source_low[i] = split(langmuir(lag, rate[...], aff[...]))

        return run(body, "late_sources", [old_near, rate, aff, after], source_outs(len(late)), [])

    def begin_late(sources, after):
        size = len(late)
        items = size * count

        def body(
            order, inv, up, side, source_high, source_low, _,
            own, tails, rows_high, rows_low, mapped, row,
        ):
            for i in range(items):
                k = at(late, i)
                tails[i] = face_maps(inv[*k, ending], up[k], side[k])
            for i in range(items):
                own[i] = times(inv[*at(late, i), ending], source_high, source_low, i)
                n, p = i // count, i % count
                step = split(tails[n * count + order[late[n], p]][:, :face])
                link(n, p, step, rows_high, rows_low, row)
            for n in range(size):
                mapped[n] = pack_map(row[n][:, :face], tracers)

        state = SimpleNamespace()
        values = run(
            body,
            "begin_late",
            [order, inv_near, up_near, side_near, *sources, after],
            [VMEM((items, face, tracers), F32)]
            + chain_outs(size)
            + [VMEM((size, packed, tracers), F32)],
            [VMEM((size, face, wide), F32)],
        )
        state.source_high, state.source_low = sources
        state.own, state.tails, state.high, state.low, state.mapped = values
        return state

    def late_maps(after):
        items = len(late) * count

        def body(inv, up, side, _, maps):
            for i in range(items):
                k = at(late, i)
                maps[i] = stack_maps(face_maps(inv[k], up[k], side[k]))

        return run(body, "late_maps", [inv_near, up_near, side_near, after], map_outs(len(late))[:1], [])[0]

    def arrived_side(arrived, j):
        return split(jnp.where(lax.axis_index("lat") > 0, arrived[j], 0.0))

    def first_sides(state, arrived):
        def body(order, inlet, arrived, own, tails, rows_high, rows_low, mapped, ends, message, high, low):
            for p in range(count):
                j = order[0, p]
                ends[p] = own[j] + side_of(tails, j, arrived_side(arrived, j))
            message[0, pl.ds(0, face)] = offset(0, known_inflow(inlet[0]), rows_high, rows_low, ends, high, low)
            if sent_rows > face:
                message[0, pl.ds(face, packed)] = mapped[0]

        state.ends, state.message = run(
            body,
            "first_sides",
            [order, inlet, arrived, state.own, state.tails, state.high, state.low, state.mapped],
            [VMEM((count, face, tracers), F32), VMEM((1, sent_rows, tracers), F32)],
            offset_scratch(1),
        )

    def combine_first(stage, own, other, after):
        rows = face if stage + 2 == stages else sent_rows

        def body(own, other, _, message):
            upper = bit(stage)
            for n in range(own.shape[0]):
                up = jnp.where(upper, own[n], other[n])
                low = jnp.where(upper, other[n], own[n])
                m = split(unpack_map(up[face:], face))
                message[n, pl.ds(0, face)] = dot_split(m, split(low[:face])) + up[:face]
                if rows > face:
                    mapped = dot_split(m, split(unpack_map(low[face:], face)))
                    message[n, pl.ds(face, packed)] = pack_map(mapped, tracers)

        return run(body, "combine", [own, other, after], [VMEM((own.shape[0], rows, tracers), F32)], [])[0]

    def combine_second(stage, own, other, old_own, old_other):
        def body(own, other, *refs):
            message = refs[-1]
            upper = bit(stage)
            for c in range(cols):
                g, n = home[c]
                mine, theirs = refs[2 * g], refs[2 * g + 1]
                m = jnp.where(upper, mine[n, pl.ds(face, packed)], theirs[n, pl.ds(face, packed)])
                up = jnp.where(upper, own[c], other[c])
                low = jnp.where(upper, other[c], own[c])
                message[c] = dot_split(split(unpack_map(m, face)), split(low)) + up

        ins = [own, other]
        for pair in zip(old_own, old_other):
            ins += pair
        return run(body, "combine", ins, [VMEM(own.shape, F32)], [])[0]

    def entering(start, offsets, maps):
        for stage in reversed(range(len(maps))):
            m = split(unpack_map(maps[stage], face))
            beyond = dot_split(m, split(start)) + offsets[stage]
            start = jnp.where(bit(stage), beyond, start)
        return start

    def lower_maps(maps):
        rows = lax.broadcasted_iota(jnp.int32, (face, face), 0)
        total = jnp.where(rows == lax.broadcasted_iota(jnp.int32, (face, face), 1), 1.0, 0.0)
        for stage in reversed(range(stages - 1)):
            beyond = dot_split(split(unpack_map(maps[stage], face)), split(total))
            total = jnp.where(bit(stage), beyond, total)
        return total

    def within_of(n, start, ends, rows_high, rows_low, high, low):
        for p in range(count):
            e = split(start if p == 0 else ends[n * count + p - 1])
            high[n, pl.ds(p * face, face)] = e[0]
            low[n, pl.ds(p * face, face)] = e[1]
        span = pl.ds(0, wide)
        return dot_split((rows_high[n, span], rows_low[n, span]), (high[n], low[n]))

    def side_rows(s):
        return jnp.concatenate([jnp.zeros((face, tracers), BF16), *stack_side(s)], axis=0)

    def prepare(group, state, sides, after):
        size = len(group)
        lower = state.received[:-1]

        def body(inv, sides, source_high, source_low, maps, ends, rows_high, rows_low, _, *refs):
            mapped, (free, within, reach_high, reach_low, high, low) = refs[: len(lower)], refs[len(lower) :]
            span = pl.ds(0, wide)
            for i in range(size * count):
                s = arrived_side(sides, i) if group[0] == 0 else split(sides[i])
                whole = times(inv[at(group, i)], source_high, source_low, i)
                free[i] = whole + dot(maps[i][:, 2 * face :], side_rows(s))
            for n in range(size):
                old = [r[n, pl.ds(face, packed)] for r in mapped]
                start = entering(jnp.zeros((face, tracers), F32), [r[n, pl.ds(0, face)] for r in mapped], old)
                within[n] = within_of(n, start, ends, rows_high, rows_low, high, low)
                rows = (rows_high[n, span][:, :face], rows_low[n, span][:, :face])
                reach_high[n], reach_low[n] = split(dot_split(rows, split(lower_maps(old))))

        state.free, state.within, *state.reach = run(
            body,
            "prepare",
            [inv_near, sides, state.source_high, state.source_low, state.maps, state.ends, state.high, state.low]
            + [after, *lower],
            [VMEM((size * count, nodes, tracers), F32), VMEM((size, wide, tracers), F32)]
            + [VMEM((size, wide, face), BF16)] * 2,
            [VMEM((size, wide, tracers), BF16)] * 2,
        )

    def enter_first(group, state, after):
        size = len(group)
        last = group[-1] == cols - 1
        newest = state.received[-1:]

        def body(order, inlet, within, reach_high, reach_low, *refs):
            got, refs = refs[: len(newest)], refs[len(newest) :]
            if last:
                (free, side_maps), refs = refs[:2], refs[3:]
            stack = refs[0]
            for n, c in enumerate(group):
                start = known_inflow(inlet[c])
                for r in got:
                    start = jnp.where(bit(stages - 1), r[n], start)
                inflow = within[n] + dot_split((reach_high[n], reach_low[n]), split(start))
                put_inflow(n, c, inflow, order, stack)
            if last:
                for j in range(count):
                    i = (size - 1) * count + j
                    part = dot(side_maps[i][:, : 3 * face], stack[i])
                    refs[1][j] = lateral_rows(free.at[i], per_side) + part

        outs = [VMEM((size * count, 3 * face, tracers), BF16)]
        if last:
            outs.append(VMEM((count, face, tracers), F32))
        ins = [order, inlet, state.within, *state.reach, *newest]
        if last:
            ins += [state.free, state.side_maps, after]
        values = run(body, "enter", ins, outs, [])
        state.stack = values[0]
        return values[1] if last else None

    def put_inflow(n, c, inflow, order, stack):
        for p in range(count):
            i = n * count + order[c, p]
            for q, part in enumerate(stack_inflow(split(inflow[p * face : (p + 1) * face]))):
                stack[i, pl.ds(q * face, face)] = part

    def second(group, state, after):
        items = len(group) * count

        def body(inv, maps, free, stack, rate, aff, _, source_high, source_low, traces, own):
            for i in range(items + 1):
                if i < items:
                    swept = free[i] + dot(maps[i][:, : 3 * face], stack[i])
                    traces[i] = lateral_rows(swept, per_side)
                    source_high[i], source_low[i] = split(langmuir(swept, rate[...], aff[...]))
                if i > 0:
                    own[i - 1] = times(inv[*at(group, i - 1), ending], source_high, source_low, i - 1)

        state.source_high, state.source_low, state.traces, state.own = run(
            body,
            "second",
            [inv_near, state.maps, state.free, state.stack, rate, aff, after],
            source_outs(len(group)) + [VMEM((items, face, tracers), F32)] * 2,
            [],
        )
        return state.own

    def fold_sides(after):
        def body(order, inlet, _, *refs):
            got = [refs[3 * g : 3 * g + 3] for g in range(len(groups))]
            outs = refs[3 * len(groups) :]
            for g, group in enumerate(groups):
                tails, rows_high, rows_low = got[g]
                high, low, begun = outs[3 * g : 3 * g + 3]
                for n, c in enumerate(group):
                    start = split(known_inflow(inlet[c]))
                    begun[n] = dot_split(last_row(rows_high, rows_low, n, 0), start)
                    for p in range(count):
                        folded = split(tails[n * count + order[c, p]][:, face:])
                        if p + 1 < count:
                            folded = split(dot_split(last_row(rows_high, rows_low, n, p + 1), folded))
                        high[n, p] = folded[0]
                        low[n, p] = folded[1]

        ins, outs = [order, inlet, after], []
        for group, state in zip(groups, states):
            ins += [state.tails, state.high, state.low]
            outs += [VMEM((len(group), count, face, face), BF16)] * 2
            outs.append(VMEM((len(group), face, tracers), F32))
        values = run(body, "fold_sides", ins, outs, [])
        for g, state in enumerate(states):
            state.side_high, state.side_low, state.begun = values[3 * g : 3 * g + 3]
        return values[0]

    def last_row(rows_high, rows_low, n, block):
        place = pl.ds(wide, face)
        return tuple(r[n, place][:, block * face : (block + 1) * face] for r in (rows_high, rows_low))

    def side_at(c, j, arrived, traces):
        if c == 0:
            return arrived_side(arrived, j)
        h, m = home[c - 1]
        return split(traces[h][m * count + j])

    def second_sides(arrived):
        def body(order, arrived, *refs):
            got = [refs[7 * g : 7 * g + 7] for g in range(len(groups))]
            message = refs[-1]
            for g, group in enumerate(groups):
                own, _, rows_high, rows_low, side_high, side_low, begun = got[g]
                for n, c in enumerate(group):
                    total = own[n * count + order[c, count - 1]] + begun[n]
                    for p in range(count):
                        s = side_at(c, order[c, p], arrived, [x[1] for x in got])
                        total = total + dot_split((side_high[n, p], side_low[n, p]), s)
                        if p + 1 < count:
                            row = last_row(rows_high, rows_low, n, p + 1)
                            total = total + dot_split(row, split(own[n * count + order[c, p]]))
                    message[c] = total

        ins = [order, arrived]
        for state in states:
            ins += [state.own, state.traces, state.high, state.low]
            ins += [state.side_high, state.side_low, state.begun]
        return run(body, "second_sides", ins, [VMEM((cols, face, tracers), F32)], [])[0]

    def settle(after, arrived, offsets):
        per_group = 8 + len(offsets)

        def body(order, inlet, _, arrived, inv, *refs):
            offs, refs = refs[: len(offsets)], refs[len(offsets) :]
            got = [refs[per_group * g : per_group * g + per_group] for g in range(len(groups))]
            outs = refs[per_group * len(groups) :]
            scratch = outs[2 * len(groups) :]
            for g, group in enumerate(groups):
                source_high, source_low, maps, rows_high, rows_low, own, traces, tails, *mapped = got[g]
                base, within = outs[2 * g : 2 * g + 2]
                ends, high, low = scratch[3 * g : 3 * g + 3]
                for i in range(len(group) * count):
                    whole = times(inv[at(group, i)], source_high, source_low, i)
                    s = side_at(group[0] + i // count, i % count, arrived, [x[6] for x in got])
                    base[i] = whole + dot(maps[i][:, 2 * face :], side_rows(s))
                for n, c in enumerate(group):
                    for p in range(count):
                        i = n * count + order[c, p]
                        s = side_at(c, order[c, p], arrived, [x[6] for x in got])
                        ends[n * count + p] = own[i] + side_of(tails, i, s)
                    old = [r[n, pl.ds(face, packed)] for r in mapped]
                    start = entering(known_inflow(inlet[c]), [r[c] for r in offs], old)
                    within[n] = within_of(n, start, ends, rows_high, rows_low, high, low)

        ins = [order, inlet, after, arrived, inv_near, *offsets]
        outs, scratch = [], []
        for group, state in zip(groups, states):
            ins += [state.source_high, state.source_low, state.maps, state.high, state.low]
            ins += [state.own, state.traces, state.tails, *state.received[:-1]]
            outs.append(VMEM((len(group) * count, nodes, tracers), F32))
            outs.append(VMEM((len(group), wide, tracers), F32))
            scratch.append(VMEM((len(group) * count, face, tracers), F32))
            scratch += [VMEM((len(group), wide, tracers), BF16)] * 2
        values = run(body, "settle", ins, outs, scratch)
        for g, state in enumerate(states):
            state.base, state.within = values[2 * g : 2 * g + 2]

    def result(offsets):
        def body(order, *refs):
            offs, refs = refs[: len(offsets)], refs[len(offsets) :]
            got = [refs[5 * g : 5 * g + 5] for g in range(len(groups))]
            out, staged, sems, *stacks = refs[5 * len(groups) :]
            for g, group in enumerate(groups):
                within, reach_high, reach_low = got[g][:3]
                for n, c in enumerate(group):
                    inflow = within[n]
                    for r in offs:
                        late_part = split(jnp.where(bit(stages - 1), r[c], 0.0))
                        inflow = inflow + dot_split((reach_high[n], reach_low[n]), late_part)
                    put_inflow(n, c, inflow, order, stacks[g])
            started = []
            for g, group in enumerate(groups):
                base, maps = got[g][3:]
                for i in range(len(group) * count):
                    k = len(started)
                    staged[k] = (base[i] + dot(maps[i][:, : 3 * face], stacks[g][i])).astype(BF16)
                    started.append(pltpu.make_async_copy(staged.at[k], out.at[at(group, i)], sems.at[k]))
                    started[-1].start()
            for copy in started:
                copy.wait()

        ins = [order, *offsets]
        scratch = [VMEM((cols * count, nodes, tracers), BF16), pltpu.SemaphoreType.DMA((cols * count,))]
        for group, state in zip(groups, states):
            ins += [state.within, *state.reach, state.base, state.maps]
            scratch.append(VMEM((len(group) * count, 3 * face, tracers), BF16))
        return run(body, "result", ins, [HBM(previous.shape, BF16)], scratch)[0]

    def exchange_first(state, beside):
        state.sent, state.received = [state.message], []
        for stage in range(stages):
            if stage:
                state.sent.append(combine_first(stage - 1, state.sent[-1], state.received[-1], after))
            state.received.append(swap(state.sent[-1], stage))
            if not stage:
                after = beside()

    (trace, order, rate, aff, inlet), one = load()
    order = (order, SMEM)
    arrived = to_next(trace)
    begin_early(one)
    exchange_first(one, lambda: early_maps(one, one.message))
    prepare(early, one, one.near, one.sent[-1])
    sources = late_sources(one.sent[-1])
    trace = enter_first(early, one, sources[0])
    arrived_next = to_next(trace)
    two = begin_late(sources, trace)
    states = [one, two]
    first_sides(two, arrived)
    exchange_first(two, lambda: second(early, one, two.message))
    two.maps = late_maps(two.sent[-1])
    prepare(late, two, arrived, two.sent[-1])
    fold_sides(two.sent[-1])
    enter_first(late, two, None)
    second(late, two, two.sent[-1])
    message, offsets = second_sides(arrived_next), []
    for stage in range(stages):
        offsets.append(swap(message, stage))
        if stage + 1 < stages:
            sent, received = [s.sent[stage] for s in states], [s.received[stage] for s in states]
            message = combine_second(stage, message, offsets[-1], sent, received)
    settle(message, arrived_next, offsets[:-1])
    return result(offsets[-1:])


def solution(mesh):
    placed = (
        P("lat", "stream", None, None, None),
        P("lat", "stream", None, None, None),
        P("lat", "stream", None, None, None),
        P("lat", None, None),
        P("lat", "stream", None, None, None),
        P(),
        P(),
        P("lat", "stream", None),
    )
    return jax.shard_map(
        per_device,
        mesh=mesh,
        in_specs=placed,
        out_specs=P("lat", "stream", None, None, None),
        check_vma=False,
    )
```

```python
from types import SimpleNamespace

import jax
import jax.numpy as jnp
from jax import lax
from jax.experimental import pallas as pl
from jax.experimental.pallas import tpu as pltpu
from jax.sharding import PartitionSpec as P

NODES_1D = 8
F32 = jnp.float32
BF16 = jnp.bfloat16
MIB = 1 << 20
VMEM = pltpu.VMEM
HBM = pltpu.HBM
SMEM = pltpu.SMEM


def run(body, name, ins, outs, scratch, work=0):
    pairs = [a if isinstance(a, tuple) else (a, VMEM) for a in ins]
    return pl.pallas_call(
        body,
        name=name,
        in_specs=[pl.BlockSpec(memory_space=space) for _, space in pairs],
        out_specs=[pl.BlockSpec(memory_space=o.memory_space) for o in outs],
        out_shape=outs,
        scratch_shapes=scratch,
        cost_estimate=pl.CostEstimate(flops=work, bytes_accessed=0, transcendentals=0),
        compiler_params=pltpu.CompilerParams(vmem_limit_bytes=24 * MIB),
    )(*[a if space is VMEM else pltpu.with_memory_space_constraint(a, space) for a, space in pairs])


def split(x):
    high = x.astype(BF16)
    return high, (x - high.astype(F32)).astype(BF16)


def dot(x, y):
    return jnp.dot(x, y, preferred_element_type=F32)


def dot_split(x, y):
    return dot(x[0], y[0]) + (dot(x[0], y[1]) + dot(x[1], y[0]))


def langmuir(lagged, rate, affinity):
    return rate * lagged * pltpu.reciprocal(1.0 + affinity * jnp.abs(lagged), approx=True)


def lateral_rows(field, per_side):
    plane = per_side * per_side
    return jnp.concatenate(
        [field[a * plane + plane - per_side : (a + 1) * plane] for a in range(per_side)], axis=0
    )


def pack_map(mapping, lanes):
    face = mapping.shape[0]
    rows = face * face // lanes
    return jnp.concatenate([mapping[q * rows : (q + 1) * rows] for q in range(lanes // face)], axis=1)


def unpack_map(packed, face):
    return jnp.concatenate(
        [packed[:, q * face : (q + 1) * face] for q in range(packed.shape[1] // face)], axis=0
    )


def stack_maps(both):
    face = both.shape[1] // 2
    turned = pltpu.roll(both, face, 1)
    first = lax.broadcasted_iota(jnp.int32, both.shape, 1) < face
    low = split(both)[1]
    return jnp.concatenate(
        [jnp.where(first, both, turned).astype(BF16), low, jnp.where(first, turned, both).astype(BF16)], axis=1
    )


def stack_inflow(f):
    return (f[0], f[1], f[0])


def stack_side(s):
    return (s[0], s[0], s[1])


def in_pairs(items, per, step):
    def turn(t, _):
        step([t * per + k for k in range(per)])
        return 0

    lax.fori_loop(0, items // per, turn, 0)


def known_inflow(inlet):
    return jnp.where(lax.axis_index("stream") == 0, inlet, 0.0)


def bit(stage):
    return ((lax.axis_index("stream") >> stage) & 1) == 1


def per_device(inverse, upwind, lateral, inlet_trace, previous, uptake_rate, affinity, flow_order):
    cols, _, count, nodes, _ = inverse.shape
    face = upwind.shape[3]
    tracers = previous.shape[-1]
    per_side = NODES_1D
    plane = per_side * per_side
    wide = count * face
    packed = face * face // tracers
    sent_rows = face + (packed if lax.axis_size("stream") > 2 else 0)
    streams, lats = lax.axis_size("stream"), lax.axis_size("lat")
    stages = streams.bit_length() - 1
    assert streams == 1 << stages
    assert cols > 1
    early, late = list(range(1, cols)), [0]
    groups = [early, late]
    home = {c: (g, n) for g, group in enumerate(groups) for n, c in enumerate(group)}
    ending = pl.ds(nodes - face, face)
    per = 2 if count % 2 == 0 else 1

    def to_next(value):
        return lax.ppermute(value, "lat", [(i, (i + 1) % lats) for i in range(lats)])

    def swap(value, stage):
        return lax.ppermute(value, "stream", [(i, i ^ (1 << stage)) for i in range(streams)])

    inv_near, up_near, side_near, old_near = (
        pltpu.with_memory_space_constraint(a, VMEM) for a in (inverse, upwind, lateral, previous)
    )
    shaped = previous.reshape(cols, count, per_side, plane, tracers)

    def map_outs(size):
        return [VMEM((size * count, nodes, 6 * face), BF16), VMEM((size * count, face, 6 * face), BF16)]

    def chain_outs(size):
        return [
            VMEM((size * count, face, 2 * face), F32),
            VMEM((size, wide + face, wide), BF16),
            VMEM((size, wide + face, wide), BF16),
        ]

    def offset_scratch(size):
        return [VMEM((size, wide, tracers), BF16)] * 2

    def source_outs(size):
        return [VMEM((size * count, nodes, tracers), BF16)] * 2

    def times(matrix, high, low, i):
        return dot(matrix, high[i]) + dot(matrix, low[i])

    def face_maps(matrix, up, side):
        faces = jnp.concatenate([up, side], axis=0)
        return lax.dot_general(matrix, faces, (((1,), (1,)), ((), ())), preferred_element_type=F32)

    def at(group, i):
        return group[0] + i // count, 0, i % count

    def side_of(tails, i, s):
        return dot_split(split(tails[i][:, face:]), s)

    def link(n, p, step, rows_high, rows_low, row):
        row_id = lax.broadcasted_iota(jnp.int32, (face, wide), 0)
        lane_id = lax.broadcasted_iota(jnp.int32, (face, wide), 1)
        unit = jnp.where(lane_id == row_id + p * face, 1.0, 0.0)
        r = split(jnp.where(p == 0, 0.0, row[n]) + unit)
        here = pl.ds(pl.multiple_of(p * face, face), face)
        rows_high[n, here] = r[0]
        rows_low[n, here] = r[1]
        r = split(dot_split(step, r))
        rows_high[n, pl.ds(wide, face)] = r[0]
        rows_low[n, pl.ds(wide, face)] = r[1]
        row[n] = r[0].astype(F32) + r[1].astype(F32)

    def offset(n, start, rows_high, rows_low, ends, high, low):
        for p in range(count):
            e = split(start if p == 0 else ends[n * count + p - 1])
            high[n, pl.ds(p * face, face)] = e[0]
            low[n, pl.ds(p * face, face)] = e[1]
        last = pl.ds(wide, face)
        return ends[n * count + count - 1] + dot_split((rows_high[n, last], rows_low[n, last]), (high[n], low[n]))

    def load():
        size = len(early)
        items = size * count

        def body(
            order, rate, aff, inlet, old, inverse, previous,
            o_order, o_rate, o_aff, o_inlet, near, o_tail, source_high, source_low, lagged,
            staged, lead_sems, sems,
        ):
            rows = pl.ds(plane - 2 * per_side, 2 * per_side)
            lead = [
                pltpu.make_async_copy(a, b, lead_sems.at[k])
                for k, (a, b) in enumerate((
                    (rate, o_rate),
                    (aff, o_aff),
                    (order, o_order),
                    (old.at[0, :, :, rows], staged),
                    (inlet, o_inlet),
                ))
            ]
            whole = pl.ds(0, count)
            fields, others = [], []
            for n, c in enumerate(early):
                for h in range(count):
                    here, there = pl.ds(h, 1), pl.ds(n * count + h, 1)
                    fields.append((previous.at[c, 0, here], lagged.at[there]))
                there = pl.ds(n * count, count)
                others.append((inverse.at[c, 0, whole, ending], o_tail.at[there]))
            copies = [pltpu.make_async_copy(a, b, sems.at[k]) for k, (a, b) in enumerate(fields + others)]
            for one in lead[:3] + copies[: len(fields)] + lead[3:4] + copies[len(fields) :] + lead[4:]:
                one.start()
            for one in lead[:3]:
                one.wait()

            def old_rows(field):
                return jnp.concatenate([field(a).astype(F32)[per_side:] for a in range(per_side)], axis=0)

            for k in range(len(fields)):
                copies[k].wait()
                for i in range(k, k + 1):
                    lag = lagged[i].astype(F32)
                    source_high[i], source_low[i] = split(langmuir(lag, o_rate[...], o_aff[...]))
                    if early[i // count] < cols - 1:
                        near[i + count] = lateral_rows(lag, per_side)
            for one in lead[3:]:
                one.wait()
            for j in range(count):
                near[j] = old_rows(lambda a: staged[j, a])
            for one in copies[len(fields) :]:
                one.wait()

        values = run(
            body,
            "load",
            [
                (flow_order.reshape(cols, count), HBM),
                (uptake_rate.reshape(1, tracers), HBM),
                (affinity.reshape(1, tracers), HBM),
                (inlet_trace, HBM),
                (shaped, HBM),
                (inverse, HBM),
                (previous, HBM),
            ],
            [
                SMEM((cols, count), jnp.int32),
                VMEM((1, tracers), F32),
                VMEM((1, tracers), F32),
                VMEM((cols, face, tracers), F32),
                VMEM((items, face, tracers), F32),
                VMEM((items, face, nodes), BF16),
                *source_outs(size),
                VMEM((items, nodes, tracers), BF16),
            ],
            [
                VMEM((count, per_side, 2 * per_side, tracers), BF16),
                pltpu.SemaphoreType.DMA((5,)),
                pltpu.SemaphoreType.DMA((size * (count + 1),)),
            ],
        )
        state = SimpleNamespace()
        state.near, state.tail, state.source_high, state.source_low, lagged = values[4:]

        def old_trace(lagged, trace):
            for j in range(count):
                for a in range(per_side):
                    start = a * plane + plane - 2 * per_side
                    rows = lagged[items - count + j, pl.ds(start, 2 * per_side)].astype(F32)
                    trace[j, pl.ds(a * per_side, per_side)] = rows[per_side:]

        trace = run(old_trace, "old_trace", [lagged], [VMEM((count, face, tracers), F32)], [], 3000000000)[0]
        return (trace, *values[:4]), state

    def begin_early(state):
        size = len(early)
        items = size * count

        def body(
            order, inlet, near, tail, up, side, source_high, source_low, tails, ends, message, own
        ):
            for i in range(items):
                tails[i] = face_maps(tail[i], up[at(early, i)], side[at(early, i)])
            for i in range(items):
                own[i] = times(tail[i], source_high, source_low, i)
            for n, c in enumerate(early):
                links = []
                for p in range(count):
                    i = n * count + order[c, p]
                    end = own[i] + side_of(tails, i, split(near[i]))
                    ends[n * count + p] = end
                    if p == 0:
                        begun = split(known_inflow(inlet[c]))
                        end = end + dot_split(split(tails[i][:, :face]), begun)
                    links.append((tails[i][:, :face], end))
                while len(links) > 1:
                    paired = []
                    for (low, start), (up, end) in zip(links[::2], links[1::2]):
                        u = split(up)
                        paired.append((dot_split(u, split(low)), end + dot_split(u, split(start))))
                    links = paired + links[2 * len(paired) :]
                message[n, pl.ds(0, face)] = links[0][1]
                if sent_rows > face:
                    message[n, pl.ds(face, packed)] = pack_map(links[0][0], tracers)

        state.tails, state.ends, state.message = run(
            body,
            "begin_early",
            [order, inlet, state.near, state.tail, up_near, side_near, state.source_high, state.source_low],
            [
                VMEM((items, face, 2 * face), F32),
                VMEM((items, face, tracers), F32),
                VMEM((size, sent_rows, tracers), F32),
            ],
            [VMEM((items, face, tracers), F32)],
        )

    def early_maps(state, after):
        size = len(early)

        def body(order, inv, up, side, tails, _, maps, side_maps, rows_high, rows_low, row):
            for i in range(size * count):
                k = at(early, i)
                both = face_maps(inv[k], up[k], side[k])
                maps[i] = stack_maps(both)
                side_maps[i] = stack_maps(lateral_rows(both, per_side))
                n, p = i // count, i % count
                head = tails[n * count + order[early[0] + n, p]][:, :face]
                link(n, p, split(head), rows_high, rows_low, row)

        state.maps, state.side_maps, state.high, state.low = run(
            body,
            "early_maps",
            [order, inv_near, up_near, side_near, state.tails, after],
            map_outs(size) + chain_outs(size)[1:],
            [VMEM((size, face, wide), F32)],
        )
        return state.maps

    def late_sources(after):
        def body(previous, rate, aff, _, source_high, source_low):
            for i in range(len(late) * count):
                lag = previous[at(late, i)].astype(F32)
                source_high[i], source_low[i] = split(langmuir(lag, rate[...], aff[...]))

        return run(body, "late_sources", [old_near, rate, aff, after], source_outs(len(late)), [])

    def begin_late(sources, after):
        size = len(late)
        items = size * count

        def body(
            order, inv, up, side, source_high, source_low, _,
            own, tails, rows_high, rows_low, mapped, row,
        ):
            for i in range(items):
                k = at(late, i)
                tails[i] = face_maps(inv[*k, ending], up[k], side[k])
            for i in range(items):
                own[i] = times(inv[*at(late, i), ending], source_high, source_low, i)
                n, p = i // count, i % count
                step = split(tails[n * count + order[late[n], p]][:, :face])
                link(n, p, step, rows_high, rows_low, row)
            for n in range(size):
                mapped[n] = pack_map(row[n][:, :face], tracers)

        state = SimpleNamespace()
        values = run(
            body,
            "begin_late",
            [order, inv_near, up_near, side_near, *sources, after],
            [VMEM((items, face, tracers), F32)]
            + chain_outs(size)
            + [VMEM((size, packed, tracers), F32)],
            [VMEM((size, face, wide), F32)],
        )
        state.source_high, state.source_low = sources
        state.own, state.tails, state.high, state.low, state.mapped = values
        return state

    def late_maps(after):
        items = len(late) * count

        def body(inv, up, side, _, maps):
            for i in range(items):
                k = at(late, i)
                maps[i] = stack_maps(face_maps(inv[k], up[k], side[k]))

        return run(body, "late_maps", [inv_near, up_near, side_near, after], map_outs(len(late))[:1], [])[0]

    def arrived_side(arrived, j):
        return split(jnp.where(lax.axis_index("lat") > 0, arrived[j], 0.0))

    def first_sides(state, arrived):
        def body(order, inlet, arrived, own, tails, rows_high, rows_low, mapped, ends, message, high, low):
            for p in range(count):
                j = order[0, p]
                ends[p] = own[j] + side_of(tails, j, arrived_side(arrived, j))
            message[0, pl.ds(0, face)] = offset(0, known_inflow(inlet[0]), rows_high, rows_low, ends, high, low)
            if sent_rows > face:
                message[0, pl.ds(face, packed)] = mapped[0]

        state.ends, state.message = run(
            body,
            "first_sides",
            [order, inlet, arrived, state.own, state.tails, state.high, state.low, state.mapped],
            [VMEM((count, face, tracers), F32), VMEM((1, sent_rows, tracers), F32)],
            offset_scratch(1),
        )

    def combine_first(stage, own, other, after):
        rows = face if stage + 2 == stages else sent_rows

        def body(own, other, _, message):
            upper = bit(stage)
            for n in range(own.shape[0]):
                up = jnp.where(upper, own[n], other[n])
                low = jnp.where(upper, other[n], own[n])
                m = split(unpack_map(up[face:], face))
                message[n, pl.ds(0, face)] = dot_split(m, split(low[:face])) + up[:face]
                if rows > face:
                    mapped = dot_split(m, split(unpack_map(low[face:], face)))
                    message[n, pl.ds(face, packed)] = pack_map(mapped, tracers)

        return run(body, "combine", [own, other, after], [VMEM((own.shape[0], rows, tracers), F32)], [])[0]

    def combine_second(stage, own, other, old_own, old_other):
        def body(own, other, *refs):
            message = refs[-1]
            upper = bit(stage)
            for c in range(cols):
                g, n = home[c]
                mine, theirs = refs[2 * g], refs[2 * g + 1]
                m = jnp.where(upper, mine[n, pl.ds(face, packed)], theirs[n, pl.ds(face, packed)])
                up = jnp.where(upper, own[c], other[c])
                low = jnp.where(upper, other[c], own[c])
                message[c] = dot_split(split(unpack_map(m, face)), split(low)) + up

        ins = [own, other]
        for pair in zip(old_own, old_other):
            ins += pair
        return run(body, "combine", ins, [VMEM(own.shape, F32)], [])[0]

    def entering(start, offsets, maps):
        for stage in reversed(range(len(maps))):
            m = split(unpack_map(maps[stage], face))
            beyond = dot_split(m, split(start)) + offsets[stage]
            start = jnp.where(bit(stage), beyond, start)
        return start

    def lower_maps(maps):
        rows = lax.broadcasted_iota(jnp.int32, (face, face), 0)
        total = jnp.where(rows == lax.broadcasted_iota(jnp.int32, (face, face), 1), 1.0, 0.0)
        for stage in reversed(range(stages - 1)):
            beyond = dot_split(split(unpack_map(maps[stage], face)), split(total))
            total = jnp.where(bit(stage), beyond, total)
        return total

    def within_of(n, start, ends, rows_high, rows_low, high, low):
        for p in range(count):
            e = split(start if p == 0 else ends[n * count + p - 1])
            high[n, pl.ds(p * face, face)] = e[0]
            low[n, pl.ds(p * face, face)] = e[1]
        span = pl.ds(0, wide)
        return dot_split((rows_high[n, span], rows_low[n, span]), (high[n], low[n]))

    def side_rows(s):
        return jnp.concatenate([jnp.zeros((face, tracers), BF16), *stack_side(s)], axis=0)

    def prepare(group, state, sides, after):
        size = len(group)
        lower = state.received[:-1]

        def body(inv, sides, source_high, source_low, maps, ends, rows_high, rows_low, _, *refs):
            mapped, (free, within, reach_high, reach_low, high, low) = refs[: len(lower)], refs[len(lower) :]
            span = pl.ds(0, wide)
            for i in range(size * count):
                s = arrived_side(sides, i) if group[0] == 0 else split(sides[i])
                whole = times(inv[at(group, i)], source_high, source_low, i)
                free[i] = whole + dot(maps[i][:, 2 * face :], side_rows(s))
            for n in range(size):
                old = [r[n, pl.ds(face, packed)] for r in mapped]
                start = entering(jnp.zeros((face, tracers), F32), [r[n, pl.ds(0, face)] for r in mapped], old)
                within[n] = within_of(n, start, ends, rows_high, rows_low, high, low)
                rows = (rows_high[n, span][:, :face], rows_low[n, span][:, :face])
                reach_high[n], reach_low[n] = split(dot_split(rows, split(lower_maps(old))))

        state.free, state.within, *state.reach = run(
            body,
            "prepare",
            [inv_near, sides, state.source_high, state.source_low, state.maps, state.ends, state.high, state.low]
            + [after, *lower],
            [VMEM((size * count, nodes, tracers), F32), VMEM((size, wide, tracers), F32)]
            + [VMEM((size, wide, face), BF16)] * 2,
            [VMEM((size, wide, tracers), BF16)] * 2,
        )

    def enter_first(group, state, after):
        size = len(group)
        last = group[-1] == cols - 1
        newest = state.received[-1:]

        def body(order, inlet, within, reach_high, reach_low, *refs):
            got, refs = refs[: len(newest)], refs[len(newest) :]
            if last:
                (free, side_maps), refs = refs[:2], refs[3:]
            stack = refs[0]
            for n, c in enumerate(group):
                start = known_inflow(inlet[c])
                for r in got:
                    start = jnp.where(bit(stages - 1), r[n], start)
                inflow = within[n] + dot_split((reach_high[n], reach_low[n]), split(start))
                for p in range(count):
                    j = order[c, p]
                    i = n * count + j
                    rows = jnp.concatenate(stack_inflow(split(inflow[p * face : (p + 1) * face])), axis=0)
                    stack[i] = rows
                    if c == cols - 1:
                        part = dot(side_maps[i][:, : 3 * face], rows)
                        refs[1][j] = lateral_rows(free.at[i], per_side) + part

        outs = [VMEM((size * count, 3 * face, tracers), BF16)]
        if last:
            outs.append(VMEM((count, face, tracers), F32))
        ins = [order, inlet, state.within, *state.reach, *newest]
        if last:
            ins += [state.free, state.side_maps, after]
        values = run(body, "enter", ins, outs, [])
        state.stack = values[0]
        return values[1] if last else None

    def put_inflow(n, c, inflow, order, stack):
        for p in range(count):
            i = n * count + order[c, p]
            for q, part in enumerate(stack_inflow(split(inflow[p * face : (p + 1) * face]))):
                stack[i, pl.ds(q * face, face)] = part

    def second(group, state, after):
        items = len(group) * count

        def body(inv, maps, free, stack, rate, aff, _, source_high, source_low, traces, own):
            for i in range(items + 1):
                if i < items:
                    swept = free[i] + dot(maps[i][:, : 3 * face], stack[i])
                    traces[i] = lateral_rows(swept, per_side)
                    source_high[i], source_low[i] = split(langmuir(swept, rate[...], aff[...]))
                if i > 0:
                    own[i - 1] = times(inv[*at(group, i - 1), ending], source_high, source_low, i - 1)

        state.source_high, state.source_low, state.traces, state.own = run(
            body,
            "second",
            [inv_near, state.maps, state.free, state.stack, rate, aff, after],
            source_outs(len(group)) + [VMEM((items, face, tracers), F32)] * 2,
            [],
        )
        return state.own

    def fold_sides(after):
        def body(order, inlet, _, *refs):
            got = [refs[3 * g : 3 * g + 3] for g in range(len(groups))]
            outs = refs[3 * len(groups) :]
            for g, group in enumerate(groups):
                tails, rows_high, rows_low = got[g]
                high, low, begun = outs[3 * g : 3 * g + 3]
                for n, c in enumerate(group):
                    start = split(known_inflow(inlet[c]))
                    begun[n] = dot_split(last_row(rows_high, rows_low, n, 0), start)
                    for p in range(count):
                        folded = split(tails[n * count + order[c, p]][:, face:])
                        if p + 1 < count:
                            folded = split(dot_split(last_row(rows_high, rows_low, n, p + 1), folded))
                        high[n, p] = folded[0]
                        low[n, p] = folded[1]

        ins, outs = [order, inlet, after], []
        for group, state in zip(groups, states):
            ins += [state.tails, state.high, state.low]
            outs += [VMEM((len(group), count, face, face), BF16)] * 2
            outs.append(VMEM((len(group), face, tracers), F32))
        values = run(body, "fold_sides", ins, outs, [])
        for g, state in enumerate(states):
            state.side_high, state.side_low, state.begun = values[3 * g : 3 * g + 3]
        return values[0]

    def last_row(rows_high, rows_low, n, block):
        place = pl.ds(wide, face)
        return tuple(r[n, place][:, block * face : (block + 1) * face] for r in (rows_high, rows_low))

    def side_at(c, j, arrived, traces):
        if c == 0:
            return arrived_side(arrived, j)
        h, m = home[c - 1]
        return split(traces[h][m * count + j])

    def second_sides(arrived):
        def body(order, arrived, *refs):
            got = [refs[7 * g : 7 * g + 7] for g in range(len(groups))]
            message = refs[-1]
            for g, group in enumerate(groups):
                own, _, rows_high, rows_low, side_high, side_low, begun = got[g]
                for n, c in enumerate(group):
                    total = own[n * count + order[c, count - 1]] + begun[n]
                    for p in range(count):
                        s = side_at(c, order[c, p], arrived, [x[1] for x in got])
                        total = total + dot_split((side_high[n, p], side_low[n, p]), s)
                        if p + 1 < count:
                            row = last_row(rows_high, rows_low, n, p + 1)
                            total = total + dot_split(row, split(own[n * count + order[c, p]]))
                    message[c] = total

        ins = [order, arrived]
        for state in states:
            ins += [state.own, state.traces, state.high, state.low]
            ins += [state.side_high, state.side_low, state.begun]
        return run(body, "second_sides", ins, [VMEM((cols, face, tracers), F32)], [])[0]

    def settle(after, arrived, offsets):
        per_group = 8 + len(offsets)

        def body(order, inlet, _, arrived, inv, *refs):
            offs, refs = refs[: len(offsets)], refs[len(offsets) :]
            got = [refs[per_group * g : per_group * g + per_group] for g in range(len(groups))]
            outs = refs[per_group * len(groups) :]
            scratch = outs[2 * len(groups) :]
            for g, group in enumerate(groups):
                source_high, source_low, maps, rows_high, rows_low, own, traces, tails, *mapped = got[g]
                base, within = outs[2 * g : 2 * g + 2]
                ends, high, low = scratch[3 * g : 3 * g + 3]
                for i in range(len(group) * count):
                    whole = times(inv[at(group, i)], source_high, source_low, i)
                    s = side_at(group[0] + i // count, i % count, arrived, [x[6] for x in got])
                    base[i] = whole + dot(maps[i][:, 2 * face :], side_rows(s))
                for n, c in enumerate(group):
                    for p in range(count):
                        i = n * count + order[c, p]
                        s = side_at(c, order[c, p], arrived, [x[6] for x in got])
                        ends[n * count + p] = own[i] + side_of(tails, i, s)
                    old = [r[n, pl.ds(face, packed)] for r in mapped]
                    start = entering(known_inflow(inlet[c]), [r[c] for r in offs], old)
                    within[n] = within_of(n, start, ends, rows_high, rows_low, high, low)

        ins = [order, inlet, after, arrived, inv_near, *offsets]
        outs, scratch = [], []
        for group, state in zip(groups, states):
            ins += [state.source_high, state.source_low, state.maps, state.high, state.low]
            ins += [state.own, state.traces, state.tails, *state.received[:-1]]
            outs.append(VMEM((len(group) * count, nodes, tracers), F32))
            outs.append(VMEM((len(group), wide, tracers), F32))
            scratch.append(VMEM((len(group) * count, face, tracers), F32))
            scratch += [VMEM((len(group), wide, tracers), BF16)] * 2
        values = run(body, "settle", ins, outs, scratch)
        for g, state in enumerate(states):
            state.base, state.within = values[2 * g : 2 * g + 2]

    def result(offsets):
        def body(order, *refs):
            offs, refs = refs[: len(offsets)], refs[len(offsets) :]
            got = [refs[5 * g : 5 * g + 5] for g in range(len(groups))]
            out, staged, sems, *stacks = refs[5 * len(groups) :]
            for g, group in enumerate(groups):
                within, reach_high, reach_low = got[g][:3]
                for n, c in enumerate(group):
                    inflow = within[n]
                    for r in offs:
                        late_part = split(jnp.where(bit(stages - 1), r[c], 0.0))
                        inflow = inflow + dot_split((reach_high[n], reach_low[n]), late_part)
                    put_inflow(n, c, inflow, order, stacks[g])
            started = []
            for g, group in enumerate(groups):
                base, maps = got[g][3:]
                for i in range(len(group) * count):
                    k = len(started)
                    staged[k] = (base[i] + dot(maps[i][:, : 3 * face], stacks[g][i])).astype(BF16)
                    started.append(pltpu.make_async_copy(staged.at[k], out.at[at(group, i)], sems.at[k]))
                    started[-1].start()
            for copy in started:
                copy.wait()

        ins = [order, *offsets]
        scratch = [VMEM((cols * count, nodes, tracers), BF16), pltpu.SemaphoreType.DMA((cols * count,))]
        for group, state in zip(groups, states):
            ins += [state.within, *state.reach, state.base, state.maps]
            scratch.append(VMEM((len(group) * count, 3 * face, tracers), BF16))
        return run(body, "result", ins, [HBM(previous.shape, BF16)], scratch)[0]

    def exchange_first(state, beside):
        state.sent, state.received = [state.message], []
        for stage in range(stages):
            if stage:
                state.sent.append(combine_first(stage - 1, state.sent[-1], state.received[-1], after))
            state.received.append(swap(state.sent[-1], stage))
            if not stage:
                after = beside()

    (trace, order, rate, aff, inlet), one = load()
    order = (order, SMEM)
    arrived = to_next(trace)
    begin_early(one)
    exchange_first(one, lambda: early_maps(one, one.message))
    prepare(early, one, one.near, one.sent[-1])
    sources = late_sources(one.sent[-1])
    trace = enter_first(early, one, sources[0])
    arrived_next = to_next(trace)
    two = begin_late(sources, trace)
    states = [one, two]
    first_sides(two, arrived)
    exchange_first(two, lambda: second(early, one, two.message))
    two.maps = late_maps(two.sent[-1])
    prepare(late, two, arrived, two.sent[-1])
    fold_sides(two.sent[-1])
    enter_first(late, two, None)
    second(late, two, two.sent[-1])
    message, offsets = second_sides(arrived_next), []
    for stage in range(stages):
        offsets.append(swap(message, stage))
        if stage + 1 < stages:
            sent, received = [s.sent[stage] for s in states], [s.received[stage] for s in states]
            message = combine_second(stage, message, offsets[-1], sent, received)
    settle(message, arrived_next, offsets[:-1])
    return result(offsets[-1:])


def solution(mesh):
    placed = (
        P("lat", "stream", None, None, None),
        P("lat", "stream", None, None, None),
        P("lat", "stream", None, None, None),
        P("lat", None, None),
        P("lat", "stream", None, None, None),
        P(),
        P(),
        P("lat", "stream", None),
    )
    return jax.shard_map(
        per_device,
        mesh=mesh,
        in_specs=placed,
        out_specs=P("lat", "stream", None, None, None),
        check_vma=False,
    )
```
